128 devices in a mesh: ctx: 32 (over z, x, core), exp: 4 (over y).
Axes of the slice: x: 4, y: 4, z: 4, core: 2. Of those that a mesh axis runs over, the one named last changes fastest.
Arguments:
- attn_query: bfloat16 [32768, 2048], P('ctx', 'exp'), may hold values from -224 to 224
- attn_key: bfloat16 [32768, 2048], P('ctx', 'exp'), may hold values from -56 to 56
- attn_value: bfloat16 [32768, 2048], P('ctx', 'exp'), may hold values from -56 to 56
- prefix_state: float32 [32, 16, 128, 128], P('ctx', 'exp'), may hold values from -163840 to 163840
- moe_in: bfloat16 [32768, 2048], P(('ctx', 'exp')), may hold values from -6 to 6
- grad_out: bfloat16 [32768, 2048], P(('ctx', 'exp')), may hold values from -6 to 6
- router_gates: bfloat16 [32768, 1], P(('ctx', 'exp')), may hold values from 0.099609375 to 1
- expert_ids: int32 [32768, 1], P(('ctx', 'exp')), may hold values from 0 to 3; in each aligned block of 256 rows (0 to 255, 256 to 511, ...) at most 96 rows name the same one
- w_gate_up: bfloat16 [4, 2048, 1024], P('exp'), may hold values from -0.125 to 0.125
- w_down: bfloat16 [4, 512, 2048], P('exp'), may hold values from -0.25 to 0.25
- w_out: bfloat16 [2048, 2048], P('exp'), may hold values from -0.125 to 0.125
Outputs:
- grad_query: bfloat16 [32768, 2048], P('ctx', 'exp')
- grad_key: bfloat16 [32768, 2048], P('ctx', 'exp')
- grad_value: bfloat16 [32768, 2048], P('ctx', 'exp')
- grad_resid: bfloat16 [32768, 2048], P(('ctx', 'exp'))
- grad_gates: bfloat16 [32768, 1], P(('ctx', 'exp'))
- grad_gate_up: float32 [4, 2048, 1024], P('exp', 'ctx')
- grad_down: float32 [4, 512, 2048], P('exp', 'ctx')
The draws below stay inside these ranges and needn't reach their ends.
Inputs may be any that keep to these rules, and one draw needn't show every extreme that they name: `expert_ids`: among the 256 rows of one device (aligned blocks of rows) no expert is named more than 96 times, a bound that some block reaches.
All inputs are finite; a program needn't handle non-finite values.
Results may differ from the reference program's by a relative error of at most 0.0063.
Values may be sent and summed in bfloat16 or wider, within the bound.
No kernel may reach another device: no remote copies, remote signals or barrier semaphores. Data moves between devices by JAX's collectives and lax.ppermute only.
A program may use at most 192 MiB of HBM per device.

```python
import math
import jax
import jax.numpy as jnp
import numpy as np
from jax import lax

D = 2048
FF = 512
HEADS = 16
HEAD_DIM = 128
TOPK = 1
ROWS = 256
FLIGHT = 4
TOK_CTX = 1024
TOKENS = 32768
BLOCKS = 32
CAP = 96


def levels(stream_key, extent, split, least, high):
    def one(axis_at, parts):
        heights = jax.random.uniform(jax.random.fold_in(jax.random.fold_in(stream_key, 6), axis_at), (parts,), jnp.float32, least / len(split), high / len(split))
        return jnp.repeat(jnp.exp(heights), extent[axis_at] // parts).reshape((-1,) + (1,) * (len(extent) - axis_at - 1))

    level = one(*split[0])
    for cut in split[1:]:
        level = level * one(*cut)
    return level


def assign_block(own_key, own, number, rows, amount, top, reach, slope):
    order = jax.random.permutation(own_key, amount)
    heavy_load, common = shares(amount, rows * top, reach, slope, True), shares(amount, rows * top, reach, slope, False)
    places = jnp.arange(amount)

    def named(lengths, turn):
        used = int((lengths > 0).sum())
        fixed = max(1, used // 4)
        passed = fixed + (places - fixed + turn * (used - fixed)) % max(1, amount - fixed)
        return jnp.zeros((amount,), jnp.int32).at[order[jnp.where(places < fixed, places, passed)]].set(jnp.asarray(lengths, jnp.int32))

    lengths = jnp.where(number % 4 == 0, named(heavy_load, number // 4), named(common, number - number // 4 - 1))
    mixed = jax.random.permutation(jax.random.fold_in(own, 3), amount)
    donor, receiver = mixed[0:amount // 2 * 2:2], mixed[1:amount // 2 * 2:2]
    margin = jnp.minimum(lengths[donor] - 1, reach - lengths[receiver]) // 2
    margin = jnp.where((donor == order[0]) | (receiver == order[0]) | (lengths[receiver] == 0), 0, jnp.maximum(margin, 0))
    passed = jax.random.randint(jax.random.fold_in(own, 4), (amount // 2,), 0, 1 << 20) % (margin + 1)
    lengths = lengths.at[donor].add(-passed).at[receiver].add(passed)
    members = jnp.searchsorted(jnp.cumsum(lengths), jnp.arange(rows * top), side="right").astype(jnp.int32)
    table = members.reshape(top, rows).T
    table = table[jax.random.permutation(jax.random.fold_in(own, 1), rows)]
    turn = jax.random.randint(jax.random.fold_in(own, 2), (rows, 1), 0, top)
    return jnp.take_along_axis(table, (jnp.arange(top)[None, :] + turn) % top, axis=1)


def shares(number_of, total, most, skew, full):
    loads = [(1 << 20) // math.isqrt(rank ** skew) + 1 for rank in range(1, number_of + 1)]
    largest = most if full else min(most, max(-(-total // number_of), total * loads[0] // sum(loads)))
    least = 1 if total - largest >= number_of - 1 else 0
    holding, rest = [largest] + [least] * (number_of - 1), total - largest - least * (number_of - 1)
    while rest > 0:
        movable = [i for i in range(1, number_of) if holding[i] < largest] or [i for i in range(1, number_of) if holding[i] < most]
        pool, remaining = sum([loads[i] for i in movable]), rest
        for i in movable:
            more = min(most - holding[i], max(1, remaining * loads[i] // pool), rest)
            holding[i] = holding[i] + more
            rest = rest - more
    return np.array(holding)


def scatter_about(key, shape, scale, bound, split=(), kind=jnp.bfloat16):
    values = scale * jax.random.normal(key, shape, jnp.float32)
    if split:
        values = values * levels(key, shape, split, -0.22, 0.18)
    return jnp.clip(values, -bound, bound).astype(kind)


def setup_inputs(seed: int = 0) -> dict:
    seeds = jax.random.split(jax.random.key(seed), 12)
    attn_query = scatter_about(seeds[0], (TOKENS, HEADS * HEAD_DIM), (0.1 * (4 * TOKENS) ** 0.5), 224.0, ((0, 32), (1, 4)))
    attn_key = scatter_about(seeds[1], (TOKENS, HEADS * HEAD_DIM), (0.5 * (4 * TOKENS) ** 0.25), 56.0, ((0, 32), (1, 4)))
    attn_value = scatter_about(seeds[2], (TOKENS, HEADS * HEAD_DIM), (0.5 * (4 * TOKENS) ** 0.25), 56.0, ((0, 32), (1, 4)))
    prefix_state = scatter_about(seeds[3], (BLOCKS, HEADS, HEAD_DIM, HEAD_DIM), (0.25 * (3 * TOKENS) ** 0.5 * (4 * TOKENS) ** 0.5), 163840.0, ((0, 32), (1, 4)), jnp.float32)
    moe_in = scatter_about(seeds[4], (TOKENS, D), 1.0, 6.0, ((0, 128),))
    grad_out = scatter_about(seeds[5], (TOKENS, D), 0.5, 6.0, ((0, 128),))
    router_gates = jnp.clip(0.099609375 + 0.9003906 * jax.random.uniform(seeds[6], (TOKENS, TOPK), jnp.float32) ** levels(seeds[6], (TOKENS, TOPK), ((0, 128),), -0.2, 0.2), 0.099609375, 1.0).astype(jnp.bfloat16)
    expert_ids_keys = jax.random.split(jax.random.fold_in(seeds[7], 1), TOKENS // ROWS)
    expert_ids_turns = jax.random.permutation(jax.random.fold_in(seeds[7], 3), TOKENS // ROWS)
    expert_ids = jax.vmap(lambda own, number: assign_block(jax.random.fold_in(seeds[7], 2), own, number, ROWS, FLIGHT, TOPK, CAP, 1))(expert_ids_keys, expert_ids_turns).reshape((TOKENS, TOPK))
    w_gate_up = scatter_about(seeds[8], (FLIGHT, D, 2 * FF), D ** -0.5, 0.125, ((0, 4),))
    w_down = scatter_about(seeds[9], (FLIGHT, FF, D), FF ** -0.5, 0.25, ((0, 4),))
    w_out = scatter_about(seeds[10], (HEADS * HEAD_DIM, D), (HEADS * HEAD_DIM) ** -0.5, 0.125, ((0, 4),))
    return dict(attn_query=attn_query, attn_key=attn_key, attn_value=attn_value, prefix_state=prefix_state, moe_in=moe_in, grad_out=grad_out, router_gates=router_gates, expert_ids=expert_ids, w_gate_up=w_gate_up, w_down=w_down, w_out=w_out)


highest = lax.Precision.HIGHEST


def silu_slope(value):
    logistic = jax.nn.sigmoid(value)
    return logistic * (1.0 + value * (1.0 - logistic))


def contract_rows(left, right):
    return lax.dot_general(left, right, (((0,), (0,)), ((), ())), preferred_element_type=jnp.float32)


def contract_cols(left, right):
    return lax.dot_general(left, right, (((1,), (1,)), ((), ())), preferred_element_type=jnp.float32)


def expert_backward(inputs, gate_vals, w_pair, w_back, hidden_units):
    width = w_back.shape[1]
    rows_in = inputs[:, :width]
    cotangent = inputs[:, width:]
    both = jnp.dot(rows_in, w_pair, preferred_element_type=jnp.float32)
    first = both[:, :hidden_units]
    second = both[:, hidden_units:]
    hidden = (jax.nn.silu(first) * second).astype(jnp.bfloat16)
    output = jnp.dot(hidden, w_back, preferred_element_type=jnp.float32)
    cot_wide = cotangent.astype(jnp.float32)
    grad_gate = jnp.sum(cot_wide * output, axis=1).astype(jnp.bfloat16)
    scaled = (gate_vals.astype(jnp.float32)[:, None] * cot_wide).astype(jnp.bfloat16)
    grad_hidden = contract_cols(scaled, w_back)
    grad_first = grad_hidden * second * silu_slope(first)
    grad_second = grad_hidden * jax.nn.silu(first)
    grad_both = jnp.concatenate([grad_first, grad_second], axis=1).astype(jnp.bfloat16)
    grad_rows = contract_cols(grad_both, w_pair).astype(jnp.bfloat16)
    return rows_in, hidden, scaled, grad_both, grad_rows, grad_gate


def block_state(query_rows, grad_rows, counts):
    query_wide = query_rows.astype(jnp.float32)
    grad_wide = grad_rows.astype(jnp.float32) / counts[:, None, None]
    return jnp.einsum("uhj,uhi->hji", query_wide, grad_wide, precision=highest)


def attend_block(query_rows, key_rows, value_rows, grad_rows, prior, later, counts):
    scale_col = counts[:, None, None]
    inverse = 1.0 / counts
    position = jnp.arange(counts.shape[0], dtype=jnp.int32)
    lower = (position[None, :] <= position[:, None]).astype(jnp.float32)
    upper = (position[None, :] >= position[:, None]).astype(jnp.float32) * inverse[None, :]
    mix_query = (jnp.einsum("thd,uhd->htu", grad_rows, value_rows, preferred_element_type=jnp.float32)
                 * lower).astype(jnp.bfloat16)
    grad_query = (jnp.einsum("htu,uhd->thd", mix_query, key_rows, preferred_element_type=jnp.float32)
                  + jnp.einsum("thi,hji->thj", grad_rows.astype(jnp.float32), prior, precision=highest)) / scale_col
    mix_key = (jnp.einsum("thd,uhd->htu", value_rows, grad_rows, preferred_element_type=jnp.float32)
               * upper).astype(jnp.bfloat16)
    grad_key = (jnp.einsum("htu,uhd->thd", mix_key, query_rows, preferred_element_type=jnp.float32)
                + jnp.einsum("thi,hji->thj", value_rows.astype(jnp.float32), later, precision=highest))
    mix_value = (jnp.einsum("thd,uhd->htu", key_rows, query_rows, preferred_element_type=jnp.float32)
                 * upper).astype(jnp.bfloat16)
    grad_value = (jnp.einsum("htu,uhd->thd", mix_value, grad_rows, preferred_element_type=jnp.float32)
                  + jnp.einsum("thj,hji->thi", key_rows.astype(jnp.float32), later, precision=highest))
    return grad_query, grad_key, grad_value


def reference(attn_query, attn_key, attn_value, prefix_state, moe_in, grad_out, router_gates, expert_ids, w_gate_up, w_down, w_out):
    pair_total = TOKENS * TOPK
    block_count = TOKENS // ROWS
    flat_ids = expert_ids.reshape(pair_total)
    member = (flat_ids[:, None] == jnp.arange(FLIGHT, dtype=jnp.int32)[None, :]).astype(jnp.int32)
    member = member.reshape(block_count, ROWS * TOPK, FLIGHT)
    earlier = jnp.cumsum(member, axis=1) - member
    slot_of = jnp.sum(earlier * member, axis=2).reshape(pair_total)
    block_of = jnp.arange(pair_total, dtype=jnp.int32) // (ROWS * TOPK)
    table = jnp.full((FLIGHT, block_count * CAP), pair_total, jnp.int32)
    table = table.at[flat_ids, block_of * CAP + slot_of].set(jnp.arange(pair_total, dtype=jnp.int32))
    flat_gates = router_gates.reshape(pair_total)

    def one_expert(inputs):
        listing, w_pair, w_back = inputs
        token_of = listing // TOPK
        rows_in = jnp.take(moe_in, token_of, axis=0, mode="fill", fill_value=0)
        cotangent = jnp.take(grad_out, token_of, axis=0, mode="fill", fill_value=0)
        gate_vals = jnp.take(flat_gates, listing, axis=0, mode="fill", fill_value=0)
        joined = jnp.concatenate([rows_in, cotangent], axis=1)
        rows_in, hidden, scaled, grad_both, grad_rows, grad_gate = expert_backward(joined, gate_vals, w_pair, w_back, FF)
        return grad_rows, grad_gate, contract_rows(rows_in, grad_both), contract_rows(hidden, scaled)

    grad_rows, grad_gate, grad_gate_up, grad_down = lax.map(one_expert, (table, w_gate_up, w_down))
    flat_table = table.reshape(-1)
    pair_rows = jnp.zeros((pair_total, D), jnp.float32).at[flat_table].set(
        grad_rows.reshape(-1, D).astype(jnp.float32), mode="drop")
    grad_resid = (grad_out.astype(jnp.float32) + pair_rows.reshape(TOKENS, TOPK, D).sum(axis=1)).astype(jnp.bfloat16)
    grad_gates = jnp.zeros((pair_total,), jnp.bfloat16).at[flat_table].set(
        grad_gate.reshape(-1), mode="drop").reshape(TOKENS, TOPK)
    attn_grad = contract_cols(grad_resid, w_out).astype(jnp.bfloat16)

    block_shape = (BLOCKS, TOK_CTX, HEADS, HEAD_DIM)
    block_ids = jnp.arange(BLOCKS, dtype=jnp.int32)

    def counts_of(block):
        return (3 * TOKENS + block * TOK_CTX + jnp.arange(TOK_CTX, dtype=jnp.int32) + 1).astype(jnp.float32)

    def state_of(inputs):
        query, grad, block = inputs
        return block_state(query, grad, counts_of(block))

    queries = attn_query.reshape(block_shape)
    keys_all = attn_key.reshape(block_shape)
    values_all = attn_value.reshape(block_shape)
    grads_all = attn_grad.reshape(block_shape)
    states = lax.map(state_of, (queries, grads_all, block_ids))
    totals = jnp.cumsum(states[::-1], axis=0)[::-1]
    later_all = jnp.concatenate([totals[1:], jnp.zeros_like(states[:1])], axis=0)

    def grads_of(inputs):
        query, key_rows, value_rows, grad, prior, later, block = inputs
        results = attend_block(query, key_rows, value_rows, grad, prior, later, counts_of(block))
        return tuple(result.reshape(TOK_CTX, HEADS * HEAD_DIM).astype(jnp.bfloat16) for result in results)

    grad_query, grad_key, grad_value = lax.map(
        grads_of, (queries, keys_all, values_all, grads_all, prefix_state, later_all, block_ids))
    flat_shape = (TOKENS, HEADS * HEAD_DIM)
    return (grad_query.reshape(flat_shape), grad_key.reshape(flat_shape), grad_value.reshape(flat_shape),
            grad_resid, grad_gates, grad_gate_up, grad_down)
```

```python
import functools

import jax
import jax.numpy as jnp
from jax import lax
from jax.experimental import pallas as pl
from jax.experimental.pallas import tpu as pltpu
from jax.sharding import PartitionSpec as P

bf16 = jnp.bfloat16
f32 = jnp.float32
VMEM = pltpu.VMEM
SMEM = pltpu.SMEM
Z, X, C, Y = 4, 4, 2, 4
CAP, ROWS, WIDTH, FF, HD, HEADS, TOK = 96, 256, 2048, 512, 128, 4, 1024
BLOCKS = Z * X * C
LIMIT = 48 * 1024 * 1024


def dot(a, b):
    return lax.dot_general(a, b, (((1,), (0,)), ((), ())), preferred_element_type=f32)


def dot_t(a, b):
    return lax.dot_general(a, b, (((1,), (1,)), ((), ())), preferred_element_type=f32)


def t_dot(a, b):
    return lax.dot_general(a, b, (((0,), (0,)), ((), ())), preferred_element_type=f32)


def split(a):
    hi = a.astype(bf16)
    return hi, (a - hi.astype(f32)).astype(bf16)


def full():
    return pl.BlockSpec(memory_space=VMEM)


def scalars():
    return pl.BlockSpec(memory_space=SMEM)


def call(body, name, outs, ins, flops=0, moved=0, grid=None, in_specs=None, out_specs=None):
    kwargs = {} if grid is None else {"grid": grid}
    return pl.pallas_call(
        body,
        name=name,
        out_shape=[jax.ShapeDtypeStruct(s, t) for s, t in outs],
        in_specs=in_specs or [full() for _ in ins],
        out_specs=out_specs or [full() for _ in outs],
        compiler_params=pltpu.CompilerParams(vmem_limit_bytes=LIMIT),
        cost_estimate=pl.CostEstimate(flops=flops, bytes_accessed=moved, transcendentals=0),
        **kwargs,
    )(*ins)


def pack_body(at_ref, ids_ref, gate_ref, moe_ref, cot_ref, place_ref, *chunks):
    me = at_ref[0]
    ids = ids_ref[...]
    rel = ids - me
    rel = jnp.where(rel < 0, rel + Y, rel)
    lanes = lax.broadcasted_iota(jnp.int32, (ROWS, HD), 1)
    member = (rel == lanes).astype(f32)
    row = lax.broadcasted_iota(jnp.int32, (ROWS, ROWS), 0)
    col = lax.broadcasted_iota(jnp.int32, (ROWS, ROWS), 1)
    earlier = dot((col < row).astype(bf16), member.astype(bf16))
    slot = jnp.sum(earlier * member, axis=1, keepdims=True).astype(jnp.int32)
    target = rel * CAP + slot
    places = lax.broadcasted_iota(jnp.int32, (ROWS, Y * CAP), 1)
    place = (places == target).astype(bf16)
    place_ref[...] = place
    gate = gate_ref[...].astype(f32)
    step = 512
    for j in range(WIDTH // step):
        part = t_dot(place, moe_ref[:, j * step : (j + 1) * step]).astype(bf16)
        for s in range(Y):
            chunks[s][:, j * step : (j + 1) * step] = part[s * CAP : (s + 1) * CAP]
    for j in range(WIDTH // step):
        scaled = (gate * cot_ref[:, j * step : (j + 1) * step].astype(f32)).astype(bf16)
        part = t_dot(place, scaled).astype(bf16)
        for s in range(Y):
            chunks[s][:, WIDTH + j * step : WIDTH + (j + 1) * step] = part[s * CAP : (s + 1) * CAP]


def pack(me, ids, gates, moe_in, grad_out):
    outs = [((ROWS, Y * CAP), bf16)] + [((CAP, 2 * WIDTH), bf16)] * Y
    ins = (me, ids, gates, moe_in, grad_out)
    specs = [scalars()] + [full()] * 4
    return call(pack_body, "pack", outs, ins, 2 * 384 * 256 * 4096, 5 << 20, in_specs=specs)


def expert_body(r0, r1, r2, r3, wp_ref, wb_ref, b0, b1, b2, b3, hid_ref, gb_ref, dot_ref, rows_ref):
    for s, r in enumerate((r0, r1, r2, r3)):
        rows_ref[s * CAP : (s + 1) * CAP, :] = r[...]
    step = 256
    total = jnp.zeros((Y * CAP, 1), f32)
    for j in range(FF // step):
        at, up = j * step, FF + j * step
        first = dot(rows_ref[:, :WIDTH], wp_ref[:, at : at + step])
        second = dot(rows_ref[:, :WIDTH], wp_ref[:, up : up + step])
        grad_hidden = dot_t(rows_ref[:, WIDTH:], wb_ref[at : at + step, :])
        s = 1.0 / (1.0 + jnp.exp(-first))
        silu = first * s
        hidden = (silu * second).astype(bf16)
        hid_ref[:, at : at + step] = hidden
        total += jnp.sum(hidden.astype(f32) * grad_hidden, axis=1, keepdims=True)
        slope = s * (1.0 + first * (1.0 - s))
        gb_ref[:, at : at + step] = (grad_hidden * second * slope).astype(bf16)
        gb_ref[:, up : up + step] = (grad_hidden * silu).astype(bf16)
    dot_ref[...] = jnp.broadcast_to(total, dot_ref.shape)
    for j in range(WIDTH // step):
        at = j * step
        back = dot_t(gb_ref[...], wp_ref[at : at + step, :]).astype(bf16)
        for s, b in enumerate((b0, b1, b2, b3)):
            b[:, at : at + step] = back[s * CAP : (s + 1) * CAP]


def expert(chunks, w_pair, w_back):
    n = Y * CAP
    outs = [((CAP, WIDTH), bf16)] * Y
    outs += [((n, FF), bf16), ((n, 2 * FF), bf16), ((n, HD), f32), ((n, 2 * WIDTH), bf16)]
    return call(expert_body, "expert", outs, (*chunks, w_pair, w_back), 5 * 2 * n * WIDTH * FF, 14 << 20)


def weights_body(core_ref, rows_ref, scaled_ref, gb_ref, hid_ref, keep_ref, send_ref):
    mine = core_ref[0] == 0
    up = t_dot(rows_ref[...], gb_ref[...])
    down = t_dot(hid_ref[...], scaled_ref[...])
    for k in range(X):
        for value, at, wide in (
            (up[k * 128 : k * 128 + 64], up[k * 128 + 64 : k * 128 + 128], None),
            (down[k * 32 : k * 32 + 16], down[k * 32 + 16 : k * 32 + 32], 1),
        ):
            keep = jnp.where(mine, value, at)
            send = jnp.where(mine, at, value).astype(bf16)
            keep = keep.astype(bf16)
            if wide is None:
                keep_ref[0, k, :64, :] = keep
                send_ref[0, k, :64, :] = send
            else:
                keep_ref[0, k, 64:80, :] = keep[:, :1024]
                send_ref[0, k, 64:80, :] = send[:, :1024]
                keep_ref[0, k, 80:96, :] = keep[:, 1024:]
                send_ref[0, k, 80:96, :] = send[:, 1024:]


def weights(core, rows, grad_both, hidden):
    n = Y * CAP
    shape = (Z, X, 96, 1024)
    block = pl.BlockSpec((1, X, 96, 1024), lambda i: (i, 0, 0, 0))
    return call(
        weights_body,
        "weights",
        [(shape, bf16), (shape, bf16)],
        (core, rows, rows, grad_both, hidden),
        3 * 2 * n * WIDTH * FF,
        12 << 20,
        grid=(Z,),
        in_specs=[
            scalars(),
            pl.BlockSpec((n, 512), lambda i: (0, i)),
            pl.BlockSpec((n, WIDTH), lambda i: (0, 1)),
            pl.BlockSpec((n, 2 * FF), lambda i: (0, 0)),
            pl.BlockSpec((n, 128), lambda i: (0, i)),
        ],
        out_specs=[block, block],
    )


def fold_core_body(at_ref, keep_ref, recv_ref, *outs):
    z, x = at_ref[0], at_ref[1]
    for s in range(4):
        xs = lax.rem(x + s, X)
        for k in range(Z):
            a = keep_ref[k, xs, :, :512].astype(f32) + recv_ref[k, xs, :, :512].astype(f32)
            outs[s][k] = a.astype(bf16)
        zs = lax.rem(z + s, Z)
        for k in range(X):
            b = keep_ref[zs, k, :, 512:].astype(f32) + recv_ref[zs, k, :, 512:].astype(f32)
            outs[4 + s][k] = b.astype(bf16)


def fold_axis_body(at_ref, a0, a1, a2, a3, b0, b1, b2, b3, *outs):
    z, x = at_ref[0], at_ref[1]
    for s in range(4):
        for refs, at, base in (((a0, a1, a2, a3), lax.rem(z + s, Z), 0), ((b0, b1, b2, b3), lax.rem(x + s, X), 4)):
            total = refs[0][at].astype(f32) + refs[1][at].astype(f32)
            total = total + refs[2][at].astype(f32) + refs[3][at].astype(f32)
            outs[base + s][...] = total.astype(outs[base + s].dtype)


def fold_last_body(a0, a1, a2, a3, b0, b1, b2, b3, up_ref, down_ref):
    for j, refs in enumerate(((a0, a1, a2, a3), (b0, b1, b2, b3))):
        total = refs[0][...] + refs[1][...].astype(f32) + refs[2][...].astype(f32) + refs[3][...].astype(f32)
        at = j * 512
        up_ref[0, :, at : at + 512] = total[:64]
        down_ref[0, :, at : at + 512] = total[64:80]
        down_ref[0, :, 1024 + at : 1024 + at + 512] = total[80:96]


def project_body(own_ref, rest_ref, resid_ref, out_ref):
    s = pl.program_id(0)

    @pl.when(s == 0)
    def _():
        out_ref[0] = dot_t(resid_ref[...], own_ref[...]).astype(bf16)

    @pl.when(s > 0)
    def _():
        out_ref[0] = dot_t(resid_ref[...], rest_ref[...].reshape(512, WIDTH)).astype(bf16)


def state_body(at_ref, g0, g1, g2, g3, q_ref, grad_ref, state_ref):
    y, block = at_ref[0], at_ref[1]
    ramp = lax.broadcasted_iota(jnp.int32, (ROWS, 1), 0)
    sums = [jnp.zeros((HD, 2 * HD), f32) for _ in range(HEADS)]
    for s, g in enumerate((g0, g1, g2, g3)):
        off = pl.multiple_of(lax.rem(y + s, Y) * ROWS, ROWS)
        inverse = 1.0 / (3 * BLOCKS * TOK + block * TOK + off + ramp + 1).astype(f32)
        grad_ref[pl.ds(off, ROWS), :] = g[...]
        for h in range(HEADS):
            cols = slice(h * HD, (h + 1) * HD)
            hi, lo = split(g[:, cols].astype(f32) * inverse)
            both = jnp.concatenate([hi, lo], axis=1)
            sums[h] += t_dot(q_ref[pl.ds(off, ROWS), cols], both)
    for h in range(HEADS):
        state_ref[h * HD : (h + 1) * HD, :] = sums[h][:, :HD] + sums[h][:, HD:]


SUB = 256
PARTS = TOK // SUB


def inverse_row(block, at):
    ramp = lax.broadcasted_iota(jnp.int32, (1, SUB), 1)
    return 1.0 / (3 * BLOCKS * TOK + block * TOK + at + ramp + 1).astype(f32)


def triangle(lower):
    row = lax.broadcasted_iota(jnp.int32, (SUB, SUB), 0)
    col = lax.broadcasted_iota(jnp.int32, (SUB, SUB), 1)
    return (col <= row) if lower else (col >= row)


def part(ref, i):
    return ref[i * SUB : (i + 1) * SUB, :]


def query_body(at_ref, g_ref, v_ref, k_ref, prior_ref, out_ref):
    block = at_ref[1]
    mask = triangle(True)
    hi, lo = split(prior_ref[0])
    ramp = lax.broadcasted_iota(jnp.int32, (SUB, 1), 0)
    for i in range(PARTS):
        g = part(g_ref, i)
        total = dot_t(g, hi) + dot_t(g, lo)
        for j in range(i + 1):
            mix = dot_t(g, part(v_ref, j))
            if j == i:
                mix = jnp.where(mask, mix, 0.0)
            total += dot(mix.astype(bf16), part(k_ref, j))
        count = (3 * BLOCKS * TOK + block * TOK + i * SUB + ramp + 1).astype(f32)
        out_ref[i * SUB : (i + 1) * SUB, :] = (total / count).astype(bf16)


def mix_body(at_ref, a_ref, b_ref, c_ref, out_ref):
    block = at_ref[1]
    mask = triangle(False)
    inverses = [inverse_row(block, j * SUB) for j in range(PARTS)]
    for i in range(PARTS):
        a = part(a_ref, i)
        total = jnp.zeros((SUB, HD), f32)
        for j in range(i, PARTS):
            mix = dot_t(a, part(b_ref, j)) * inverses[j]
            if j == i:
                mix = jnp.where(mask, mix, 0.0)
            total += dot(mix.astype(bf16), part(c_ref, j))
        out_ref[i * SUB : (i + 1) * SUB, :] = total


def head_call(body, name, ins, out_type, prior=None):
    cols = pl.BlockSpec((TOK, HD), lambda h: (0, h))
    specs = [scalars()] + [cols] * 3
    if prior is not None:
        specs.append(pl.BlockSpec((1, HD, HD), lambda h: (h, 0, 0)))
        ins = (*ins, prior)
    return call(
        body,
        name,
        [((TOK, HEADS * HD), out_type)],
        ins,
        10 * HEADS * 4 * SUB * SUB * HD,
        6 << 20,
        grid=(HEADS,),
        in_specs=specs,
        out_specs=[cols],
    )[0]


def final_body(later_ref, v_ref, k_ref, key_ref, value_ref, out_key, out_value):
    for h in range(HEADS):
        cols = slice(h * HD, (h + 1) * HD)
        hi, lo = split(later_ref[h * HD : (h + 1) * HD, :])
        v, k = v_ref[:, cols], k_ref[:, cols]
        out_key[:, cols] = (key_ref[:, cols] + dot_t(v, hi) + dot_t(v, lo)).astype(bf16)
        out_value[:, cols] = (value_ref[:, cols] + dot(k, hi) + dot(k, lo)).astype(bf16)


def index(z, x, c):
    return (z * X + x) * C + c


def spots():
    return [(z, x, c) for z in range(Z) for x in range(X) for c in range(C)]


def along_y(a, s):
    return lax.ppermute(a, "exp", [(i, (i + s) % Y) for i in range(Y)])


def along_x(a, s):
    return lax.ppermute(a, "ctx", [(index(z, x, c), index(z, (x + s) % X, c)) for z, x, c in spots()])


def along_z(a, s):
    return lax.ppermute(a, "ctx", [(index(z, x, c), index((z + s) % Z, x, c)) for z, x, c in spots()])


def across(a):
    return lax.ppermute(a, "ctx", [(i, i ^ 1) for i in range(BLOCKS)])


def on_device(
    attn_query,
    attn_key,
    attn_value,
    prefix_state,
    moe_in,
    grad_out,
    router_gates,
    expert_ids,
    w_gate_up,
    w_down,
    w_out,
):
    y = lax.axis_index("exp")
    block = lax.axis_index("ctx")
    z, x, c = block // (X * C), (block // C) % X, block % C
    at = jnp.stack([y, block]).astype(jnp.int32)
    spot = jnp.stack([z, x]).astype(jnp.int32)
    core = c.astype(jnp.int32)[None]

    slab = w_out.shape[0] // BLOCKS
    piece = lax.dynamic_slice_in_dim(w_out, block * slab, slab, 0)
    pieces = jnp.concatenate([along_y(piece, s) for s in (1, 2, 3)], axis=0)
    rest = lax.all_gather(pieces[None], "ctx", axis=0, tiled=True)
    rest = rest.reshape(BLOCKS, 3, slab, WIDTH)

    place, *chunks = pack(at, expert_ids, router_gates, moe_in, grad_out)
    held = [chunks[0]] + [along_y(chunks[s], s) for s in (1, 2, 3)]
    b0, b1, b2, b3, hidden, grad_both, dots, rows = expert(held, w_gate_up[0], w_down[0])
    back = [b0] + [along_y(b, -s) for s, b in ((1, b1), (2, b2), (3, b3))]
    dots = dots[:, 0].reshape(Y, 1, CAP)
    dots = [dots[0]] + [along_y(dots[s], -s) for s in (1, 2, 3)]

    pair_grads = dot(place, jnp.concatenate(back, axis=0))
    grad_resid = (grad_out.astype(f32) + pair_grads).astype(bf16)
    picked = jnp.sum(place.astype(f32) * jnp.concatenate(dots, axis=1), axis=1, keepdims=True)
    grad_gates = (picked / router_gates.astype(f32)).astype(bf16)

    per_head = call(
        project_body,
        "project",
        [((Y, ROWS, 512), bf16)],
        (w_out, rest, grad_resid),
        2 * ROWS * WIDTH * WIDTH,
        10 << 20,
        grid=(Y,),
        in_specs=[
            pl.BlockSpec((512, WIDTH), lambda s: (0, 0)),
            pl.BlockSpec((BLOCKS, 1, slab, WIDTH), lambda s: (0, jnp.maximum(s - 1, 0), 0, 0)),
            pl.BlockSpec((ROWS, WIDTH), lambda s: (0, 0)),
        ],
        out_specs=[pl.BlockSpec((1, ROWS, 512), lambda s: (s, 0, 0))],
    )[0]
    grads = [per_head[0]] + [along_y(per_head[s], -s) for s in (1, 2, 3)]
    attn_grad, state = call(
        state_body,
        "state",
        [((TOK, HEADS * HD), bf16), ((HEADS * HD, HD), f32)],
        (at, *grads, attn_query),
        HEADS * 2 * TOK * HD * 2 * HD,
        4 << 20,
        in_specs=[scalars()] + [full()] * 5,
    )

    keep, send = weights(core, rows, grad_both, hidden)
    outs = [((Z, 96, 512), bf16)] * 8
    ins = (spot, keep, across(send))
    specs = [scalars()] + [full()] * 2
    half = call(fold_core_body, "fold_core", outs, ins, 0, 9 << 20, in_specs=specs)
    ins = (spot, half[0], *(along_x(half[s], s) for s in (1, 2, 3)))
    ins = (*ins, half[4], *(along_z(half[4 + s], s) for s in (1, 2, 3)))
    outs = ([((96, 512), f32)] + [((96, 512), bf16)] * 3) * 2
    specs = [scalars()] + [full()] * 8
    half = call(fold_axis_body, "fold_axis", outs, ins, 0, 4 << 20, in_specs=specs)
    ins = (half[0], *(along_z(half[s], s) for s in (1, 2, 3)))
    ins = (*ins, half[4], *(along_x(half[4 + s], s) for s in (1, 2, 3)))
    outs = [((1, 64, 1024), f32), ((1, 16, WIDTH), f32)]
    grad_gate_up, grad_down = call(fold_last_body, "fold_last", outs, ins, 0, 2 << 20)

    other = across(state)
    chip = state + other
    chip16 = chip.astype(bf16)
    from_x = [along_x(chip16, s).astype(f32) for s in (1, 2, 3)]
    line = chip + from_x[0] + from_x[1] + from_x[2]
    line16 = line.astype(bf16)
    from_z = [along_z(line16, s).astype(f32) for s in (1, 2, 3)]
    later = jnp.where(c == 0, other, 0.0)
    for s in (1, 2, 3):
        later += jnp.where(s > x, from_x[s - 1], 0.0) + jnp.where(s > z, from_z[s - 1], 0.0)

    grad_query = head_call(query_body, "grad_query", (at, attn_grad, attn_value, attn_key), bf16, prefix_state[0])
    key_here = head_call(mix_body, "mix_key", (at, attn_value, attn_grad, attn_query), f32)
    value_here = head_call(mix_body, "mix_value", (at, attn_key, attn_query, attn_grad), f32)
    shape = (TOK, HEADS * HD)
    grad_key, grad_value = call(
        final_body,
        "final",
        [(shape, bf16), (shape, bf16)],
        (later, attn_value, attn_key, key_here, value_here),
        HEADS * 8 * TOK * HD * HD,
        8 << 20,
    )
    return (grad_query, grad_key, grad_value, grad_resid, grad_gates, grad_gate_up, grad_down)


def solution(mesh):
    whole = P(("ctx", "exp"), None)
    split_cols = P("ctx", "exp")
    return jax.shard_map(
        on_device,
        mesh=mesh,
        in_specs=(
            split_cols,
            split_cols,
            split_cols,
            P("ctx", "exp", None, None),
            whole,
            whole,
            whole,
            whole,
            P("exp", None, None),
            P("exp", None, None),
            P("exp", None),
        ),
        out_specs=(
            split_cols,
            split_cols,
            split_cols,
            whole,
            whole,
            P("exp", "ctx", None),
            P("exp", "ctx", None),
        ),
        check_vma=False,
    )
```

```python
import jax
import jax.numpy as jnp
from jax import lax
from jax.experimental import pallas as pl
from jax.experimental.pallas import tpu as pltpu
from jax.sharding import PartitionSpec as P

bf16 = jnp.bfloat16
f32 = jnp.float32
VMEM = pltpu.VMEM
SMEM = pltpu.SMEM
Z, X, C, Y = 4, 4, 2, 4
CAP, ROWS, WIDTH, FF, HD, HEADS, TOK = 96, 256, 2048, 512, 128, 4, 1024
BLOCKS = Z * X * C


def dot(a, b):
    return lax.dot_general(a, b, (((1,), (0,)), ((), ())), preferred_element_type=f32)


def dot_t(a, b):
    return lax.dot_general(a, b, (((1,), (1,)), ((), ())), preferred_element_type=f32)


def t_dot(a, b):
    return lax.dot_general(a, b, (((0,), (0,)), ((), ())), preferred_element_type=f32)


def split(a):
    hi = a.astype(bf16)
    return hi, (a - hi.astype(f32)).astype(bf16)


def full():
    return pl.BlockSpec(memory_space=VMEM)


def scalars():
    return pl.BlockSpec(memory_space=SMEM)


def call(body, name, outs, ins, flops=0, moved=0, grid=None, in_specs=None, out_specs=None, limit=24, scratch=()):
    kwargs = {} if grid is None else {"grid": grid}
    return pl.pallas_call(
        body,
        name=name,
        out_shape=[jax.ShapeDtypeStruct(s, t) for s, t in outs],
        in_specs=in_specs or [full() for _ in ins],
        out_specs=out_specs or [full() for _ in outs],
        scratch_shapes=scratch,
        compiler_params=pltpu.CompilerParams(vmem_limit_bytes=limit << 20),
        cost_estimate=pl.CostEstimate(flops=flops, bytes_accessed=moved, transcendentals=0),
        **kwargs,
    )(*ins)


def pack_body(at_ref, ids_ref, gate_ref, moe_ref, cot_ref, place_ref, c0, c1, c2, c3, gate_col):
    @pl.when(pl.program_id(0) == 0)
    def _():
        rel = ids_ref[...] - at_ref[0]
        rel = jnp.where(rel < 0, rel + Y, rel)
        member = (lax.broadcasted_iota(jnp.int32, (8, ROWS), 0) == rel).astype(f32)
        row = lax.broadcasted_iota(jnp.int32, (ROWS, ROWS), 0)
        col = lax.broadcasted_iota(jnp.int32, (ROWS, ROWS), 1)
        earlier = dot(member.astype(bf16), (row < col).astype(bf16))
        slot = jnp.sum(earlier * member, axis=0, keepdims=True).astype(jnp.int32)
        target = rel * CAP + slot
        places = lax.broadcasted_iota(jnp.int32, (Y * CAP, ROWS), 0)
        place_ref[...] = (places == target).astype(bf16)
        gate = gate_ref[...].astype(f32)
        gate_col[...] = jnp.sum(jnp.where(row == col, gate, 0.0), axis=1, keepdims=True)

    place = place_ref[...]
    scaled = (gate_col[...] * cot_ref[...].astype(f32)).astype(bf16)
    for half, rows in enumerate((moe_ref[...], scaled)):
        part = dot(place, rows).astype(bf16)
        for s, chunk in enumerate((c0, c1, c2, c3)):
            chunk[half] = part[s * CAP : (s + 1) * CAP]


def pack(at, ids, gates, moe_in, grad_out):
    step = 512
    outs = [((Y * CAP, ROWS), bf16)] + [((2, CAP, WIDTH), bf16)] * Y
    ins = (at, ids, gates, moe_in, grad_out)
    row = pl.BlockSpec((1, ROWS), lambda j: (0, 0))
    tile = pl.BlockSpec((ROWS, step), lambda j: (0, j))
    return call(
        pack_body,
        "pack",
        outs,
        ins,
        2 * 384 * 256 * 4096,
        5 << 20,
        grid=(WIDTH // step,),
        in_specs=[scalars(), row, row, tile, tile],
        out_specs=[pl.BlockSpec((Y * CAP, ROWS), lambda j: (0, 0))]
        + [pl.BlockSpec((2, CAP, step), lambda j: (0, 0, j))] * Y,
        scratch=[VMEM((ROWS, 1), f32)],
        limit=16,
    )


BACK = WIDTH + 128


def expert_body(r0, r1, r2, r3, wp_ref, wb_ref, b0, b1, b2, b3, hid_ref, gb_ref, rows_ref, cots_ref):
    for s, r in enumerate((r0, r1, r2, r3)):
        rows_ref[s * CAP : (s + 1) * CAP, :] = r[0]
        cots_ref[s * CAP : (s + 1) * CAP, :] = r[1]
    step = 256
    total = jnp.zeros((Y * CAP, 1), f32)
    for j in range(FF // step):
        at, up = j * step, FF + j * step
        first = dot(rows_ref[...], wp_ref[:, at : at + step])
        second = dot(rows_ref[...], wp_ref[:, up : up + step])
        grad_hidden = dot_t(cots_ref[...], wb_ref[at : at + step, :])
        s = 1.0 / (1.0 + jnp.exp(-first))
        silu = first * s
        hidden = (silu * second).astype(bf16)
        hid_ref[:, at : at + step] = hidden
        total += jnp.sum(hidden.astype(f32) * grad_hidden, axis=1, keepdims=True)
        slope = s * (1.0 + first * (1.0 - s))
        gb_ref[:, at : at + step] = (grad_hidden * second * slope).astype(bf16)
        gb_ref[:, up : up + step] = (grad_hidden * silu).astype(bf16)
    backs = (b0, b1, b2, b3)
    hi, lo = split(total)
    lane = lax.broadcasted_iota(jnp.int32, (Y * CAP, 128), 1)
    tail = jnp.where(lane == 0, hi.astype(f32), lo.astype(f32)).astype(bf16)
    for s, b in enumerate(backs):
        b[:, WIDTH:] = tail[s * CAP : (s + 1) * CAP]
    for j in range(WIDTH // step):
        at = j * step
        back = dot_t(gb_ref[...], wp_ref[at : at + step, :]).astype(bf16)
        for s, b in enumerate(backs):
            b[:, at : at + step] = back[s * CAP : (s + 1) * CAP]


def expert(chunks, w_pair, w_back):
    n = Y * CAP
    outs = [((CAP, BACK), bf16)] * Y
    outs += [((n, FF), bf16), ((n, 2 * FF), bf16), ((n, WIDTH), bf16), ((n, WIDTH), bf16)]
    return call(expert_body, "expert", outs, (*chunks, w_pair, w_back), 5 * 2 * n * WIDTH * FF, 14 << 20)


def weights_body(core_ref, rows_ref, scaled_ref, gb_ref, hid_ref, keep_ref, send_ref):
    mine = core_ref[0] == 0
    up = t_dot(rows_ref[...], gb_ref[...])
    down = t_dot(hid_ref[...], scaled_ref[...])
    for k in range(X):
        for even, odd, narrow in (
            (up[k * 128 : k * 128 + 64], up[k * 128 + 64 : k * 128 + 128], True),
            (down[k * 32 : k * 32 + 16], down[k * 32 + 16 : k * 32 + 32], False),
        ):
            keep = jnp.where(mine, even, odd).astype(bf16)
            send = jnp.where(mine, odd, even).astype(bf16)
            for ref, value in ((keep_ref, keep), (send_ref, send)):
                if narrow:
                    ref[k, :64, :] = value
                else:
                    ref[k, 64:80, :] = value[:, :1024]
                    ref[k, 80:96, :] = value[:, 1024:]


def weights(core, rows, scaled, grad_both, hidden):
    n = Y * CAP
    shape = (Z * X, 96, 1024)
    block = pl.BlockSpec((X, 96, 1024), lambda i: (i, 0, 0))
    return call(
        weights_body,
        "weights",
        [(shape, bf16), (shape, bf16)],
        (core, rows, scaled, grad_both, hidden),
        3 * 2 * n * WIDTH * FF,
        12 << 20,
        grid=(Z,),
        in_specs=[
            scalars(),
            pl.BlockSpec((n, 512), lambda i: (0, i)),
            pl.BlockSpec((n, WIDTH), lambda i: (0, 0)),
            pl.BlockSpec((n, 2 * FF), lambda i: (0, 0)),
            pl.BlockSpec((n, 128), lambda i: (0, i)),
        ],
        out_specs=[block, block],
    )


def gather_sum_body(pieces_ref, up_ref, down_ref):
    for j in range(2):
        at = j * 512
        total = pieces_ref[0, :, at : at + 512].astype(f32)
        for k in range(1, Z * X):
            total = total + pieces_ref[k, :, at : at + 512].astype(f32)
        up_ref[0, :, at : at + 512] = total[:64]
        down_ref[0, :, at : at + 512] = total[64:80]
        down_ref[0, :, 1024 + at : 1024 + at + 512] = total[80:96]


def project_body(own_ref, rest_ref, place_ref, gate_ref, cot_ref, r0, r1, r2, r3, resid_ref, gates_ref, *outs):
    step = pl.program_id(0)
    backs = (r0, r1, r2, r3)

    @pl.when(step == 0)
    def _():
        place = place_ref[...]
        wide = 512
        for j in range(WIDTH // wide):
            cols = slice(j * wide, (j + 1) * wide)
            back = jnp.concatenate([b[:, cols] for b in backs], axis=0)
            resid_ref[:, cols] = (cot_ref[:, cols].astype(f32) + t_dot(place, back)).astype(bf16)
        tail = jnp.concatenate([b[:, WIDTH:] for b in backs], axis=0).astype(f32)
        picked = jnp.sum(place.astype(f32) * (tail[:, 0:1] + tail[:, 1:2]), axis=0, keepdims=True)
        gates_ref[...] = (picked / gate_ref[...].astype(f32)).astype(bf16)
        outs[0][...] = dot_t(resid_ref[...], own_ref[...]).astype(bf16)

    for s in range(1, Y):

        @pl.when(step == s)
        def _():
            outs[s][...] = dot_t(resid_ref[...], rest_ref[...].reshape(512, WIDTH)).astype(bf16)


def project(w_out, rest, place, gate_row, grad_out, backs):
    def once(shape):
        return pl.BlockSpec(shape, lambda s: (0,) * len(shape))

    slab = rest.shape[2]
    shapes = [(ROWS, WIDTH), (1, ROWS)] + [(ROWS, 512)] * Y
    return call(
        project_body,
        "project",
        [(s, bf16) for s in shapes],
        (w_out, rest, place, gate_row, grad_out, *backs),
        2 * ROWS * WIDTH * WIDTH + 2 * ROWS * 384 * WIDTH,
        10 << 20,
        grid=(Y,),
        in_specs=[
            once((512, WIDTH)),
            pl.BlockSpec((BLOCKS, 1, slab, WIDTH), lambda s: (0, jnp.maximum(s - 1, 0), 0, 0)),
            once((Y * CAP, ROWS)),
            once((1, ROWS)),
            once((ROWS, WIDTH)),
        ]
        + [once((CAP, BACK))] * Y,
        out_specs=[once(s) for s in shapes],
    )


def state_body(at_ref, g0, g1, g2, g3, q_ref, grad_ref, state_ref):
    y, block = at_ref[0], at_ref[1]
    ramp = lax.broadcasted_iota(jnp.int32, (ROWS, 1), 0)
    sums = [jnp.zeros((HD, 2 * HD), f32) for _ in range(HEADS)]
    for s, g in enumerate((g0, g1, g2, g3)):
        off = pl.multiple_of(lax.rem(y + s, Y) * ROWS, ROWS)
        inverse = 1.0 / (3 * BLOCKS * TOK + block * TOK + off + ramp + 1).astype(f32)
        grad_ref[pl.ds(off, ROWS), :] = g[...]
        for h in range(HEADS):
            cols = slice(h * HD, (h + 1) * HD)
            hi, lo = split(g[:, cols].astype(f32) * inverse)
            both = jnp.concatenate([hi, lo], axis=1)
            sums[h] += t_dot(q_ref[pl.ds(off, ROWS), cols], both)
    for h in range(HEADS):
        state_ref[h * HD : (h + 1) * HD, :] = sums[h][:, :HD] + sums[h][:, HD:]


SUB = 256
PARTS = TOK // SUB
PAIR = 2


def triangle(lower):
    row = lax.broadcasted_iota(jnp.int32, (SUB, SUB), 0)
    col = lax.broadcasted_iota(jnp.int32, (SUB, SUB), 1)
    return (col <= row) if lower else (col >= row)


def query_body(at_ref, g_ref, v_ref, k_ref, prior_ref, out_ref):
    block = at_ref[1]
    mask = triangle(True)
    ramp = lax.broadcasted_iota(jnp.int32, (SUB, 1), 0)
    for h in range(PAIR):
        cols = slice(h * HD, (h + 1) * HD)
        prior = jnp.concatenate(split(prior_ref[h]), axis=0)
        for i in range(PARTS):
            rows, upto = slice(i * SUB, (i + 1) * SUB), (i + 1) * SUB
            g = g_ref[rows, cols]
            mix = dot_t(g, v_ref[:upto, cols])
            edge = jnp.where(mask, mix[:, i * SUB :], 0.0).astype(bf16)
            if i:
                edge = jnp.concatenate([mix[:, : i * SUB].astype(bf16), edge], axis=1)
            before = dot_t(g, prior)
            total = before[:, :HD] + before[:, HD:] + dot(edge, k_ref[:upto, cols])
            count = (3 * BLOCKS * TOK + block * TOK + i * SUB + ramp + 1).astype(f32)
            out_ref[rows, cols] = (total / count).astype(bf16)


def mix_body(at_ref, a_ref, b_ref, c_ref, out_ref):
    block = at_ref[1]
    mask = triangle(False)
    ramp = lax.broadcasted_iota(jnp.int32, (1, TOK), 1)
    inverse = 1.0 / (3 * BLOCKS * TOK + block * TOK + ramp + 1).astype(f32)
    for h in range(PAIR):
        cols = slice(h * HD, (h + 1) * HD)
        for i in range(PARTS):
            at = i * SUB
            rows = slice(at, at + SUB)
            mix = dot_t(a_ref[rows, cols], b_ref[at:, cols]) * inverse[:, at:]
            edge = jnp.where(mask, mix[:, :SUB], 0.0).astype(bf16)
            if i < PARTS - 1:
                edge = jnp.concatenate([edge, mix[:, SUB:].astype(bf16)], axis=1)
            out_ref[rows, cols] = dot(edge, c_ref[at:, cols])


def head_call(body, name, ins, out_type, prior=None):
    cols = pl.BlockSpec((TOK, PAIR * HD), lambda h: (0, h))
    specs = [scalars()] + [cols] * 3
    if prior is not None:
        specs.append(pl.BlockSpec((PAIR, HD, HD), lambda h: (h, 0, 0)))
        ins = (*ins, prior)
    return call(
        body,
        name,
        [((TOK, HEADS * HD), out_type)],
        ins,
        10 * HEADS * 4 * SUB * SUB * HD,
        6 << 20,
        grid=(HEADS // PAIR,),
        in_specs=specs,
        out_specs=[cols],
    )[0]


def final_body(later_ref, v_ref, k_ref, key_ref, value_ref, out_key, out_value):
    hi, lo = split(later_ref[...])
    key = dot_t(v_ref[...], jnp.concatenate([hi, lo], axis=0))
    out_key[...] = (key_ref[...] + key[:, :HD] + key[:, HD:]).astype(bf16)
    value = dot(k_ref[...], jnp.concatenate([hi, lo], axis=1))
    out_value[...] = (value_ref[...] + value[:, :HD] + value[:, HD:]).astype(bf16)


def final(later, values, keys, key_here, value_here):
    cols = pl.BlockSpec((TOK, HD), lambda h: (0, h))
    return call(
        final_body,
        "final",
        [((TOK, HEADS * HD), bf16)] * 2,
        (later, values, keys, key_here, value_here),
        HEADS * 8 * TOK * HD * HD,
        8 << 20,
        grid=(HEADS,),
        in_specs=[pl.BlockSpec((HD, HD), lambda h: (h, 0))] + [cols] * 4,
        out_specs=[cols, cols],
    )


def index(z, x, c):
    return (z * X + x) * C + c


def spots():
    return [(z, x, c) for z in range(Z) for x in range(X) for c in range(C)]


def along_y(a, s):
    return lax.ppermute(a, "exp", [(i, (i + s) % Y) for i in range(Y)])


def along_x(a, s):
    return lax.ppermute(a, "ctx", [(index(z, x, c), index(z, (x + s) % X, c)) for z, x, c in spots()])


def along_z(a, s):
    return lax.ppermute(a, "ctx", [(index(z, x, c), index((z + s) % Z, x, c)) for z, x, c in spots()])


def across(a):
    return lax.ppermute(a, "ctx", [(i, i ^ 1) for i in range(BLOCKS)])


def on_device(
    attn_query,
    attn_key,
    attn_value,
    prefix_state,
    moe_in,
    grad_out,
    router_gates,
    expert_ids,
    w_gate_up,
    w_down,
    w_out,
):
    y = lax.axis_index("exp")
    block = lax.axis_index("ctx")
    z, x, c = block >> 3, (block >> 1) & 3, block & 1
    at = jnp.stack([y, block]).astype(jnp.int32)
    core = c.astype(jnp.int32)[None]

    slab = w_out.shape[0] // BLOCKS
    piece = lax.dynamic_slice_in_dim(w_out, block * slab, slab, 0)
    pieces = jnp.concatenate([along_y(piece, s) for s in (1, 2, 3)], axis=0)
    gate_row = router_gates.reshape(1, ROWS)
    place, *chunks = pack(at, expert_ids.reshape(1, ROWS), gate_row, moe_in, grad_out)
    pieces, chunks[1] = lax.optimization_barrier((pieces, chunks[1]))
    rest = lax.all_gather(pieces[None], "ctx", axis=0, tiled=True)
    rest = rest.reshape(BLOCKS, 3, slab, WIDTH)

    held = [chunks[0]] + [along_y(chunks[s], s) for s in (1, 2, 3)]
    b0, b1, b2, b3, hidden, grad_both, rows, scaled = expert(held, w_gate_up[0], w_down[0])
    backs = [b0] + [along_y(b, -s) for s, b in ((1, b1), (2, b2), (3, b3))]
    keep, send = weights(core, rows, scaled, grad_both, hidden)
    send, backs[1], backs[2], backs[3] = lax.optimization_barrier((send, backs[1], backs[2], backs[3]))
    recv = across(send)

    grad_resid, gates_out, *per_head = project(w_out, rest, place, gate_row, grad_out, backs)
    grad_gates = gates_out.reshape(ROWS, 1)
    grads = [per_head[0]] + [along_y(per_head[s], -s) for s in (1, 2, 3)]
    attn_grad, state = call(
        state_body,
        "state",
        [((TOK, HEADS * HD), bf16), ((HEADS * HD, HD), f32)],
        (at, *grads, attn_query),
        HEADS * 2 * TOK * HD * 2 * HD,
        4 << 20,
        in_specs=[scalars()] + [full()] * 5,
    )

    recv, _ = lax.optimization_barrier((recv, per_head[0]))
    folded = (keep.astype(f32) + recv.astype(f32)).astype(bf16)
    groups = [[index(i, j, k) for i in range(Z) for j in range(X)] for k in range(C)]
    exchanged = lax.all_to_all(folded, "ctx", 0, 0, axis_index_groups=groups, tiled=True)

    other = across(state)
    chip = state + other
    chip16 = chip.astype(bf16)
    from_x = [along_x(chip16, s).astype(f32) for s in (1, 2, 3)]
    line = chip + from_x[0] + from_x[1] + from_x[2]
    line16 = line.astype(bf16)
    from_z = [along_z(line16, s).astype(f32) for s in (1, 2, 3)]
    later = jnp.where(c == 0, other, 0.0)
    for s in (1, 2, 3):
        later += jnp.where(s > x, from_x[s - 1], 0.0) + jnp.where(s > z, from_z[s - 1], 0.0)

    grad_query = head_call(query_body, "grad_query", (at, attn_grad, attn_value, attn_key), bf16, prefix_state[0])
    key_here = head_call(mix_body, "mix_key", (at, attn_value, attn_grad, attn_query), f32)
    value_here = head_call(mix_body, "mix_value", (at, attn_key, attn_query, attn_grad), f32)
    grad_key, grad_value = final(later, attn_value, attn_key, key_here, value_here)

    exchanged, grad_key = lax.optimization_barrier((exchanged, grad_key))
    outs = [((1, 64, 1024), f32), ((1, 16, WIDTH), f32)]
    grad_gate_up, grad_down = call(gather_sum_body, "gather_sum", outs, (exchanged,), 0, 4 << 20)
    return (grad_query, grad_key, grad_value, grad_resid, grad_gates, grad_gate_up, grad_down)


def solution(mesh):
    whole = P(("ctx", "exp"), None)
    split_cols = P("ctx", "exp")
    return jax.shard_map(
        on_device,
        mesh=mesh,
        in_specs=(
            split_cols,
            split_cols,
            split_cols,
            P("ctx", "exp", None, None),
            whole,
            whole,
            whole,
            whole,
            P("exp", None, None),
            P("exp", None, None),
            P("exp", None),
        ),
        out_specs=(
            split_cols,
            split_cols,
            split_cols,
            whole,
            whole,
            P("exp", "ctx", None),
            P("exp", "ctx", None),
        ),
        check_vma=False,
    )
```

```python
import jax
import jax.numpy as jnp
from jax import lax
from jax.experimental import pallas as pl
from jax.experimental.pallas import tpu as pltpu
from jax.sharding import PartitionSpec as P

bf16 = jnp.bfloat16
f32 = jnp.float32
VMEM = pltpu.VMEM
SMEM = pltpu.SMEM
Z, X, C, Y = 4, 4, 2, 4
CAP, ROWS, WIDTH, FF, HD, HEADS, TOK = 96, 256, 2048, 512, 128, 4, 1024
WEIGHT = 4
BLOCKS = Z * X * C


def dot(a, b):
    return lax.dot_general(a, b, (((1,), (0,)), ((), ())), preferred_element_type=f32)


def dot_t(a, b):
    return lax.dot_general(a, b, (((1,), (1,)), ((), ())), preferred_element_type=f32)


def t_dot(a, b):
    return lax.dot_general(a, b, (((0,), (0,)), ((), ())), preferred_element_type=f32)


def split(a):
    hi = a.astype(bf16)
    return hi, (a - hi.astype(f32)).astype(bf16)


def full():
    return pl.BlockSpec(memory_space=VMEM)


def scalars():
    return pl.BlockSpec(memory_space=SMEM)


def call(body, name, outs, ins, flops=0, moved=0, grid=None, in_specs=None, out_specs=None, limit=24, scratch=(), free=()):
    kwargs = {} if grid is None else {"grid": grid}
    specs = in_specs or [full() for _ in ins]
    ins = [
        a if spec.memory_space is SMEM or i in free else pltpu.with_memory_space_constraint(a, pltpu.HBM)
        for i, (a, spec) in enumerate(zip(ins, specs))
    ]
    return pl.pallas_call(
        body,
        name=name,
        out_shape=[pltpu.HBM(s, t) for s, t in outs],
        in_specs=specs,
        out_specs=out_specs or [full() for _ in outs],
        scratch_shapes=scratch,
        compiler_params=pltpu.CompilerParams(vmem_limit_bytes=limit << 20),
        cost_estimate=pl.CostEstimate(flops=WEIGHT * flops, bytes_accessed=WEIGHT * moved, transcendentals=0),
        **kwargs,
    )(*ins)


def pack_body(at_ref, ids_ref, gate_ref, moe_ref, cot_ref, place_ref, c0, c1, c2, c3, gate_col):
    @pl.when(pl.program_id(0) == 0)
    def _():
        rel = ids_ref[...] - at_ref[0]
        rel = jnp.where(rel < 0, rel + Y, rel)
        member = (lax.broadcasted_iota(jnp.int32, (8, ROWS), 0) == rel).astype(f32)
        row = lax.broadcasted_iota(jnp.int32, (ROWS, ROWS), 0)
        col = lax.broadcasted_iota(jnp.int32, (ROWS, ROWS), 1)
        earlier = dot(member.astype(bf16), (row < col).astype(bf16))
        slot = jnp.sum(earlier * member, axis=0, keepdims=True).astype(jnp.int32)
        target = rel * CAP + slot
        places = lax.broadcasted_iota(jnp.int32, (Y * CAP, ROWS), 0)
        place_ref[...] = (places == target).astype(bf16)
        gate = gate_ref[...].astype(f32)
        gate_col[...] = jnp.sum(jnp.where(row == col, gate, 0.0), axis=1, keepdims=True)

    place = place_ref[...]
    scaled = (gate_col[...] * cot_ref[...].astype(f32)).astype(bf16)
    for half, rows in enumerate((moe_ref[...], scaled)):
        part = dot(place, rows).astype(bf16)
        for s, chunk in enumerate((c0, c1, c2, c3)):
            chunk[half] = part[s * CAP : (s + 1) * CAP]


def pack(at, ids, gates, moe_in, grad_out):
    step = 512
    outs = [((Y * CAP, ROWS), bf16)] + [((2, CAP, WIDTH), bf16)] * Y
    ins = (at, ids, gates, moe_in, grad_out)
    row = pl.BlockSpec((1, ROWS), lambda j: (0, 0))
    tile = pl.BlockSpec((ROWS, step), lambda j: (0, j))
    return call(
        pack_body,
        "pack",
        outs,
        ins,
        2 * 384 * 256 * 4096,
        5 << 20,
        grid=(WIDTH // step,),
        in_specs=[scalars(), row, row, tile, tile],
        out_specs=[pl.BlockSpec((Y * CAP, ROWS), lambda j: (0, 0))]
        + [pl.BlockSpec((2, CAP, step), lambda j: (0, 0, j))] * Y,
        scratch=[VMEM((ROWS, 1), f32)],
        limit=16,
    )


BACK = WIDTH + 128
N = Y * CAP
BUNDLE = 2 * WIDTH + 3 * FF
GB, HID = 2 * WIDTH, 2 * WIDTH + 2 * FF
STEP = 256


def expert_body(r0, r1, r2, r3, wp_hbm, wb_hbm, b0, b1, b2, b3, out_hbm, held, back, wp, wb, in_sem, w_sem, out_sem):
    arrived = (r0, r1, r2, r3)
    backs = (b0, b1, b2, b3)
    tiles = FF // STEP

    def incoming(half, s):
        dst = held.at[pl.ds(s * CAP, CAP), pl.ds(half * WIDTH, WIDTH)]
        return pltpu.make_async_copy(arrived[s].at[half], dst, in_sem.at[half * Y + s])

    def weight(j):
        cols, ups = pl.ds(j * STEP, STEP), pl.ds(FF + j * STEP, STEP)
        return (
            pltpu.make_async_copy(wp_hbm.at[0, :, cols], wp.at[:, cols], w_sem.at[3 * j]),
            pltpu.make_async_copy(wp_hbm.at[0, :, ups], wp.at[:, ups], w_sem.at[3 * j + 1]),
            pltpu.make_async_copy(wb_hbm.at[0, cols, :], wb.at[cols, :], w_sem.at[3 * j + 2]),
        )

    for s in range(Y):
        incoming(0, s).start()
    first_tile = weight(0)
    first_tile[0].start()
    first_tile[1].start()
    for s in range(Y):
        incoming(1, s).start()
    first_tile[2].start()
    for j in range(1, tiles):
        for copy in weight(j):
            copy.start()
    for s in range(Y):
        incoming(0, s).wait()
    total = jnp.zeros((N, 1), f32)
    for j in range(tiles):
        at, up = j * STEP, FF + j * STEP
        copies = weight(j)
        copies[0].wait()
        first = dot(held[:, :WIDTH], wp[:, at : at + STEP])
        copies[1].wait()
        second = dot(held[:, :WIDTH], wp[:, up : up + STEP])
        if j == 0:
            for s in range(Y):
                incoming(1, s).wait()
            rows_out = pltpu.make_async_copy(held.at[:, pl.ds(0, GB)], out_hbm.at[:, pl.ds(0, GB)], out_sem.at[0])
            rows_out.start()
        copies[2].wait()
        grad_hidden = dot_t(held[:, WIDTH:GB], wb[at : at + STEP, :])
        s = 1.0 / (1.0 + jnp.exp(-first))
        silu = first * s
        hidden = (silu * second).astype(bf16)
        held[:, HID + at : HID + at + STEP] = hidden
        total += jnp.sum(hidden.astype(f32) * grad_hidden, axis=1, keepdims=True)
        slope = s * (1.0 + first * (1.0 - s))
        held[:, GB + at : GB + at + STEP] = (grad_hidden * second * slope).astype(bf16)
        held[:, GB + up : GB + up + STEP] = (grad_hidden * silu).astype(bf16)
    rest = pl.ds(GB, BUNDLE - GB)
    grads_out = pltpu.make_async_copy(held.at[:, rest], out_hbm.at[:, rest], out_sem.at[1])
    grads_out.start()
    hi, lo = split(total)
    lane = lax.broadcasted_iota(jnp.int32, (N, 128), 1)
    back[:, WIDTH:] = jnp.where(lane == 0, hi.astype(f32), lo.astype(f32)).astype(bf16)
    outgoing = []
    bounds = (0, WIDTH // 2, BACK)
    for part in range(2):
        lo_col, hi_col = bounds[part], bounds[part + 1]
        for at in range(lo_col, min(hi_col, WIDTH), STEP):
            back[:, at : at + STEP] = dot_t(held[:, GB:HID], wp[at : at + STEP, :]).astype(bf16)
        cols = pl.ds(lo_col, hi_col - lo_col)
        for s in range(Y):
            src = back.at[pl.ds(s * CAP, CAP), cols]
            copy = pltpu.make_async_copy(src, backs[s].at[:, cols], out_sem.at[2 + part * Y + s])
            copy.start()
            outgoing.append(copy)
    rows_out.wait()
    grads_out.wait()
    for copy in outgoing:
        copy.wait()


def anywhere():
    return pl.BlockSpec(memory_space=pl.ANY)


def expert(chunks, w_pair, w_back):
    outs = [((CAP, BACK), bf16)] * Y + [((N, BUNDLE), bf16)]
    ins = (*chunks, w_pair, w_back)
    return call(
        expert_body,
        "expert",
        outs,
        ins,
        5 * 2 * N * WIDTH * FF,
        14 << 20,
        in_specs=[anywhere() for _ in ins],
        out_specs=[anywhere() for _ in outs],
        scratch=[
            VMEM((N, BUNDLE), bf16),
            VMEM((N, BACK), bf16),
            VMEM((WIDTH, 2 * FF), bf16),
            VMEM((FF, WIDTH), bf16),
            pltpu.SemaphoreType.DMA((2 * Y,)),
            pltpu.SemaphoreType.DMA((3 * FF // STEP,)),
            pltpu.SemaphoreType.DMA((2 + 2 * Y,)),
        ],
        limit=32,
        free=(1, 2, 3),
    )


def chooser(core, wide, run):
    row = lax.broadcasted_iota(jnp.int32, (wide, wide // 2), 0)
    col = lax.broadcasted_iota(jnp.int32, (wide, wide // 2), 1)
    return (row == (col // run) * (2 * run) + core * run + col % run).astype(bf16)


def weights_body(core_ref, ra, sa, ga, ha, rb, sb, gb, hb, out_ref):
    core = core_ref[0]
    pick_row, pick_hid = chooser(core, 512, 64), chooser(core, 128, 16)
    up = down = None
    for r, s, g, h in ((ra, sa, ga, ha), (rb, sb, gb, hb)):
        rows = dot(r[...], pick_row).astype(bf16)
        hid = dot(h[...], pick_hid).astype(bf16)
        more_up, more_down = t_dot(rows, g[...]), t_dot(hid, s[...])
        up = more_up if up is None else up + more_up
        down = more_down if down is None else down + more_down
    up, down = up.astype(bf16), down.astype(bf16)
    for k in range(X):
        out_ref[k, :64, :] = up[k * 64 : k * 64 + 64]
        out_ref[k, 64:80, :] = down[k * 16 : k * 16 + 16, :1024]
        out_ref[k, 80:96, :] = down[k * 16 : k * 16 + 16, 1024:]


def weights(core, mine, other):
    specs = [
        pl.BlockSpec((N, 512), lambda i: (0, i)),
        pl.BlockSpec((N, WIDTH), lambda i: (0, 1)),
        pl.BlockSpec((N, 2 * FF), lambda i: (0, GB // (2 * FF))),
        pl.BlockSpec((N, 128), lambda i: (0, HID // 128 + i)),
    ]
    return call(
        weights_body,
        "weights",
        [((Z * X, 96, 1024), bf16)],
        (core, *([mine] * 4), *([other] * 4)),
        3 * 2 * N * WIDTH * FF,
        12 << 20,
        grid=(Z,),
        in_specs=[scalars()] + specs + specs,
        out_specs=[pl.BlockSpec((X, 96, 1024), lambda i: (i, 0, 0))],
        limit=32,
    )[0]


def gather_sum_body(pieces_ref, up_ref, down_ref):
    for j in range(2):
        at = j * 512
        total = pieces_ref[0, :, at : at + 512].astype(f32)
        for k in range(1, Z * X):
            total = total + pieces_ref[k, :, at : at + 512].astype(f32)
        up_ref[0, :, at : at + 512] = total[:64]
        down_ref[0, :, at : at + 512] = total[64:80]
        down_ref[0, :, 1024 + at : 1024 + at + 512] = total[80:96]


def project_body(*refs):
    own, rest, place_hbm, gate, cot_hbm, r0, r1, r2, r3, resid_hbm, gates, o0, o1, o2, o3 = refs[:15]
    place, cot, back, w, resid, outs, in_sem, w_sem, out_sem = refs[15:]
    copies = [
        pltpu.make_async_copy(r, back.at[pl.ds(s * CAP, CAP), :], in_sem.at[s]) for s, r in enumerate((r0, r1, r2, r3))
    ]
    copies.append(pltpu.make_async_copy(place_hbm, place, in_sem.at[4]))
    copies.append(pltpu.make_async_copy(cot_hbm, cot, in_sem.at[5]))
    slabs = [pltpu.make_async_copy(own, w.at[0], w_sem.at[0])]
    for s in range(1, Y):
        slabs.append(pltpu.make_async_copy(rest.at[:, s - 1], w.at[s].reshape(rest.shape[0], -1, WIDTH), w_sem.at[s]))
    for copy in copies + slabs:
        copy.start()
    for copy in copies:
        copy.wait()
    wide = 512
    for j in range(WIDTH // wide):
        cols = slice(j * wide, (j + 1) * wide)
        resid[:, cols] = (cot[:, cols].astype(f32) + t_dot(place[...], back[:, cols])).astype(bf16)
    sent = [pltpu.make_async_copy(resid, resid_hbm, out_sem.at[4])]
    sent[0].start()
    tail = back[:, WIDTH:].astype(f32)
    picked = jnp.sum(place[...].astype(f32) * (tail[:, 0:1] + tail[:, 1:2]), axis=0, keepdims=True)
    gates[...] = (picked / gate[...].astype(f32)).astype(bf16)
    for s, out in enumerate((o0, o1, o2, o3)):
        slabs[s].wait()
        outs[s] = dot_t(resid[...], w[s]).astype(bf16)
        copy = pltpu.make_async_copy(outs.at[s], out, out_sem.at[s])
        copy.start()
        sent.append(copy)
    for copy in sent:
        copy.wait()


def project(w_out, rest, place, gate_row, grad_out, backs):
    shapes = [(ROWS, WIDTH), (1, ROWS)] + [(ROWS, 512)] * Y
    ins = (w_out, rest, place, gate_row, grad_out, *backs)
    in_specs, out_specs = [anywhere() for _ in ins], [anywhere() for _ in shapes]
    in_specs[3], out_specs[1] = full(), full()
    return call(
        project_body,
        "project",
        [(s, bf16) for s in shapes],
        ins,
        2 * ROWS * WIDTH * WIDTH + 2 * ROWS * N * WIDTH,
        10 << 20,
        in_specs=in_specs,
        out_specs=out_specs,
        scratch=[
            VMEM((N, ROWS), bf16),
            VMEM((ROWS, WIDTH), bf16),
            VMEM((N, BACK), bf16),
            VMEM((Y, 512, WIDTH), bf16),
            VMEM((ROWS, WIDTH), bf16),
            VMEM((Y, ROWS, 512), bf16),
            pltpu.SemaphoreType.DMA((6,)),
            pltpu.SemaphoreType.DMA((Y,)),
            pltpu.SemaphoreType.DMA((Y + 1,)),
        ],
        limit=32,
    )


def state_body(at_ref, g0, g1, g2, g3, q_ref, grad_ref, state_ref):
    y, block = at_ref[0], at_ref[1]
    ramp = lax.broadcasted_iota(jnp.int32, (ROWS, 1), 0)
    sums = [jnp.zeros((HD, 2 * HD), f32) for _ in range(HEADS)]
    for s, g in enumerate((g0, g1, g2, g3)):
        off = pl.multiple_of(lax.rem(y + s, Y) * ROWS, ROWS)
        inverse = 1.0 / (3 * BLOCKS * TOK + block * TOK + off + ramp + 1).astype(f32)
        grad_ref[pl.ds(off, ROWS), :] = g[...]
        for h in range(HEADS):
            cols = slice(h * HD, (h + 1) * HD)
            hi, lo = split(g[:, cols].astype(f32) * inverse)
            both = jnp.concatenate([hi, lo], axis=1)
            sums[h] += t_dot(q_ref[pl.ds(off, ROWS), cols], both)
    for h in range(HEADS):
        state_ref[h * HD : (h + 1) * HD, :] = sums[h][:, :HD] + sums[h][:, HD:]


SUB = 256
PARTS = TOK // SUB
PAIR = 2


def triangle(lower):
    row = lax.broadcasted_iota(jnp.int32, (SUB, SUB), 0)
    col = lax.broadcasted_iota(jnp.int32, (SUB, SUB), 1)
    return (col <= row) if lower else (col >= row)


def query_part(block, h, g_ref, v_ref, k_ref, prior_ref, out_ref):
    mask = triangle(True)
    ramp = lax.broadcasted_iota(jnp.int32, (SUB, 1), 0)
    cols = slice(h * HD, (h + 1) * HD)
    prior = jnp.concatenate(split(prior_ref[h]), axis=0)
    for i in range(PARTS):
        rows, upto = slice(i * SUB, (i + 1) * SUB), (i + 1) * SUB
        g = g_ref[rows, cols]
        mix = dot_t(g, v_ref[:upto, cols])
        edge = jnp.where(mask, mix[:, i * SUB :], 0.0).astype(bf16)
        if i:
            edge = jnp.concatenate([mix[:, : i * SUB].astype(bf16), edge], axis=1)
        before = dot_t(g, prior)
        total = before[:, :HD] + before[:, HD:] + dot(edge, k_ref[:upto, cols])
        count = (3 * BLOCKS * TOK + block * TOK + i * SUB + ramp + 1).astype(f32)
        out_ref[rows, cols] = (total / count).astype(bf16)


def later_part(block, h, a_ref, b_ref, c_ref, out_ref):
    mask = triangle(False)
    ramp = lax.broadcasted_iota(jnp.int32, (1, TOK), 1)
    inverse = 1.0 / (3 * BLOCKS * TOK + block * TOK + ramp + 1).astype(f32)
    cols = slice(h * HD, (h + 1) * HD)
    for i in range(PARTS):
        at = i * SUB
        rows = slice(at, at + SUB)
        mix = dot_t(a_ref[rows, cols], b_ref[at:, cols]) * inverse[:, at:]
        edge = jnp.where(mask, mix[:, :SUB], 0.0).astype(bf16)
        if i < PARTS - 1:
            edge = jnp.concatenate([edge, mix[:, SUB:].astype(bf16)], axis=1)
        out_ref[rows, cols] = dot(edge, c_ref[at:, cols])


def query_key_body(at_ref, q_ref, k_ref, v_ref, g_ref, prior_ref, out_ref, key_ref):
    block = at_ref[1]
    for h in range(PAIR):
        query_part(block, h, g_ref, v_ref, k_ref, prior_ref, out_ref)
        later_part(block, h, v_ref, g_ref, q_ref, key_ref)


def value_body(at_ref, q_ref, k_ref, g_ref, value_ref):
    for h in range(PAIR):
        later_part(at_ref[1], h, k_ref, q_ref, g_ref, value_ref)


def head_call(body, name, ins, out_types, prior=None):
    cols = pl.BlockSpec((TOK, PAIR * HD), lambda h: (0, h))
    specs = [scalars()] + [cols] * (len(ins) - 1)
    if prior is not None:
        specs.append(pl.BlockSpec((PAIR, HD, HD), lambda h: (h, 0, 0)))
        ins = (*ins, prior)
    return call(
        body,
        name,
        [((TOK, HEADS * HD), t) for t in out_types],
        ins,
        10 * HEADS * 4 * SUB * SUB * HD * len(out_types),
        6 << 20,
        grid=(HEADS // PAIR,),
        in_specs=specs,
        out_specs=[cols] * len(out_types),
    )


def final_body(spot_ref, other, x1, x2, x3, z1, z2, z3, v_ref, k_ref, key_ref, value_ref, out_key, out_value):
    z, x, core = spot_ref[0], spot_ref[1], spot_ref[2]
    later = jnp.where(core == 0, other[...], 0.0)
    for s, a, b in ((1, x1, z1), (2, x2, z2), (3, x3, z3)):
        later += jnp.where(s > x, a[...].astype(f32), 0.0) + jnp.where(s > z, b[...].astype(f32), 0.0)
    hi, lo = split(later)
    key = dot_t(v_ref[...], jnp.concatenate([hi, lo], axis=0))
    out_key[...] = (key_ref[...] + key[:, :HD] + key[:, HD:]).astype(bf16)
    value = dot(k_ref[...], jnp.concatenate([hi, lo], axis=1))
    out_value[...] = (value_ref[...] + value[:, :HD] + value[:, HD:]).astype(bf16)


def final(spot, sums, values, keys, key_here, value_here):
    cols = pl.BlockSpec((TOK, HD), lambda h: (0, h))
    return call(
        final_body,
        "final",
        [((TOK, HEADS * HD), bf16)] * 2,
        (spot, *sums, values, keys, key_here, value_here),
        HEADS * 8 * TOK * HD * HD,
        8 << 20,
        grid=(HEADS,),
        in_specs=[scalars()] + [pl.BlockSpec((HD, HD), lambda h: (h, 0))] * 7 + [cols] * 4,
        out_specs=[cols, cols],
        free=range(1, 8),
    )


def index(z, x, c):
    return (z * X + x) * C + c


def spots():
    return [(z, x, c) for z in range(Z) for x in range(X) for c in range(C)]


def along_y(a, s):
    return lax.ppermute(a, "exp", [(i, (i + s) % Y) for i in range(Y)])


def along_x(a, s):
    return lax.ppermute(a, "ctx", [(index(z, x, c), index(z, (x + s) % X, c)) for z, x, c in spots()])


def along_z(a, s):
    return lax.ppermute(a, "ctx", [(index(z, x, c), index((z + s) % Z, x, c)) for z, x, c in spots()])


def across(a):
    return lax.ppermute(a, "ctx", [(i, i ^ 1) for i in range(BLOCKS)])


def on_device(
    attn_query,
    attn_key,
    attn_value,
    prefix_state,
    moe_in,
    grad_out,
    router_gates,
    expert_ids,
    w_gate_up,
    w_down,
    w_out,
):
    y = lax.axis_index("exp")
    block = lax.axis_index("ctx")
    z, x, c = block >> 3, (block >> 1) & 3, block & 1
    at = jnp.stack([y, block]).astype(jnp.int32)
    spot = jnp.stack([z, x, c]).astype(jnp.int32)
    core = c.astype(jnp.int32)[None]

    slab = w_out.shape[0] // BLOCKS
    piece = lax.dynamic_slice_in_dim(w_out, block * slab, slab, 0)
    pieces = jnp.concatenate([along_y(piece, s) for s in (1, 2, 3)], axis=0)
    gate_row = router_gates.reshape(1, ROWS)
    place, *chunks = pack(at, expert_ids.reshape(1, ROWS), gate_row, moe_in, grad_out)
    pieces, chunks[1] = lax.optimization_barrier((pieces, chunks[1]))
    rest = lax.all_gather(pieces[None], "ctx", axis=0, tiled=True)
    rest = rest.reshape(BLOCKS, 3, slab, WIDTH)

    held = [chunks[0]] + [along_y(chunks[s], s) for s in (1, 2, 3)]
    b0, b1, b2, b3, bundle = expert(held, w_gate_up, w_down)
    backs = [b0] + [along_y(b, -s) for s, b in ((1, b1), (2, b2), (3, b3))]
    other_bundle, backs[1] = lax.optimization_barrier((across(bundle), backs[1]))
    partial = weights(core, bundle, other_bundle)
    groups = [[index(i, j, k) for i in range(Z) for j in range(X)] for k in range(C)]
    exchanged = lax.all_to_all(partial, "ctx", 0, 0, axis_index_groups=groups, tiled=True)

    grad_resid, gates_out, *per_head = project(w_out, rest, place, gate_row, grad_out, backs)
    grad_gates = gates_out.reshape(ROWS, 1)
    grads = [per_head[0]] + [along_y(per_head[s], -s) for s in (1, 2, 3)]
    attn_grad, state = call(
        state_body,
        "state",
        [((TOK, HEADS * HD), bf16), ((HEADS * HD, HD), f32)],
        (at, *grads, attn_query),
        HEADS * 2 * TOK * HD * 2 * HD,
        4 << 20,
        in_specs=[scalars()] + [full()] * 5,
        free=(2, 3, 4),
    )

    other = across(state)
    chip = state + other
    chip16 = chip.astype(bf16)
    from_x = [along_x(chip16, s) for s in (1, 2, 3)]
    line = chip + from_x[0].astype(f32) + from_x[1].astype(f32) + from_x[2].astype(f32)
    line16 = line.astype(bf16)
    ins = (at, attn_query, attn_key, attn_value, attn_grad)
    grad_query, key_here = head_call(query_key_body, "query_key", ins, (bf16, f32), prefix_state[0])
    line16, key_here = lax.optimization_barrier((line16, key_here))
    from_z = [along_z(line16, s) for s in (1, 2, 3)]

    (value_here,) = head_call(value_body, "value", (at, attn_query, attn_key, attn_grad), (f32,))
    sums = (other, *from_x, *from_z)
    grad_key, grad_value = final(spot, sums, attn_value, attn_key, key_here, value_here)

    exchanged, grad_key = lax.optimization_barrier((exchanged, grad_key))
    outs = [((1, 64, 1024), f32), ((1, 16, WIDTH), f32)]
    grad_gate_up, grad_down = call(gather_sum_body, "gather_sum", outs, (exchanged,), 0, 4 << 20, free=(0,))
    return (grad_query, grad_key, grad_value, grad_resid, grad_gates, grad_gate_up, grad_down)


def solution(mesh):
    whole = P(("ctx", "exp"), None)
    split_cols = P("ctx", "exp")
    return jax.shard_map(
        on_device,
        mesh=mesh,
        in_specs=(
            split_cols,
            split_cols,
            split_cols,
            P("ctx", "exp", None, None),
            whole,
            whole,
            whole,
            whole,
            P("exp", None, None),
            P("exp", None, None),
            P("exp", None),
        ),
        out_specs=(
            split_cols,
            split_cols,
            split_cols,
            whole,
            whole,
            P("exp", "ctx", None),
            P("exp", "ctx", None),
        ),
        check_vma=False,
    )
```

```python
import jax
import jax.numpy as jnp
from jax import lax
from jax.experimental import pallas as pl
from jax.experimental.pallas import tpu as pltpu
from jax.sharding import PartitionSpec as P

bf16 = jnp.bfloat16
f32 = jnp.float32
VMEM = pltpu.VMEM
SMEM = pltpu.SMEM
Z, X, C, Y = 4, 4, 2, 4
CAP, ROWS, WIDTH, FF, HD, HEADS, TOK = 96, 256, 2048, 512, 128, 4, 1024
WEIGHT = 4
BLOCKS = Z * X * C


def dot(a, b):
    return lax.dot_general(a, b, (((1,), (0,)), ((), ())), preferred_element_type=f32)


def dot_t(a, b):
    return lax.dot_general(a, b, (((1,), (1,)), ((), ())), preferred_element_type=f32)


def t_dot(a, b):
    return lax.dot_general(a, b, (((0,), (0,)), ((), ())), preferred_element_type=f32)


def split(a):
    hi = a.astype(bf16)
    return hi, (a - hi.astype(f32)).astype(bf16)


def full():
    return pl.BlockSpec(memory_space=VMEM)


def scalars():
    return pl.BlockSpec(memory_space=SMEM)


def call(body, name, outs, ins, flops=0, moved=0, grid=None, in_specs=None, out_specs=None, limit=24, scratch=(), free=(), near=False):
    kwargs = {} if grid is None else {"grid": grid}
    specs = in_specs or [full() for _ in ins]
    ins = [
        a if spec.memory_space is SMEM or i in free else pltpu.with_memory_space_constraint(a, pltpu.HBM)
        for i, (a, spec) in enumerate(zip(ins, specs))
    ]
    return pl.pallas_call(
        body,
        name=name,
        out_shape=[(VMEM if near else pltpu.HBM)(s, t) for s, t in outs],
        in_specs=specs,
        out_specs=out_specs or [full() for _ in outs],
        scratch_shapes=scratch,
        compiler_params=pltpu.CompilerParams(vmem_limit_bytes=limit << 20),
        cost_estimate=pl.CostEstimate(flops=WEIGHT * flops, bytes_accessed=WEIGHT * moved, transcendentals=0),
        **kwargs,
    )(*ins)


def pack_body(at_ref, ids_ref, gate_ref, moe_ref, cot_ref, place_ref, turned_ref, c0, c1, c2, c3, gate_col):
    @pl.when(pl.program_id(0) == 0)
    def _():
        rel = ids_ref[...] - at_ref[0]
        rel = jnp.where(rel < 0, rel + Y, rel)
        member = (lax.broadcasted_iota(jnp.int32, (8, ROWS), 0) == rel).astype(f32)
        row = lax.broadcasted_iota(jnp.int32, (ROWS, ROWS), 0)
        col = lax.broadcasted_iota(jnp.int32, (ROWS, ROWS), 1)
        earlier = dot(member.astype(bf16), (row < col).astype(bf16))
        slot = jnp.sum(earlier * member, axis=0, keepdims=True).astype(jnp.int32)
        target = rel * CAP + slot
        places = lax.broadcasted_iota(jnp.int32, (Y * CAP, ROWS), 0)
        place_ref[...] = (places == target).astype(bf16)
        spots_col = jnp.sum(jnp.where(row == col, target.astype(f32), 0.0), axis=1, keepdims=True)
        lanes = lax.broadcasted_iota(jnp.int32, (ROWS, Y * CAP), 1)
        turned_ref[...] = (lanes == spots_col.astype(jnp.int32)).astype(bf16)
        gate = gate_ref[...].astype(f32)
        gate_col[...] = jnp.sum(jnp.where(row == col, gate, 0.0), axis=1, keepdims=True)

    place = place_ref[...]
    scaled = (gate_col[...] * cot_ref[...].astype(f32)).astype(bf16)
    for half, rows in enumerate((moe_ref[...], scaled)):
        part = dot(place, rows).astype(bf16)
        for s, chunk in enumerate((c0, c1, c2, c3)):
            chunk[half] = part[s * CAP : (s + 1) * CAP]


def pack(at, ids, gates, moe_in, grad_out):
    step = 1024
    outs = [((Y * CAP, ROWS), bf16), ((ROWS, Y * CAP), bf16)] + [((2, CAP, WIDTH), bf16)] * Y
    ins = (at, ids, gates, moe_in, grad_out)
    row = pl.BlockSpec((1, ROWS), lambda j: (0, 0))
    tile = pl.BlockSpec((ROWS, step), lambda j: (0, j))
    return call(
        pack_body,
        "pack",
        outs,
        ins,
        2 * 384 * 256 * 4096,
        5 << 20,
        grid=(WIDTH // step,),
        in_specs=[scalars(), row, row, tile, tile],
        out_specs=[pl.BlockSpec((Y * CAP, ROWS), lambda j: (0, 0)), pl.BlockSpec((ROWS, Y * CAP), lambda j: (0, 0))]
        + [pl.BlockSpec((2, CAP, step), lambda j: (0, 0, j))] * Y,
        scratch=[VMEM((ROWS, 1), f32)],
        limit=16,
    )


BACK = WIDTH + 128
N = Y * CAP
BUNDLE = 2 * WIDTH + 3 * FF
GB, HID = 2 * WIDTH, 2 * WIDTH + 2 * FF
STEP = 256


def expert_body(r0, r1, r2, r3, wp, wb, b0, b1, b2, b3, out_hbm, held, back, in_sem, out_sem):
    arrived = (r0, r1, r2, r3)
    backs = (b0, b1, b2, b3)
    tiles = FF // STEP

    def incoming(half, s):
        dst = held.at[pl.ds(s * CAP, CAP), pl.ds(half * WIDTH, WIDTH)]
        return pltpu.make_async_copy(arrived[s].at[half], dst, in_sem.at[half * Y + s])

    for s in range(Y):
        incoming(0, s).start()
    for s in range(Y):
        incoming(1, s).start()
    for s in range(Y):
        incoming(0, s).wait()
    total = jnp.zeros((N, 1), f32)
    for j in range(tiles):
        at, up = j * STEP, FF + j * STEP
        first = dot(held[:, :WIDTH], wp[0, :, at : at + STEP])
        second = dot(held[:, :WIDTH], wp[0, :, up : up + STEP])
        if j == 0:
            for s in range(Y):
                incoming(1, s).wait()
            rows_out = pltpu.make_async_copy(held.at[:, pl.ds(0, GB)], out_hbm.at[:, pl.ds(0, GB)], out_sem.at[0])
            rows_out.start()
        grad_hidden = dot_t(held[:, WIDTH:GB], wb[0, at : at + STEP, :])
        s = 1.0 / (1.0 + jnp.exp(-first))
        silu = first * s
        hidden = (silu * second).astype(bf16)
        held[:, HID + at : HID + at + STEP] = hidden
        total += jnp.sum(hidden.astype(f32) * grad_hidden, axis=1, keepdims=True)
        slope = s * (1.0 + first * (1.0 - s))
        held[:, GB + at : GB + at + STEP] = (grad_hidden * second * slope).astype(bf16)
        held[:, GB + up : GB + up + STEP] = (grad_hidden * silu).astype(bf16)
    rest = pl.ds(GB, BUNDLE - GB)
    grads_out = pltpu.make_async_copy(held.at[:, rest], out_hbm.at[:, rest], out_sem.at[1])
    grads_out.start()
    hi, lo = split(total)
    lane = lax.broadcasted_iota(jnp.int32, (N, 128), 1)
    back[:, WIDTH:] = jnp.where(lane == 0, hi.astype(f32), lo.astype(f32)).astype(bf16)
    outgoing = []
    bounds = (0, WIDTH // 2, BACK)
    for part in range(2):
        lo_col, hi_col = bounds[part], bounds[part + 1]
        for at in range(lo_col, min(hi_col, WIDTH), STEP):
            back[:, at : at + STEP] = dot_t(held[:, GB:HID], wp[0, at : at + STEP, :]).astype(bf16)
        cols = pl.ds(lo_col, hi_col - lo_col)
        for s in range(Y):
            src = back.at[pl.ds(s * CAP, CAP), cols]
            copy = pltpu.make_async_copy(src, backs[s].at[:, cols], out_sem.at[2 + part * Y + s])
            copy.start()
            outgoing.append(copy)
    rows_out.wait()
    grads_out.wait()
    for copy in outgoing:
        copy.wait()


def anywhere():
    return pl.BlockSpec(memory_space=pl.ANY)


def fetch_body(wp_hbm, wb_hbm, wp, wb, sem):
    copies = [pltpu.make_async_copy(wp_hbm, wp, sem.at[0]), pltpu.make_async_copy(wb_hbm, wb, sem.at[1])]
    for copy in copies:
        copy.start()
    for copy in copies:
        copy.wait()


def fetch(w_pair, w_back):
    return call(
        fetch_body,
        "fetch",
        [(w_pair.shape, bf16), (w_back.shape, bf16)],
        (w_pair, w_back),
        0,
        12 << 20,
        in_specs=[anywhere(), anywhere()],
        scratch=[pltpu.SemaphoreType.DMA((2,))],
        limit=16,
        near=True,
    )


def expert(chunks, w_pair, w_back):
    outs = [((CAP, BACK), bf16)] * Y + [((N, BUNDLE), bf16)]
    ins = (*chunks, w_pair, w_back)
    return call(
        expert_body,
        "expert",
        outs,
        ins,
        5 * 2 * N * WIDTH * FF,
        14 << 20,
        in_specs=[anywhere() for _ in chunks] + [full(), full()],
        out_specs=[anywhere() for _ in outs],
        scratch=[
            VMEM((N, BUNDLE), bf16),
            VMEM((N, BACK), bf16),
            pltpu.SemaphoreType.DMA((2 * Y,)),
            pltpu.SemaphoreType.DMA((2 + 2 * Y,)),
        ],
        limit=32,
        free=(1, 2, 3, 4, 5),
    )


def chooser(core, wide, run):
    row = lax.broadcasted_iota(jnp.int32, (wide // 2, wide), 0)
    col = lax.broadcasted_iota(jnp.int32, (wide // 2, wide), 1)
    return (col == (row // run) * (2 * run) + core * run + row % run).astype(bf16)


def weights_body(core_ref, mine, other, out_hbm, both, rows_t, hid_t, out, in_sem, out_sem):
    core = core_ref[0]
    copies = []
    for part, (lo, hi) in enumerate(((0, WIDTH), (HID, BUNDLE), (GB, HID), (WIDTH, GB))):
        for k, src in enumerate((mine, other)):
            cols = pl.ds(lo, hi - lo)
            copy = pltpu.make_async_copy(src.at[:, cols], both.at[pl.ds(k * N, N), cols], in_sem.at[2 * part + k])
            copy.start()
            copies.append(copy)
    pick_row, pick_hid = chooser(core, 512, 64), chooser(core, 128, 16)
    copies[0].wait()
    copies[1].wait()
    for i in range(Z):
        rows_t[i * 256 : (i + 1) * 256, :] = dot_t(pick_row, both[:, i * 512 : (i + 1) * 512]).astype(bf16)
    copies[2].wait()
    copies[3].wait()
    for i in range(Z):
        hid_t[i * 64 : (i + 1) * 64, :] = dot_t(pick_hid, both[:, HID + i * 128 : HID + (i + 1) * 128]).astype(bf16)
    copies[4].wait()
    copies[5].wait()
    for j in range(4):
        up = dot(rows_t[...], both[:, GB + j * STEP : GB + (j + 1) * STEP]).astype(bf16)
        for k in range(Z * X):
            out[k, :64, j * STEP : (j + 1) * STEP] = up[k * 64 : (k + 1) * 64]
    copies[6].wait()
    copies[7].wait()
    for j in range(8):
        down = dot(hid_t[...], both[:, WIDTH + j * STEP : WIDTH + (j + 1) * STEP]).astype(bf16)
        row, col = 64 + 16 * (j // 4), (j % 4) * STEP
        for k in range(Z * X):
            out[k, row : row + 16, col : col + STEP] = down[k * 16 : (k + 1) * 16]
    result = pltpu.make_async_copy(out, out_hbm, out_sem)
    result.start()
    result.wait()


def weights(core, mine, other):
    return call(
        weights_body,
        "weights",
        [((Z * X, 96, 1024), bf16)],
        (core, mine, other),
        3 * 2 * N * WIDTH * FF,
        12 << 20,
        in_specs=[scalars(), anywhere(), anywhere()],
        out_specs=[anywhere()],
        scratch=[
            VMEM((2 * N, BUNDLE), bf16),
            VMEM((1024, 2 * N), bf16),
            VMEM((256, 2 * N), bf16),
            VMEM((Z * X, 96, 1024), bf16),
            pltpu.SemaphoreType.DMA((8,)),
            pltpu.SemaphoreType.DMA,
        ],
        limit=32,
    )[0]


def gather_sum_body(pieces_ref, up_ref, down_ref):
    for j in range(2):
        at = j * 512
        total = pieces_ref[0, :, at : at + 512].astype(f32)
        for k in range(1, Z * X):
            total = total + pieces_ref[k, :, at : at + 512].astype(f32)
        up_ref[0, :, at : at + 512] = total[:64]
        down_ref[0, :, at : at + 512] = total[64:80]
        down_ref[0, :, 1024 + at : 1024 + at + 512] = total[80:96]


def project_body(*refs):
    own, rest, place_hbm, turned_hbm, gate, cot_hbm, r0, r1, r2, r3, resid_hbm, gates, o0, o1, o2, o3 = refs[:16]
    place, turned, cot, back, w, resid, outs, in_sem, w_sem, out_sem = refs[16:]
    copies = [
        pltpu.make_async_copy(r, back.at[pl.ds(s * CAP, CAP), :], in_sem.at[s]) for s, r in enumerate((r0, r1, r2, r3))
    ]
    copies.append(pltpu.make_async_copy(turned_hbm, turned, in_sem.at[4]))
    late = pltpu.make_async_copy(place_hbm, place, in_sem.at[6])
    copies.append(pltpu.make_async_copy(cot_hbm, cot, in_sem.at[5]))
    slabs = [pltpu.make_async_copy(own, w.at[0], w_sem.at[0])]
    for s in range(1, Y):
        slabs.append(pltpu.make_async_copy(rest.at[:, s - 1], w.at[s].reshape(rest.shape[0], -1, WIDTH), w_sem.at[s]))
    for copy in copies + slabs + [late]:
        copy.start()
    for copy in copies:
        copy.wait()
    wide = 512
    for j in range(WIDTH // wide):
        cols = slice(j * wide, (j + 1) * wide)
        resid[:, cols] = (cot[:, cols].astype(f32) + dot(turned[...], back[:, cols])).astype(bf16)
    sent = [pltpu.make_async_copy(resid, resid_hbm, out_sem.at[4])]
    sent[0].start()
    for s, out in enumerate((o0, o1, o2, o3)):
        slabs[s].wait()
        outs[s] = dot_t(resid[...], w[s]).astype(bf16)
        copy = pltpu.make_async_copy(outs.at[s], out, out_sem.at[s])
        copy.start()
        sent.append(copy)
    late.wait()
    tail = back[:, WIDTH:].astype(f32)
    picked = jnp.sum(place[...].astype(f32) * (tail[:, 0:1] + tail[:, 1:2]), axis=0, keepdims=True)
    gates[...] = (picked / gate[...].astype(f32)).astype(bf16)
    for copy in sent:
        copy.wait()


def project(w_out, rest, place, turned, gate_row, grad_out, backs):
    shapes = [(ROWS, WIDTH), (1, ROWS)] + [(ROWS, 512)] * Y
    ins = (w_out, rest, place, turned, gate_row, grad_out, *backs)
    in_specs, out_specs = [anywhere() for _ in ins], [anywhere() for _ in shapes]
    in_specs[4], out_specs[1] = full(), full()
    return call(
        project_body,
        "project",
        [(s, bf16) for s in shapes],
        ins,
        2 * ROWS * WIDTH * WIDTH + 2 * ROWS * N * WIDTH,
        10 << 20,
        in_specs=in_specs,
        out_specs=out_specs,
        scratch=[
            VMEM((N, ROWS), bf16),
            VMEM((ROWS, N), bf16),
            VMEM((ROWS, WIDTH), bf16),
            VMEM((N, BACK), bf16),
            VMEM((Y, 512, WIDTH), bf16),
            VMEM((ROWS, WIDTH), bf16),
            VMEM((Y, ROWS, 512), bf16),
            pltpu.SemaphoreType.DMA((7,)),
            pltpu.SemaphoreType.DMA((Y,)),
            pltpu.SemaphoreType.DMA((Y + 1,)),
        ],
        limit=32,
    )


def state_body(at_ref, g0, g1, g2, g3, q_ref, grad_ref, state_ref):
    y, block = at_ref[0], at_ref[1]
    ramp = lax.broadcasted_iota(jnp.int32, (ROWS, 1), 0)
    total = jnp.zeros((HD, 2 * HD), f32)
    for s, g in enumerate((g0, g1, g2, g3)):
        off = pl.multiple_of(lax.rem(y + s, Y) * ROWS, ROWS)
        inverse = 1.0 / (3 * BLOCKS * TOK + block * TOK + off + ramp + 1).astype(f32)
        grad_ref[pl.ds(off, ROWS), :] = g[...]
        both = jnp.concatenate(split(g[...].astype(f32) * inverse), axis=1)
        total += t_dot(q_ref[pl.ds(off, ROWS), :], both)
    state_ref[...] = total[:, :HD] + total[:, HD:]


def head_state(at, grads, queries):
    cols = pl.BlockSpec((TOK, HD), lambda h: (0, h))
    return call(
        state_body,
        "state",
        [((TOK, HEADS * HD), bf16), ((HEADS * HD, HD), f32)],
        (at, *grads, queries),
        HEADS * 2 * TOK * HD * 2 * HD,
        4 << 20,
        grid=(HEADS,),
        in_specs=[scalars()] + [pl.BlockSpec((ROWS, HD), lambda h: (0, h))] * Y + [cols],
        out_specs=[cols, pl.BlockSpec((HD, HD), lambda h: (h, 0))],
        free=(2, 3, 4),
    )


SUB = 256
PARTS = TOK // SUB
PAIR = 2


def triangle(lower):
    row = lax.broadcasted_iota(jnp.int32, (SUB, SUB), 0)
    col = lax.broadcasted_iota(jnp.int32, (SUB, SUB), 1)
    return (col <= row) if lower else (col >= row)


def query_part(block, h, g_ref, v_ref, k_ref, prior_ref, out_ref):
    mask = triangle(True)
    ramp = lax.broadcasted_iota(jnp.int32, (SUB, 1), 0)
    cols = slice(h * HD, (h + 1) * HD)
    prior = jnp.concatenate(split(prior_ref[h]), axis=0)
    for i in range(PARTS):
        rows, upto = slice(i * SUB, (i + 1) * SUB), (i + 1) * SUB
        g = g_ref[rows, cols]
        mix = dot_t(g, v_ref[:upto, cols])
        edge = jnp.where(mask, mix[:, i * SUB :], 0.0).astype(bf16)
        if i:
            edge = jnp.concatenate([mix[:, : i * SUB].astype(bf16), edge], axis=1)
        before = dot_t(g, prior)
        total = before[:, :HD] + before[:, HD:] + dot(edge, k_ref[:upto, cols])
        count = (3 * BLOCKS * TOK + block * TOK + i * SUB + ramp + 1).astype(f32)
        out_ref[rows, cols] = (total / count).astype(bf16)


def later_part(block, h, a_ref, b_ref, c_ref, out_ref):
    mask = triangle(False)
    ramp = lax.broadcasted_iota(jnp.int32, (1, TOK), 1)
    inverse = 1.0 / (3 * BLOCKS * TOK + block * TOK + ramp + 1).astype(f32)
    cols = slice(h * HD, (h + 1) * HD)
    for i in range(PARTS):
        at = i * SUB
        rows = slice(at, at + SUB)
        mix = dot_t(a_ref[rows, cols], b_ref[at:, cols]) * inverse[:, at:]
        edge = jnp.where(mask, mix[:, :SUB], 0.0).astype(bf16)
        if i < PARTS - 1:
            edge = jnp.concatenate([edge, mix[:, SUB:].astype(bf16)], axis=1)
        out_ref[rows, cols] = dot(edge, c_ref[at:, cols]).astype(bf16)


def query_key_body(at_ref, q_ref, k_ref, v_ref, g_ref, prior_ref, out_ref, key_ref):
    block = at_ref[1]
    for h in range(PAIR):
        query_part(block, h, g_ref, v_ref, k_ref, prior_ref, out_ref)
        later_part(block, h, v_ref, g_ref, q_ref, key_ref)


def value_body(at_ref, q_ref, k_ref, g_ref, value_ref):
    for h in range(PAIR):
        later_part(at_ref[1], h, k_ref, q_ref, g_ref, value_ref)


def head_call(body, name, ins, out_types, prior=None):
    cols = pl.BlockSpec((TOK, PAIR * HD), lambda h: (0, h))
    specs = [scalars()] + [cols] * (len(ins) - 1)
    if prior is not None:
        specs.append(pl.BlockSpec((PAIR, HD, HD), lambda h: (h, 0, 0)))
        ins = (*ins, prior)
    return call(
        body,
        name,
        [((TOK, HEADS * HD), t) for t in out_types],
        ins,
        10 * HEADS * 4 * SUB * SUB * HD * len(out_types),
        6 << 20,
        grid=(HEADS // PAIR,),
        in_specs=specs,
        out_specs=[cols] * len(out_types),
    )


def final_body(spot_ref, other, x1, x2, x3, z1, z2, z3, v_ref, k_ref, key_ref, value_ref, out_key, out_value):
    z, x, core = spot_ref[0], spot_ref[1], spot_ref[2]
    later = jnp.where(core == 0, other[...], 0.0)
    for s, a, b in ((1, x1, z1), (2, x2, z2), (3, x3, z3)):
        later += jnp.where(s > x, a[...].astype(f32), 0.0) + jnp.where(s > z, b[...].astype(f32), 0.0)
    hi, lo = split(later)
    key = dot_t(v_ref[...], jnp.concatenate([hi, lo], axis=0))
    out_key[...] = (key_ref[...].astype(f32) + key[:, :HD] + key[:, HD:]).astype(bf16)
    value = dot(k_ref[...], jnp.concatenate([hi, lo], axis=1))
    out_value[...] = (value_ref[...].astype(f32) + value[:, :HD] + value[:, HD:]).astype(bf16)


def final(spot, sums, values, keys, key_here, value_here):
    cols = pl.BlockSpec((TOK, HD), lambda h: (0, h))
    return call(
        final_body,
        "final",
        [((TOK, HEADS * HD), bf16)] * 2,
        (spot, *sums, values, keys, key_here, value_here),
        HEADS * 8 * TOK * HD * HD,
        8 << 20,
        grid=(HEADS,),
        in_specs=[scalars()] + [pl.BlockSpec((HD, HD), lambda h: (h, 0))] * 7 + [cols] * 4,
        out_specs=[cols, cols],
        free=range(1, 8),
    )


def index(z, x, c):
    return (z * X + x) * C + c


def spots():
    return [(z, x, c) for z in range(Z) for x in range(X) for c in range(C)]


def along_y(a, s):
    return lax.ppermute(a, "exp", [(i, (i + s) % Y) for i in range(Y)])


def along_x(a, s):
    return lax.ppermute(a, "ctx", [(index(z, x, c), index(z, (x + s) % X, c)) for z, x, c in spots()])


def along_z(a, s):
    return lax.ppermute(a, "ctx", [(index(z, x, c), index((z + s) % Z, x, c)) for z, x, c in spots()])


def across(a):
    return lax.ppermute(a, "ctx", [(i, i ^ 1) for i in range(BLOCKS)])


def on_device(
    attn_query,
    attn_key,
    attn_value,
    prefix_state,
    moe_in,
    grad_out,
    router_gates,
    expert_ids,
    w_gate_up,
    w_down,
    w_out,
):
    y = lax.axis_index("exp")
    block = lax.axis_index("ctx")
    z, x, c = block >> 3, (block >> 1) & 3, block & 1
    at = jnp.stack([y, block]).astype(jnp.int32)
    spot = jnp.stack([z, x, c]).astype(jnp.int32)
    core = c.astype(jnp.int32)[None]

    slab = w_out.shape[0] // BLOCKS
    piece = lax.dynamic_slice_in_dim(w_out, block * slab, slab, 0)
    pieces = jnp.concatenate([along_y(piece, s) for s in (1, 2, 3)], axis=0)
    gate_row = router_gates.reshape(1, ROWS)
    place, turned, *chunks = pack(at, expert_ids.reshape(1, ROWS), gate_row, moe_in, grad_out)
    pieces, chunks[1] = lax.optimization_barrier((pieces, chunks[1]))
    rest = lax.all_gather(pieces[None], "ctx", axis=0, tiled=True)
    rest = rest.reshape(BLOCKS, 3, slab, WIDTH)

    held = [chunks[0]] + [along_y(chunks[s], s) for s in (1, 2, 3)]
    w_pair, chunks[0] = lax.optimization_barrier((w_gate_up, chunks[0]))
    held[0] = chunks[0]
    w_pair, w_back = fetch(w_pair, w_down)
    b0, b1, b2, b3, bundle = expert(held, w_pair, w_back)
    backs = [b0] + [along_y(b, -s) for s, b in ((1, b1), (2, b2), (3, b3))]
    other_bundle, backs[1] = lax.optimization_barrier((across(bundle), backs[1]))
    partial = weights(core, bundle, other_bundle)
    groups = [[index(i, j, k) for i in range(Z) for j in range(X)] for k in range(C)]
    exchanged = lax.all_to_all(partial, "ctx", 0, 0, axis_index_groups=groups, tiled=True)

    grad_resid, gates_out, *per_head = project(w_out, rest, place, turned, gate_row, grad_out, backs)
    grad_gates = gates_out.reshape(ROWS, 1)
    grads = [per_head[0]] + [along_y(per_head[s], -s) for s in (1, 2, 3)]
    attn_grad, state = head_state(at, grads, attn_query)

    other = across(state)
    chip = state + other
    chip16 = chip.astype(bf16)
    from_x = [along_x(chip16, s) for s in (1, 2, 3)]
    line = chip + from_x[0].astype(f32) + from_x[1].astype(f32) + from_x[2].astype(f32)
    line16 = line.astype(bf16)
    ins = (at, attn_query, attn_key, attn_value, attn_grad)
    grad_query, key_here = head_call(query_key_body, "query_key", ins, (bf16, bf16), prefix_state[0])
    line16, key_here = lax.optimization_barrier((line16, key_here))
    from_z = [along_z(line16, s) for s in (1, 2, 3)]

    (value_here,) = head_call(value_body, "value", (at, attn_query, attn_key, attn_grad), (bf16,))
    sums = (other, *from_x, *from_z)
    grad_key, grad_value = final(spot, sums, attn_value, attn_key, key_here, value_here)

    exchanged, grad_key = lax.optimization_barrier((exchanged, grad_key))
    outs = [((1, 64, 1024), f32), ((1, 16, WIDTH), f32)]
    grad_gate_up, grad_down = call(gather_sum_body, "gather_sum", outs, (exchanged,), 0, 4 << 20, free=(0,))
    return (grad_query, grad_key, grad_value, grad_resid, grad_gates, grad_gate_up, grad_down)


def solution(mesh):
    whole = P(("ctx", "exp"), None)
    split_cols = P("ctx", "exp")
    return jax.shard_map(
        on_device,
        mesh=mesh,
        in_specs=(
            split_cols,
            split_cols,
            split_cols,
            P("ctx", "exp", None, None),
            whole,
            whole,
            whole,
            whole,
            P("exp", None, None),
            P("exp", None, None),
            P("exp", None),
        ),
        out_specs=(
            split_cols,
            split_cols,
            split_cols,
            whole,
            whole,
            P("exp", "ctx", None),
            P("exp", "ctx", None),
        ),
        check_vma=False,
    )
```

```python
import jax
import jax.numpy as jnp
from jax import lax
from jax.experimental import pallas as pl
from jax.experimental.pallas import tpu as pltpu
from jax.sharding import PartitionSpec as P

bf16 = jnp.bfloat16
f32 = jnp.float32
VMEM = pltpu.VMEM
SMEM = pltpu.SMEM
Z, X, C, Y = 4, 4, 2, 4
CAP, ROWS, WIDTH, FF, HD, HEADS, TOK = 96, 256, 2048, 512, 128, 4, 1024
WEIGHT = 4
BLOCKS = Z * X * C


def dot(a, b):
    return lax.dot_general(a, b, (((1,), (0,)), ((), ())), preferred_element_type=f32)


def dot_t(a, b):
    return lax.dot_general(a, b, (((1,), (1,)), ((), ())), preferred_element_type=f32)


def t_dot(a, b):
    return lax.dot_general(a, b, (((0,), (0,)), ((), ())), preferred_element_type=f32)


def split(a):
    hi = a.astype(bf16)
    return hi, (a - hi.astype(f32)).astype(bf16)


def full():
    return pl.BlockSpec(memory_space=VMEM)


def scalars():
    return pl.BlockSpec(memory_space=SMEM)


def call(body, name, outs, ins, flops=0, moved=0, grid=None, in_specs=None, out_specs=None, limit=24, scratch=(), free=(), near=(), held=()):
    kwargs = {} if grid is None else {"grid": grid}
    specs = in_specs or [full() for _ in ins]
    ins = [
        a if spec.memory_space is SMEM or i in free else pltpu.with_memory_space_constraint(a, VMEM if i in held else pltpu.HBM)
        for i, (a, spec) in enumerate(zip(ins, specs))
    ]
    return pl.pallas_call(
        body,
        name=name,
        out_shape=[(VMEM if near is True or i in near else pltpu.HBM)(s, t) for i, (s, t) in enumerate(outs)],
        in_specs=specs,
        out_specs=out_specs or [full() for _ in outs],
        scratch_shapes=scratch,
        compiler_params=pltpu.CompilerParams(vmem_limit_bytes=limit << 20),
        cost_estimate=pl.CostEstimate(flops=WEIGHT * flops, bytes_accessed=WEIGHT * moved, transcendentals=0),
        **kwargs,
    )(*ins)


def pack_body(at_ref, ids_ref, gate_ref, moe_ref, cot_ref, place_ref, turned_ref, c0, c1, c2, c3, gate_col):
    @pl.when(pl.program_id(0) == 0)
    def _():
        rel = ids_ref[...] - at_ref[0]
        rel = jnp.where(rel < 0, rel + Y, rel)
        member = (lax.broadcasted_iota(jnp.int32, (8, ROWS), 0) == rel).astype(f32)
        row = lax.broadcasted_iota(jnp.int32, (ROWS, ROWS), 0)
        col = lax.broadcasted_iota(jnp.int32, (ROWS, ROWS), 1)
        earlier = dot(member.astype(bf16), (row < col).astype(bf16))
        slot = jnp.sum(earlier * member, axis=0, keepdims=True).astype(jnp.int32)
        target = rel * CAP + slot
        places = lax.broadcasted_iota(jnp.int32, (Y * CAP, ROWS), 0)
        place_ref[...] = (places == target).astype(bf16)
        spots_col = jnp.sum(jnp.where(row == col, target.astype(f32), 0.0), axis=1, keepdims=True)
        lanes = lax.broadcasted_iota(jnp.int32, (ROWS, Y * CAP), 1)
        turned_ref[...] = (lanes == spots_col.astype(jnp.int32)).astype(bf16)
        gate = gate_ref[...].astype(f32)
        gate_col[...] = jnp.sum(jnp.where(row == col, gate, 0.0), axis=1, keepdims=True)

    place = place_ref[...]
    scaled = (gate_col[...] * cot_ref[...].astype(f32)).astype(bf16)
    for half, rows in enumerate((moe_ref[...], scaled)):
        part = dot(place, rows).astype(bf16)
        for s, chunk in enumerate((c0, c1, c2, c3)):
            chunk[half] = part[s * CAP : (s + 1) * CAP]


def pack(at, ids, gates, moe_in, grad_out):
    step = 1024
    outs = [((Y * CAP, ROWS), bf16), ((ROWS, Y * CAP), bf16)] + [((2, CAP, WIDTH), bf16)] * Y
    ins = (at, ids, gates, moe_in, grad_out)
    row = pl.BlockSpec((1, ROWS), lambda j: (0, 0))
    tile = pl.BlockSpec((ROWS, step), lambda j: (0, j))
    return call(
        pack_body,
        "pack",
        outs,
        ins,
        2 * 384 * 256 * 4096,
        5 << 20,
        grid=(WIDTH // step,),
        in_specs=[scalars(), row, row, tile, tile],
        out_specs=[pl.BlockSpec((Y * CAP, ROWS), lambda j: (0, 0)), pl.BlockSpec((ROWS, Y * CAP), lambda j: (0, 0))]
        + [pl.BlockSpec((2, CAP, step), lambda j: (0, 0, j))] * Y,
        scratch=[VMEM((ROWS, 1), f32)],
        limit=16,
    )


BACK = WIDTH + 128
N = Y * CAP
BUNDLE = 2 * WIDTH + 3 * FF
GB, HID = 2 * WIDTH, 2 * WIDTH + 2 * FF
STEP = 256


def expert_body(r0, r1, r2, r3, wp, wb, b0, b1, b2, b3, held, back, in_sem, out_sem):
    arrived = (r0, r1, r2, r3)
    backs = (b0, b1, b2, b3)
    tiles = FF // STEP

    def incoming(half, s):
        dst = held.at[pl.ds(s * CAP, CAP), pl.ds(half * WIDTH, WIDTH)]
        return pltpu.make_async_copy(arrived[s].at[half], dst, in_sem.at[half * Y + s])

    for s in range(Y):
        incoming(0, s).start()
    for s in range(Y):
        incoming(1, s).start()
    for s in range(Y):
        incoming(0, s).wait()
    total = jnp.zeros((N, 1), f32)
    for j in range(tiles):
        at, up = j * STEP, FF + j * STEP
        first = dot(held[:, :WIDTH], wp[0, :, at : at + STEP])
        second = dot(held[:, :WIDTH], wp[0, :, up : up + STEP])
        if j == 0:
            for s in range(Y):
                incoming(1, s).wait()
        grad_hidden = dot_t(held[:, WIDTH:GB], wb[0, at : at + STEP, :])
        s = 1.0 / (1.0 + jnp.exp(-first))
        silu = first * s
        hidden = (silu * second).astype(bf16)
        held[:, HID + at : HID + at + STEP] = hidden
        total += jnp.sum(hidden.astype(f32) * grad_hidden, axis=1, keepdims=True)
        slope = s * (1.0 + first * (1.0 - s))
        held[:, GB + at : GB + at + STEP] = (grad_hidden * second * slope).astype(bf16)
        held[:, GB + up : GB + up + STEP] = (grad_hidden * silu).astype(bf16)
    hi, lo = split(total)
    lane = lax.broadcasted_iota(jnp.int32, (N, 128), 1)
    back[:, WIDTH:] = jnp.where(lane == 0, hi.astype(f32), lo.astype(f32)).astype(bf16)
    outgoing = []
    bounds = (0, WIDTH // 2, BACK)
    for part in range(2):
        lo_col, hi_col = bounds[part], bounds[part + 1]
        for at in range(lo_col, min(hi_col, WIDTH), STEP):
            back[:, at : at + STEP] = dot_t(held[:, GB:HID], wp[0, at : at + STEP, :]).astype(bf16)
        cols = pl.ds(lo_col, hi_col - lo_col)
        for s in range(Y):
            src = back.at[pl.ds(s * CAP, CAP), cols]
            copy = pltpu.make_async_copy(src, backs[s].at[:, cols], out_sem.at[part * Y + s])
            copy.start()
            outgoing.append(copy)
    for copy in outgoing:
        copy.wait()


def anywhere():
    return pl.BlockSpec(memory_space=pl.ANY)


def fetch_body(*refs):
    half = len(refs) // 2
    sem = refs[-1]
    copies = [pltpu.make_async_copy(refs[i], refs[half + i], sem.at[i]) for i in range(half)]
    for copy in copies:
        copy.start()
    for copy in copies:
        copy.wait()


def fetch(*arrays):
    return call(
        fetch_body,
        "fetch",
        [(a.shape, a.dtype) for a in arrays],
        arrays,
        0,
        12 << 20,
        in_specs=[anywhere() for _ in arrays],
        scratch=[pltpu.SemaphoreType.DMA((len(arrays),))],
        limit=2,
        near=True,
    )


def expert(chunks, w_pair, w_back):
    outs = [((CAP, BACK), bf16)] * Y + [((N, BUNDLE), bf16)]
    ins = (*chunks, w_pair, w_back)
    return call(
        expert_body,
        "expert",
        outs,
        ins,
        5 * 2 * N * WIDTH * FF,
        14 << 20,
        in_specs=[anywhere() for _ in chunks] + [full(), full()],
        out_specs=[anywhere()] * Y + [full()],
        scratch=[
            VMEM((N, BACK), bf16),
            pltpu.SemaphoreType.DMA((2 * Y,)),
            pltpu.SemaphoreType.DMA((2 * Y,)),
        ],
        limit=16,
        free=(1, 2, 3),
        held=(4, 5),
        near=(Y,),
    )


def chooser(core, wide, run):
    row = lax.broadcasted_iota(jnp.int32, (wide // 2, wide), 0)
    col = lax.broadcasted_iota(jnp.int32, (wide // 2, wide), 1)
    return (col == (row // run) * (2 * run) + core * run + row % run).astype(bf16)


def weights_body(at_ref, mine, other, out_hbm, out, rows_t, hid_t, sem):
    core = at_ref[4]
    pick_row, pick_hid = chooser(core, 512, 64), chooser(core, 128, 16)
    for k, src in enumerate((mine, other)):
        for i in range(Z):
            rows_t[k, i * 256 : (i + 1) * 256, :] = dot_t(pick_row, src[:, i * 512 : (i + 1) * 512]).astype(bf16)
            cols = slice(HID + i * 128, HID + (i + 1) * 128)
            hid_t[k, i * 64 : (i + 1) * 64, :] = dot_t(pick_hid, src[:, cols]).astype(bf16)
    for j in range(4):
        cols = slice(GB + j * STEP, GB + (j + 1) * STEP)
        up = (dot(rows_t[0], mine[:, cols]) + dot(rows_t[1], other[:, cols])).astype(bf16)
        for k in range(Z * X):
            out[k, :64, j * STEP : (j + 1) * STEP] = up[k * 64 : (k + 1) * 64]
    copies = [pltpu.make_async_copy(out.at[:, pl.ds(0, 64)], out_hbm.at[:, pl.ds(0, 64)], sem.at[0])]
    copies[0].start()
    for j in range(8):
        cols = slice(WIDTH + j * STEP, WIDTH + (j + 1) * STEP)
        down = (dot(hid_t[0], mine[:, cols]) + dot(hid_t[1], other[:, cols])).astype(bf16)
        row, col = 64 + 16 * (j // 4), (j % 4) * STEP
        for k in range(Z * X):
            out[k, row : row + 16, col : col + STEP] = down[k * 16 : (k + 1) * 16]
        if j % 4 == 3:
            part = pl.ds(row, 16)
            copies.append(pltpu.make_async_copy(out.at[:, part], out_hbm.at[:, part], sem.at[1 + j // 4]))
            copies[-1].start()
    for copy in copies:
        copy.wait()


def weights(at, mine, other):
    return call(
        weights_body,
        "weights",
        [((Z * X, 96, 1024), bf16)],
        (at, mine, other),
        3 * 2 * N * WIDTH * FF,
        12 << 20,
        in_specs=[scalars(), full(), full()],
        out_specs=[anywhere()],
        scratch=[
            VMEM((Z * X, 96, 1024), bf16),
            VMEM((2, 1024, N), bf16),
            VMEM((2, 256, N), bf16),
            pltpu.SemaphoreType.DMA((3,)),
        ],
        limit=16,
        held=(1, 2),
    )[0]


def gather_sum_body(pieces_ref, up_ref, down_ref):
    for j in range(2):
        at = j * 512
        total = pieces_ref[0, :, at : at + 512].astype(f32)
        for k in range(1, Z * X):
            total = total + pieces_ref[k, :, at : at + 512].astype(f32)
        up_ref[0, :, at : at + 512] = total[:64]
        down_ref[0, :, at : at + 512] = total[64:80]
        down_ref[0, :, 1024 + at : 1024 + at + 512] = total[80:96]


def project_body(*refs):
    own, rest, place_hbm, turned_hbm, gate, cot_hbm, r0, r1, r2, r3, resid_hbm, gates, o0, o1, o2, o3 = refs[:16]
    place, turned, cot, back, w, resid, in_sem, w_sem, out_sem = refs[16:]
    copies = [
        pltpu.make_async_copy(r, back.at[pl.ds(s * CAP, CAP), :], in_sem.at[s]) for s, r in enumerate((r0, r1, r2, r3))
    ]
    copies.append(pltpu.make_async_copy(turned_hbm, turned, in_sem.at[4]))
    late = pltpu.make_async_copy(place_hbm, place, in_sem.at[6])
    copies.append(pltpu.make_async_copy(cot_hbm, cot, in_sem.at[5]))
    slabs = [pltpu.make_async_copy(own, w.at[0], w_sem.at[0])]
    for s in range(1, Y):
        slabs.append(pltpu.make_async_copy(rest.at[:, s - 1], w.at[s].reshape(rest.shape[0], -1, WIDTH), w_sem.at[s]))
    for copy in copies + slabs + [late]:
        copy.start()
    for copy in copies:
        copy.wait()
    wide = 512
    for j in range(WIDTH // wide):
        cols = slice(j * wide, (j + 1) * wide)
        resid[:, cols] = (cot[:, cols].astype(f32) + dot(turned[...], back[:, cols])).astype(bf16)
    sent = [pltpu.make_async_copy(resid, resid_hbm, out_sem)]
    sent[0].start()
    for s, out in enumerate((o0, o1, o2, o3)):
        slabs[s].wait()
        out[...] = dot_t(resid[...], w[s]).astype(bf16)
    late.wait()
    tail = back[:, WIDTH:].astype(f32)
    picked = jnp.sum(place[...].astype(f32) * (tail[:, 0:1] + tail[:, 1:2]), axis=0, keepdims=True)
    gates[...] = (picked / gate[...].astype(f32)).astype(bf16)
    for copy in sent:
        copy.wait()


def project(w_out, rest, place, turned, gate_row, grad_out, backs):
    shapes = [(ROWS, WIDTH), (1, ROWS)] + [(ROWS, 512)] * Y
    ins = (w_out, rest, place, turned, gate_row, grad_out, *backs)
    in_specs, out_specs = [anywhere() for _ in ins], [anywhere() for _ in shapes]
    in_specs[4] = full()
    out_specs[1:] = [full()] * 5
    return call(
        project_body,
        "project",
        [(s, bf16) for s in shapes],
        ins,
        2 * ROWS * WIDTH * WIDTH + 2 * ROWS * N * WIDTH,
        10 << 20,
        in_specs=in_specs,
        out_specs=out_specs,
        scratch=[
            VMEM((N, ROWS), bf16),
            VMEM((ROWS, N), bf16),
            VMEM((ROWS, WIDTH), bf16),
            VMEM((N, BACK), bf16),
            VMEM((Y, 512, WIDTH), bf16),
            VMEM((ROWS, WIDTH), bf16),
            pltpu.SemaphoreType.DMA((7,)),
            pltpu.SemaphoreType.DMA((Y,)),
            pltpu.SemaphoreType.DMA,
        ],
        limit=20,
        near=(2, 3, 4, 5),
    )


def state_body(at_ref, g0, g1, g2, g3, q_ref, grad_ref, state_ref):
    y, block = at_ref[0], at_ref[1]
    ramp = lax.broadcasted_iota(jnp.int32, (ROWS, 1), 0)
    sums = [jnp.zeros((HD, 2 * HD), f32) for _ in range(HEADS)]
    for s, g in enumerate((g0, g1, g2, g3)):
        off = pl.multiple_of(lax.rem(y + s, Y) * ROWS, ROWS)
        inverse = 1.0 / (3 * BLOCKS * TOK + block * TOK + off + ramp + 1).astype(f32)
        grad_ref[pl.ds(off, ROWS), :] = g[...]
        for h in range(HEADS):
            cols = slice(h * HD, (h + 1) * HD)
            both = jnp.concatenate(split(g[:, cols].astype(f32) * inverse), axis=1)
            sums[h] += t_dot(q_ref[pl.ds(off, ROWS), cols], both)
    for h in range(HEADS):
        state_ref[h * HD : (h + 1) * HD, :] = sums[h][:, :HD] + sums[h][:, HD:]


def head_state(at, grads, queries):
    return call(
        state_body,
        "state",
        [((TOK, HEADS * HD), bf16), ((HEADS * HD, HD), f32)],
        (at, *grads, queries),
        HEADS * 2 * TOK * HD * 2 * HD,
        4 << 20,
        in_specs=[scalars()] + [full()] * 5,
        limit=8,
        held=(1, 2, 3, 4, 5),
        near=(0, 1),
    )


def chip_body(state, other, chip, chip16):
    chip[...] = state[...] + other[...]
    chip16[...] = chip[...].astype(bf16)


def line_body(chip, x1, x2, x3, line16):
    total = chip[...] + x1[...].astype(f32) + x2[...].astype(f32) + x3[...].astype(f32)
    line16[...] = total.astype(bf16)


SUB = 256
PARTS = TOK // SUB
PAIR = 2


def triangle(lower):
    row = lax.broadcasted_iota(jnp.int32, (SUB, SUB), 0)
    col = lax.broadcasted_iota(jnp.int32, (SUB, SUB), 1)
    return (col <= row) if lower else (col >= row)


def query_part(block, h, g_ref, v_ref, k_ref, prior_ref, out_ref):
    mask = triangle(True)
    ramp = lax.broadcasted_iota(jnp.int32, (SUB, 1), 0)
    cols = slice(h * HD, (h + 1) * HD)
    prior = jnp.concatenate(split(prior_ref[h]), axis=0)
    for i in range(PARTS):
        rows, upto = slice(i * SUB, (i + 1) * SUB), (i + 1) * SUB
        g = g_ref[rows, cols]
        mix = dot_t(g, v_ref[:upto, cols])
        edge = jnp.where(mask, mix[:, i * SUB :], 0.0).astype(bf16)
        if i:
            edge = jnp.concatenate([mix[:, : i * SUB].astype(bf16), edge], axis=1)
        before = dot_t(g, prior)
        total = before[:, :HD] + before[:, HD:] + dot(edge, k_ref[:upto, cols])
        count = (3 * BLOCKS * TOK + block * TOK + i * SUB + ramp + 1).astype(f32)
        out_ref[rows, cols] = (total / count).astype(bf16)


def later_part(block, h, a_ref, b_ref, c_ref, out_ref):
    mask = triangle(False)
    ramp = lax.broadcasted_iota(jnp.int32, (1, TOK), 1)
    inverse = 1.0 / (3 * BLOCKS * TOK + block * TOK + ramp + 1).astype(f32)
    cols = slice(h * HD, (h + 1) * HD)
    for i in range(PARTS):
        at = i * SUB
        rows = slice(at, at + SUB)
        mix = dot_t(a_ref[rows, cols], b_ref[at:, cols]) * inverse[:, at:]
        edge = jnp.where(mask, mix[:, :SUB], 0.0).astype(bf16)
        if i < PARTS - 1:
            edge = jnp.concatenate([edge, mix[:, SUB:].astype(bf16)], axis=1)
        out_ref[rows, cols] = dot(edge, c_ref[at:, cols]).astype(bf16)


def query_key_body(at_ref, q_ref, k_ref, v_ref, g_ref, prior_ref, out_ref, key_ref):
    block = at_ref[1]
    for h in range(HEADS):
        query_part(block, h, g_ref, v_ref, k_ref, prior_ref, out_ref)
        later_part(block, h, v_ref, g_ref, q_ref, key_ref)


def value_body(at_ref, q_ref, k_ref, g_ref, value_ref):
    for h in range(HEADS):
        later_part(at_ref[1], h, k_ref, q_ref, g_ref, value_ref)


def head_call(body, name, ins, outs, near):
    return call(
        body,
        name,
        [((TOK, HEADS * HD), bf16)] * outs,
        ins,
        10 * HEADS * 4 * SUB * SUB * HD * outs,
        6 << 20,
        in_specs=[scalars()] + [full()] * (len(ins) - 1),
        limit=16,
        held=range(1, len(ins)),
        near=(near,),
    )


def final_body(spot_ref, other, x1, x2, x3, z1, z2, z3, v_ref, k_ref, key_ref, value_ref, key_hbm, value_hbm, outs, sem):
    z, x, core = spot_ref[2], spot_ref[3], spot_ref[4]
    copies = []
    for h in range(HEADS):
        rows, cols = slice(h * HD, (h + 1) * HD), slice(h * HD, (h + 1) * HD)
        later = jnp.where(core == 0, other[rows], 0.0)
        for s, a, b in ((1, x1, z1), (2, x2, z2), (3, x3, z3)):
            later += jnp.where(s > x, a[rows].astype(f32), 0.0) + jnp.where(s > z, b[rows].astype(f32), 0.0)
        hi, lo = split(later)
        key = dot_t(v_ref[:, cols], jnp.concatenate([hi, lo], axis=0))
        outs[0, :, cols] = (key_ref[:, cols].astype(f32) + key[:, :HD] + key[:, HD:]).astype(bf16)
        value = dot(k_ref[:, cols], jnp.concatenate([hi, lo], axis=1))
        outs[1, :, cols] = (value_ref[:, cols].astype(f32) + value[:, :HD] + value[:, HD:]).astype(bf16)
        here = pl.ds(h * HD, HD)
        for k, out in enumerate((key_hbm, value_hbm)):
            copy = pltpu.make_async_copy(outs.at[k, :, here], out.at[:, here], sem.at[2 * h + k])
            copy.start()
            copies.append(copy)
    for copy in copies:
        copy.wait()


def final(spot, sums, values, keys, key_here, value_here):
    return call(
        final_body,
        "final",
        [((TOK, HEADS * HD), bf16)] * 2,
        (spot, *sums, values, keys, key_here, value_here),
        HEADS * 8 * TOK * HD * HD,
        8 << 20,
        in_specs=[scalars()] + [full()] * 11,
        out_specs=[anywhere()] * 2,
        scratch=[VMEM((2, TOK, HEADS * HD), bf16), pltpu.SemaphoreType.DMA((2 * HEADS,))],
        limit=12,
        held=range(1, 12),
    )


def index(z, x, c):
    return (z * X + x) * C + c


def spots():
    return [(z, x, c) for z in range(Z) for x in range(X) for c in range(C)]


def along_y(a, s):
    return lax.ppermute(a, "exp", [(i, (i + s) % Y) for i in range(Y)])


def along_x(a, s):
    return lax.ppermute(a, "ctx", [(index(z, x, c), index(z, (x + s) % X, c)) for z, x, c in spots()])


def along_z(a, s):
    return lax.ppermute(a, "ctx", [(index(z, x, c), index((z + s) % Z, x, c)) for z, x, c in spots()])


def across(a):
    return lax.ppermute(a, "ctx", [(i, i ^ 1) for i in range(BLOCKS)])


def on_device(
    attn_query,
    attn_key,
    attn_value,
    prefix_state,
    moe_in,
    grad_out,
    router_gates,
    expert_ids,
    w_gate_up,
    w_down,
    w_out,
):
    y = lax.axis_index("exp")
    block = lax.axis_index("ctx")
    z, x, c = block >> 3, (block >> 1) & 3, block & 1
    at = jnp.stack([y, block, z, x, c]).astype(jnp.int32)

    slab = w_out.shape[0] // BLOCKS
    piece = lax.dynamic_slice_in_dim(w_out, block * slab, slab, 0)
    pieces = jnp.concatenate([along_y(piece, s) for s in (1, 2, 3)], axis=0)
    gate_row = router_gates.reshape(1, ROWS)
    place, turned, *chunks = pack(at, expert_ids.reshape(1, ROWS), gate_row, moe_in, grad_out)
    pieces, chunks[1] = lax.optimization_barrier((pieces, chunks[1]))
    rest = lax.all_gather(pieces[None], "ctx", axis=0, tiled=True)
    rest = rest.reshape(BLOCKS, 3, slab, WIDTH)

    held = [chunks[0]] + [along_y(chunks[s], s) for s in (1, 2, 3)]
    w_pair, chunks[0] = lax.optimization_barrier((w_gate_up, chunks[0]))
    held[0] = chunks[0]
    prior = prefix_state[0]
    w_pair, w_back = fetch(w_pair, w_down)
    queries, keys, values = attn_query, attn_key, attn_value
    b0, b1, b2, b3, bundle = expert(held, w_pair, w_back)
    backs = [b0] + [along_y(b, -s) for s, b in ((1, b1), (2, b2), (3, b3))]
    other_bundle, backs[1] = lax.optimization_barrier((across(bundle), backs[1]))
    partial = weights(at, bundle, other_bundle)
    groups = [[index(i, j, k) for i in range(Z) for j in range(X)] for k in range(C)]
    exchanged = lax.all_to_all(partial, "ctx", 0, 0, axis_index_groups=groups, tiled=True)

    grad_resid, gates_out, *per_head = project(w_out, rest, place, turned, gate_row, grad_out, backs)
    grad_gates = gates_out.reshape(ROWS, 1)
    grads = [per_head[0]] + [along_y(per_head[s], -s) for s in (1, 2, 3)]
    attn_grad, state = head_state(at, grads, queries)

    other = across(state)
    size = (HEADS * HD, HD)
    outs = [(size, f32), (size, bf16)]
    chip, chip16 = call(chip_body, "chip", outs, (state, other), limit=4, held=(0, 1), near=(0, 1))
    from_x = [along_x(chip16, s) for s in (1, 2, 3)]
    ins = (at, queries, keys, values, attn_grad, prior)
    grad_query, key_here = head_call(query_key_body, "query_key", ins, 2, 1)
    chip, key_here = lax.optimization_barrier((chip, key_here))
    (line16,) = call(line_body, "line", [(size, bf16)], (chip, *from_x), limit=4, held=range(4), near=(0,))
    from_z = [along_z(line16, s) for s in (1, 2, 3)]
    (value_here,) = head_call(value_body, "value", (at, queries, keys, attn_grad), 1, 0)
    sums = (other, *from_x, *from_z)
    grad_key, grad_value = final(at, sums, values, keys, key_here, value_here)

    exchanged, grad_key = lax.optimization_barrier((exchanged, grad_key))
    outs = [((1, 64, 1024), f32), ((1, 16, WIDTH), f32)]
    grad_gate_up, grad_down = call(gather_sum_body, "gather_sum", outs, (exchanged,), 0, 4 << 20, free=(0,))
    return (grad_query, grad_key, grad_value, grad_resid, grad_gates, grad_gate_up, grad_down)


def solution(mesh):
    whole = P(("ctx", "exp"), None)
    split_cols = P("ctx", "exp")
    return jax.shard_map(
        on_device,
        mesh=mesh,
        in_specs=(
            split_cols,
            split_cols,
            split_cols,
            P("ctx", "exp", None, None),
            whole,
            whole,
            whole,
            whole,
            P("exp", None, None),
            P("exp", None, None),
            P("exp", None),
        ),
        out_specs=(
            split_cols,
            split_cols,
            split_cols,
            whole,
            whole,
            P("exp", "ctx", None),
            P("exp", "ctx", None),
        ),
        check_vma=False,
    )
```

```python
import jax
import jax.numpy as jnp
from jax import lax
from jax.experimental import pallas as pl
from jax.experimental.pallas import tpu as pltpu
from jax.sharding import PartitionSpec as P

bf16 = jnp.bfloat16
f32 = jnp.float32
VMEM = pltpu.VMEM
SMEM = pltpu.SMEM
Z, X, C, Y = 4, 4, 2, 4
CAP, ROWS, WIDTH, FF, HD, HEADS, TOK = 96, 256, 2048, 512, 128, 4, 1024
WEIGHT = 3
EARLY = ("pack", "fetch", "expert", "down_grad", "up_grad")
BLOCKS = Z * X * C


def dot(a, b):
    return lax.dot_general(a, b, (((1,), (0,)), ((), ())), preferred_element_type=f32)


def dot_t(a, b):
    return lax.dot_general(a, b, (((1,), (1,)), ((), ())), preferred_element_type=f32)


def t_dot(a, b):
    return lax.dot_general(a, b, (((0,), (0,)), ((), ())), preferred_element_type=f32)


def split(a):
    hi = a.astype(bf16)
    return hi, (a - hi.astype(f32)).astype(bf16)


def full():
    return pl.BlockSpec(memory_space=VMEM)


def scalars():
    return pl.BlockSpec(memory_space=SMEM)


def call(body, name, outs, ins, flops=0, moved=0, grid=None, in_specs=None, out_specs=None, limit=24, scratch=(), free=(), near=(), held=()):
    weight = 4 if name in EARLY else WEIGHT
    kwargs = {} if grid is None else {"grid": grid}
    specs = in_specs or [full() for _ in ins]
    ins = [
        a if spec.memory_space is SMEM or i in free else pltpu.with_memory_space_constraint(a, VMEM if i in held else pltpu.HBM)
        for i, (a, spec) in enumerate(zip(ins, specs))
    ]
    return pl.pallas_call(
        body,
        name=name,
        out_shape=[(VMEM if near is True or i in near else pltpu.HBM)(s, t) for i, (s, t) in enumerate(outs)],
        in_specs=specs,
        out_specs=out_specs or [full() for _ in outs],
        scratch_shapes=scratch,
        compiler_params=pltpu.CompilerParams(vmem_limit_bytes=limit << 20),
        cost_estimate=pl.CostEstimate(flops=weight * flops, bytes_accessed=weight * moved, transcendentals=0),
        **kwargs,
    )(*ins)


def pack_body(at_ref, ids_ref, gate_ref, moe_ref, cot_ref, place_ref, turned_ref, c0, c1, c2, c3, gate_col):
    @pl.when(pl.program_id(0) == 0)
    def _():
        rel = ids_ref[...] - at_ref[0]
        rel = jnp.where(rel < 0, rel + Y, rel)
        member = (lax.broadcasted_iota(jnp.int32, (8, ROWS), 0) == rel).astype(f32)
        row = lax.broadcasted_iota(jnp.int32, (ROWS, ROWS), 0)
        col = lax.broadcasted_iota(jnp.int32, (ROWS, ROWS), 1)
        earlier = dot(member.astype(bf16), (row < col).astype(bf16))
        slot = jnp.sum(earlier * member, axis=0, keepdims=True).astype(jnp.int32)
        target = rel * CAP + slot
        places = lax.broadcasted_iota(jnp.int32, (Y * CAP, ROWS), 0)
        place_ref[...] = (places == target).astype(bf16)
        spots_col = jnp.sum(jnp.where(row == col, target.astype(f32), 0.0), axis=1, keepdims=True)
        lanes = lax.broadcasted_iota(jnp.int32, (ROWS, Y * CAP), 1)
        turned_ref[...] = (lanes == spots_col.astype(jnp.int32)).astype(bf16)
        gate = gate_ref[...].astype(f32)
        gate_col[...] = jnp.sum(jnp.where(row == col, gate, 0.0), axis=1, keepdims=True)

    place = place_ref[...]
    scaled = (gate_col[...] * cot_ref[...].astype(f32)).astype(bf16)
    for half, rows in enumerate((moe_ref[...], scaled)):
        part = dot(place, rows).astype(bf16)
        for s, chunk in enumerate((c0, c1, c2, c3)):
            chunk[half] = part[s * CAP : (s + 1) * CAP]


def pack(at, ids, gates, moe_in, grad_out):
    step = 1024
    outs = [((Y * CAP, ROWS), bf16), ((ROWS, Y * CAP), bf16)] + [((2, CAP, WIDTH), bf16)] * Y
    ins = (at, ids, gates, moe_in, grad_out)
    row = pl.BlockSpec((1, ROWS), lambda j: (0, 0))
    tile = pl.BlockSpec((ROWS, step), lambda j: (0, j))
    return call(
        pack_body,
        "pack",
        outs,
        ins,
        2 * 384 * 256 * 4096,
        5 << 20,
        grid=(WIDTH // step,),
        in_specs=[scalars(), row, row, tile, tile],
        out_specs=[pl.BlockSpec((Y * CAP, ROWS), lambda j: (0, 0)), pl.BlockSpec((ROWS, Y * CAP), lambda j: (0, 0))]
        + [pl.BlockSpec((2, CAP, step), lambda j: (0, 0, j))] * Y,
        scratch=[VMEM((ROWS, 1), f32)],
        limit=16,
    )


BACK = WIDTH + 128
N = Y * CAP
BUNDLE = WIDTH + 2 * FF
SIDE = WIDTH + FF
GB = HID = WIDTH
STEP = 256


def expert_body(r0, r1, r2, r3, wp, wb, b0, b1, b2, b3, held, side, back, in_sem, out_sem):
    arrived = (r0, r1, r2, r3)
    backs = (b0, b1, b2, b3)
    tiles = FF // STEP

    def incoming(half, s):
        dst = (side if half else held).at[pl.ds(s * CAP, CAP), pl.ds(0, WIDTH)]
        return pltpu.make_async_copy(arrived[s].at[half], dst, in_sem.at[half * Y + s])

    for s in range(Y):
        incoming(0, s).start()
    for s in range(Y):
        incoming(1, s).start()
    for s in range(Y):
        incoming(0, s).wait()
    total = jnp.zeros((N, 1), f32)
    for j in range(tiles):
        at, up = j * STEP, FF + j * STEP
        first = dot(held[:, :WIDTH], wp[0, :, at : at + STEP])
        second = dot(held[:, :WIDTH], wp[0, :, up : up + STEP])
        if j == 0:
            for s in range(Y):
                incoming(1, s).wait()
        grad_hidden = dot_t(side[:, :WIDTH], wb[0, at : at + STEP, :])
        s = 1.0 / (1.0 + jnp.exp(-first))
        silu = first * s
        hidden = (silu * second).astype(bf16)
        side[:, HID + at : HID + at + STEP] = hidden
        total += jnp.sum(hidden.astype(f32) * grad_hidden, axis=1, keepdims=True)
        slope = s * (1.0 + first * (1.0 - s))
        held[:, GB + at : GB + at + STEP] = (grad_hidden * second * slope).astype(bf16)
        held[:, GB + up : GB + up + STEP] = (grad_hidden * silu).astype(bf16)
    hi, lo = split(total)
    lane = lax.broadcasted_iota(jnp.int32, (N, 128), 1)
    back[:, WIDTH:] = jnp.where(lane == 0, hi.astype(f32), lo.astype(f32)).astype(bf16)
    outgoing = []
    bounds = (0, WIDTH // 2, BACK)
    for part in range(2):
        lo_col, hi_col = bounds[part], bounds[part + 1]
        for at in range(lo_col, min(hi_col, WIDTH), STEP):
            back[:, at : at + STEP] = dot_t(held[:, GB:], wp[0, at : at + STEP, :]).astype(bf16)
        cols = pl.ds(lo_col, hi_col - lo_col)
        for s in range(Y):
            src = back.at[pl.ds(s * CAP, CAP), cols]
            copy = pltpu.make_async_copy(src, backs[s].at[:, cols], out_sem.at[part * Y + s])
            copy.start()
            outgoing.append(copy)
    for copy in outgoing:
        copy.wait()


def anywhere():
    return pl.BlockSpec(memory_space=pl.ANY)


def fetch_body(*refs):
    half = len(refs) // 2
    sem = refs[-1]
    copies = [pltpu.make_async_copy(refs[i], refs[half + i], sem.at[i]) for i in range(half)]
    for copy in copies:
        copy.start()
    for copy in copies:
        copy.wait()


def fetch(*arrays):
    return call(
        fetch_body,
        "fetch",
        [(a.shape, a.dtype) for a in arrays],
        arrays,
        0,
        12 << 20,
        in_specs=[anywhere() for _ in arrays],
        scratch=[pltpu.SemaphoreType.DMA((len(arrays),))],
        limit=2,
        near=True,
    )


def expert(chunks, w_pair, w_back):
    outs = [((CAP, BACK), bf16)] * Y + [((N, BUNDLE), bf16), ((N, SIDE), bf16)]
    ins = (*chunks, w_pair, w_back)
    return call(
        expert_body,
        "expert",
        outs,
        ins,
        5 * 2 * N * WIDTH * FF,
        14 << 20,
        in_specs=[anywhere() for _ in chunks] + [full(), full()],
        out_specs=[anywhere()] * Y + [full()] * 2,
        scratch=[
            VMEM((N, BACK), bf16),
            pltpu.SemaphoreType.DMA((2 * Y,)),
            pltpu.SemaphoreType.DMA((2 * Y,)),
        ],
        limit=16,
        free=(1, 2, 3),
        held=(4, 5),
        near=(Y, Y + 1),
    )


def chooser(core, wide, run):
    row = lax.broadcasted_iota(jnp.int32, (wide // 2, wide), 0)
    col = lax.broadcasted_iota(jnp.int32, (wide // 2, wide), 1)
    return (col == (row // run) * (2 * run) + core * run + row % run).astype(bf16)


def down_body(side, out_hbm, out, hid_t, sem):
    row = lax.broadcasted_iota(jnp.int32, (FF, FF), 0)
    col = lax.broadcasted_iota(jnp.int32, (FF, FF), 1)
    hid_t[...] = dot_t((row == col).astype(bf16), side[:, HID:]).astype(bf16)
    copies = []
    for j in range(WIDTH // 512):
        cols = slice(j * 512, (j + 1) * 512)
        out[:, cols] = dot(hid_t[...], side[:, cols]).astype(bf16)
        here = pl.ds(j * 512, 512)
        copies.append(pltpu.make_async_copy(out.at[:, here], out_hbm.at[:, here], sem.at[j]))
        copies[-1].start()
    for copy in copies:
        copy.wait()


def down_grad(side):
    return call(
        down_body,
        "down_grad",
        [((FF, WIDTH), bf16)],
        (side,),
        2 * N * WIDTH * FF,
        4 << 20,
        in_specs=[full()],
        out_specs=[anywhere()],
        scratch=[VMEM((FF, WIDTH), bf16), VMEM((FF, N), bf16), pltpu.SemaphoreType.DMA((4,))],
        limit=8,
        held=(0,),
    )[0]


def up_body(at_ref, mine, other, out_hbm, out, rows_t, sem):
    pick_row = chooser(at_ref[4], 512, 64)
    for k, src in enumerate((mine, other)):
        for i in range(Z):
            rows_t[k, i * 256 : (i + 1) * 256, :] = dot_t(pick_row, src[:, i * 512 : (i + 1) * 512]).astype(bf16)
    copies = []
    for j in range(4):
        cols = slice(GB + j * STEP, GB + (j + 1) * STEP)
        up = (dot(rows_t[0], mine[:, cols]) + dot(rows_t[1], other[:, cols])).astype(bf16)
        for k in range(Z * X):
            out[k, :, j * STEP : (j + 1) * STEP] = up[k * 64 : (k + 1) * 64]
        here = pl.ds(j * STEP, STEP)
        copies.append(pltpu.make_async_copy(out.at[:, :, here], out_hbm.at[:, :, here], sem.at[j]))
        copies[-1].start()
    for copy in copies:
        copy.wait()


def up_grad(at, mine, other):
    shape = (Z * X, 64, 1024)
    return call(
        up_body,
        "up_grad",
        [(shape, bf16)],
        (at, mine, other),
        2 * 2 * N * WIDTH * FF,
        8 << 20,
        in_specs=[scalars(), full(), full()],
        out_specs=[anywhere()],
        scratch=[VMEM(shape, bf16), VMEM((2, 1024, N), bf16), pltpu.SemaphoreType.DMA((4,))],
        limit=12,
        held=(1, 2),
    )[0]


def gather_sum_body(pieces_ref, up_ref):
    for j in range(2):
        cols = slice(j * 512, (j + 1) * 512)
        total = pieces_ref[0, :, cols].astype(f32)
        for k in range(1, Z * X):
            total = total + pieces_ref[k, :, cols].astype(f32)
        up_ref[0, :, cols] = total


def project_body(*refs):
    own, rest, place_hbm, turned_hbm, gate, cot_hbm, r0, r1, r2, r3, resid_hbm, gates, o0, o1, o2, o3 = refs[:16]
    place, turned, cot, back, w, resid, in_sem, w_sem, out_sem = refs[16:]
    copies = [
        pltpu.make_async_copy(r, back.at[pl.ds(s * CAP, CAP), :], in_sem.at[s]) for s, r in enumerate((r0, r1, r2, r3))
    ]
    copies.append(pltpu.make_async_copy(turned_hbm, turned, in_sem.at[4]))
    late = pltpu.make_async_copy(place_hbm, place, in_sem.at[6])
    copies.append(pltpu.make_async_copy(cot_hbm, cot, in_sem.at[5]))
    slabs = [pltpu.make_async_copy(own, w.at[0], w_sem.at[0])]
    for s in range(1, Y):
        slabs.append(pltpu.make_async_copy(rest.at[:, s - 1], w.at[s].reshape(rest.shape[0], -1, WIDTH), w_sem.at[s]))
    for copy in copies + slabs + [late]:
        copy.start()
    for copy in copies:
        copy.wait()
    wide = 512
    for j in range(WIDTH // wide):
        cols = slice(j * wide, (j + 1) * wide)
        resid[:, cols] = (cot[:, cols].astype(f32) + dot(turned[...], back[:, cols])).astype(bf16)
    sent = [pltpu.make_async_copy(resid, resid_hbm, out_sem)]
    sent[0].start()
    for s, out in enumerate((o0, o1, o2, o3)):
        slabs[s].wait()
        out[...] = dot_t(resid[...], w[s]).astype(bf16)
    late.wait()
    tail = back[:, WIDTH:].astype(f32)
    picked = jnp.sum(place[...].astype(f32) * (tail[:, 0:1] + tail[:, 1:2]), axis=0, keepdims=True)
    gates[...] = (picked / gate[...].astype(f32)).astype(bf16)
    for copy in sent:
        copy.wait()


def project(w_out, rest, place, turned, gate_row, grad_out, backs):
    shapes = [(ROWS, WIDTH), (1, ROWS)] + [(ROWS, 512)] * Y
    ins = (w_out, rest, place, turned, gate_row, grad_out, *backs)
    in_specs, out_specs = [anywhere() for _ in ins], [anywhere() for _ in shapes]
    in_specs[4] = full()
    out_specs[1:] = [full()] * 5
    return call(
        project_body,
        "project",
        [(s, bf16) for s in shapes],
        ins,
        2 * ROWS * WIDTH * WIDTH + 2 * ROWS * N * WIDTH,
        10 << 20,
        in_specs=in_specs,
        out_specs=out_specs,
        scratch=[
            VMEM((N, ROWS), bf16),
            VMEM((ROWS, N), bf16),
            VMEM((ROWS, WIDTH), bf16),
            VMEM((N, BACK), bf16),
            VMEM((Y, 512, WIDTH), bf16),
            VMEM((ROWS, WIDTH), bf16),
            pltpu.SemaphoreType.DMA((7,)),
            pltpu.SemaphoreType.DMA((Y,)),
            pltpu.SemaphoreType.DMA,
        ],
        limit=20,
        near=(2, 3, 4, 5),
    )


def state_body(at_ref, g0, g1, g2, g3, q_ref, grad_ref, state_ref):
    y, block = at_ref[0], at_ref[1]
    ramp = lax.broadcasted_iota(jnp.int32, (ROWS, 1), 0)
    sums = [jnp.zeros((HD, 2 * HD), f32) for _ in range(HEADS)]
    for s, g in enumerate((g0, g1, g2, g3)):
        off = pl.multiple_of(lax.rem(y + s, Y) * ROWS, ROWS)
        inverse = 1.0 / (3 * BLOCKS * TOK + block * TOK + off + ramp + 1).astype(f32)
        grad_ref[pl.ds(off, ROWS), :] = g[...]
        for h in range(HEADS):
            cols = slice(h * HD, (h + 1) * HD)
            both = jnp.concatenate(split(g[:, cols].astype(f32) * inverse), axis=1)
            sums[h] += t_dot(q_ref[pl.ds(off, ROWS), cols], both)
    for h in range(HEADS):
        state_ref[h * HD : (h + 1) * HD, :] = sums[h][:, :HD] + sums[h][:, HD:]


def head_state(at, grads, queries):
    return call(
        state_body,
        "state",
        [((TOK, HEADS * HD), bf16), ((HEADS * HD, HD), f32)],
        (at, *grads, queries),
        HEADS * 2 * TOK * HD * 2 * HD,
        4 << 20,
        in_specs=[scalars()] + [full()] * 5,
        limit=8,
        held=(1, 2, 3, 4, 5),
        near=(0, 1),
    )


def chip_body(state, other, chip, chip16):
    chip[...] = state[...] + other[...]
    chip16[...] = chip[...].astype(bf16)


def line_body(chip, x1, x2, x3, line16):
    total = chip[...] + x1[...].astype(f32) + x2[...].astype(f32) + x3[...].astype(f32)
    line16[...] = total.astype(bf16)


SUB = 256
PARTS = TOK // SUB
PAIR = 2


def triangle(lower):
    row = lax.broadcasted_iota(jnp.int32, (SUB, SUB), 0)
    col = lax.broadcasted_iota(jnp.int32, (SUB, SUB), 1)
    return (col <= row) if lower else (col >= row)


def query_part(block, h, g_ref, v_ref, k_ref, prior_ref, out_ref):
    mask = triangle(True)
    ramp = lax.broadcasted_iota(jnp.int32, (SUB, 1), 0)
    cols = slice(h * HD, (h + 1) * HD)
    prior = jnp.concatenate(split(prior_ref[h]), axis=0)
    for i in range(PARTS):
        rows, upto = slice(i * SUB, (i + 1) * SUB), (i + 1) * SUB
        g = g_ref[rows, cols]
        mix = dot_t(g, v_ref[:upto, cols])
        edge = jnp.where(mask, mix[:, i * SUB :], 0.0).astype(bf16)
        if i:
            edge = jnp.concatenate([mix[:, : i * SUB].astype(bf16), edge], axis=1)
        before = dot_t(g, prior)
        total = before[:, :HD] + before[:, HD:] + dot(edge, k_ref[:upto, cols])
        count = (3 * BLOCKS * TOK + block * TOK + i * SUB + ramp + 1).astype(f32)
        out_ref[rows, cols] = (total / count).astype(bf16)


def later_part(block, h, a_ref, b_ref, c_ref, out_ref):
    mask = triangle(False)
    ramp = lax.broadcasted_iota(jnp.int32, (1, TOK), 1)
    inverse = 1.0 / (3 * BLOCKS * TOK + block * TOK + ramp + 1).astype(f32)
    cols = slice(h * HD, (h + 1) * HD)
    for i in range(PARTS):
        at = i * SUB
        rows = slice(at, at + SUB)
        mix = dot_t(a_ref[rows, cols], b_ref[at:, cols]) * inverse[:, at:]
        edge = jnp.where(mask, mix[:, :SUB], 0.0).astype(bf16)
        if i < PARTS - 1:
            edge = jnp.concatenate([edge, mix[:, SUB:].astype(bf16)], axis=1)
        out_ref[rows, cols] = dot(edge, c_ref[at:, cols]).astype(bf16)


def query_key_body(at_ref, q_ref, k_ref, v_ref, g_ref, prior_ref, out_ref, key_ref):
    block = at_ref[1]
    for h in range(HEADS):
        query_part(block, h, g_ref, v_ref, k_ref, prior_ref, out_ref)
        later_part(block, h, v_ref, g_ref, q_ref, key_ref)


def value_body(at_ref, q_ref, k_ref, g_ref, value_ref):
    for h in range(HEADS):
        later_part(at_ref[1], h, k_ref, q_ref, g_ref, value_ref)


def head_call(body, name, ins, outs, near):
    return call(
        body,
        name,
        [((TOK, HEADS * HD), bf16)] * outs,
        ins,
        10 * HEADS * 4 * SUB * SUB * HD * outs,
        6 << 20,
        in_specs=[scalars()] + [full()] * (len(ins) - 1),
        limit=16,
        held=range(1, len(ins)),
        near=(near,),
    )


def final_body(spot_ref, other, x1, x2, x3, z1, z2, z3, v_ref, k_ref, key_ref, value_ref, key_hbm, value_hbm, outs, sem):
    z, x, core = spot_ref[2], spot_ref[3], spot_ref[4]
    copies = []
    for h in range(HEADS):
        rows, cols = slice(h * HD, (h + 1) * HD), slice(h * HD, (h + 1) * HD)
        later = jnp.where(core == 0, other[rows], 0.0)
        for s, a, b in ((1, x1, z1), (2, x2, z2), (3, x3, z3)):
            later += jnp.where(s > x, a[rows].astype(f32), 0.0) + jnp.where(s > z, b[rows].astype(f32), 0.0)
        hi, lo = split(later)
        key = dot_t(v_ref[:, cols], jnp.concatenate([hi, lo], axis=0))
        outs[0, :, cols] = (key_ref[:, cols].astype(f32) + key[:, :HD] + key[:, HD:]).astype(bf16)
        value = dot(k_ref[:, cols], jnp.concatenate([hi, lo], axis=1))
        outs[1, :, cols] = (value_ref[:, cols].astype(f32) + value[:, :HD] + value[:, HD:]).astype(bf16)
        here = pl.ds(h * HD, HD)
        for k, out in enumerate((key_hbm, value_hbm)):
            copy = pltpu.make_async_copy(outs.at[k, :, here], out.at[:, here], sem.at[2 * h + k])
            copy.start()
            copies.append(copy)
    for copy in copies:
        copy.wait()


def final(spot, sums, values, keys, key_here, value_here):
    return call(
        final_body,
        "final",
        [((TOK, HEADS * HD), bf16)] * 2,
        (spot, *sums, values, keys, key_here, value_here),
        HEADS * 8 * TOK * HD * HD,
        8 << 20,
        in_specs=[scalars()] + [full()] * 11,
        out_specs=[anywhere()] * 2,
        scratch=[VMEM((2, TOK, HEADS * HD), bf16), pltpu.SemaphoreType.DMA((2 * HEADS,))],
        limit=12,
        held=range(1, 12),
    )


def index(z, x, c):
    return (z * X + x) * C + c


def spots():
    return [(z, x, c) for z in range(Z) for x in range(X) for c in range(C)]


def along_y(a, s):
    return lax.ppermute(a, "exp", [(i, (i + s) % Y) for i in range(Y)])


def along_x(a, s):
    return lax.ppermute(a, "ctx", [(index(z, x, c), index(z, (x + s) % X, c)) for z, x, c in spots()])


def along_z(a, s):
    return lax.ppermute(a, "ctx", [(index(z, x, c), index((z + s) % Z, x, c)) for z, x, c in spots()])


def across(a):
    return lax.ppermute(a, "ctx", [(i, i ^ 1) for i in range(BLOCKS)])


def on_device(
    attn_query,
    attn_key,
    attn_value,
    prefix_state,
    moe_in,
    grad_out,
    router_gates,
    expert_ids,
    w_gate_up,
    w_down,
    w_out,
):
    y = lax.axis_index("exp")
    block = lax.axis_index("ctx")
    z, x, c = block >> 3, (block >> 1) & 3, block & 1
    at = jnp.stack([y, block, z, x, c]).astype(jnp.int32)

    slab = w_out.shape[0] // BLOCKS
    piece = lax.dynamic_slice_in_dim(w_out, block * slab, slab, 0)
    pieces = jnp.concatenate([along_y(piece, s) for s in (1, 2, 3)], axis=0)
    gate_row = router_gates.reshape(1, ROWS)
    place, turned, *chunks = pack(at, expert_ids.reshape(1, ROWS), gate_row, moe_in, grad_out)
    pieces, chunks[1] = lax.optimization_barrier((pieces, chunks[1]))
    rest = lax.all_gather(pieces[None], "ctx", axis=0, tiled=True)
    rest = rest.reshape(BLOCKS, 3, slab, WIDTH)

    held = [chunks[0]] + [along_y(chunks[s], s) for s in (1, 2, 3)]
    w_pair, chunks[0] = lax.optimization_barrier((w_gate_up, chunks[0]))
    held[0] = chunks[0]
    prior = prefix_state[0]
    w_pair, w_back = fetch(w_pair, w_down)
    queries, keys, values = attn_query, attn_key, attn_value
    b0, b1, b2, b3, bundle, side = expert(held, w_pair, w_back)
    backs = [b0] + [along_y(b, -s) for s, b in ((1, b1), (2, b2), (3, b3))]
    down = lax.psum_scatter(down_grad(side), "ctx", scatter_dimension=0, tiled=True)
    other_bundle = across(bundle)
    partial = up_grad(at, bundle, other_bundle)
    _, backs[2], backs[3] = lax.optimization_barrier((partial, backs[2], backs[3]))
    groups = [[index(i, j, k) for i in range(Z) for j in range(X)] for k in range(C)]
    exchanged = lax.all_to_all(partial, "ctx", 0, 0, axis_index_groups=groups, tiled=True)

    grad_resid, gates_out, *per_head = project(w_out, rest, place, turned, gate_row, grad_out, backs)
    grad_gates = gates_out.reshape(ROWS, 1)
    grads = [per_head[0]] + [along_y(per_head[s], -s) for s in (1, 2, 3)]
    attn_grad, state = head_state(at, grads, queries)

    other = across(state)
    size = (HEADS * HD, HD)
    outs = [(size, f32), (size, bf16)]
    chip, chip16 = call(chip_body, "chip", outs, (state, other), limit=4, held=(0, 1), near=(0, 1))
    from_x = [along_x(chip16, s) for s in (1, 2, 3)]
    ins = (at, queries, keys, values, attn_grad, prior)
    grad_query, key_here = head_call(query_key_body, "query_key", ins, 2, 1)
    chip, key_here = lax.optimization_barrier((chip, key_here))
    (line16,) = call(line_body, "line", [(size, bf16)], (chip, *from_x), limit=4, held=range(4), near=(0,))
    from_z = [along_z(line16, s) for s in (1, 2, 3)]
    (value_here,) = head_call(value_body, "value", (at, queries, keys, attn_grad), 1, 0)
    sums = (other, *from_x, *from_z)
    grad_key, grad_value = final(at, sums, values, keys, key_here, value_here)

    exchanged, down, grad_key = lax.optimization_barrier((exchanged, down, grad_key))
    outs = [((1, 64, 1024), f32)]
    (grad_gate_up,) = call(gather_sum_body, "gather_sum", outs, (exchanged,), 0, 4 << 20, limit=8, free=(0,))
    grad_down = down.astype(f32)[None]
    return (grad_query, grad_key, grad_value, grad_resid, grad_gates, grad_gate_up, grad_down)


def solution(mesh):
    whole = P(("ctx", "exp"), None)
    split_cols = P("ctx", "exp")
    return jax.shard_map(
        on_device,
        mesh=mesh,
        in_specs=(
            split_cols,
            split_cols,
            split_cols,
            P("ctx", "exp", None, None),
            whole,
            whole,
            whole,
            whole,
            P("exp", None, None),
            P("exp", None, None),
            P("exp", None),
        ),
        out_specs=(
            split_cols,
            split_cols,
            split_cols,
            whole,
            whole,
            P("exp", "ctx", None),
            P("exp", "ctx", None),
        ),
        check_vma=False,
    )
```

```python
import jax
import jax.numpy as jnp
from jax import lax
from jax.experimental import pallas as pl
from jax.experimental.pallas import tpu as pltpu
from jax.sharding import PartitionSpec as P

bf16 = jnp.bfloat16
f32 = jnp.float32
VMEM = pltpu.VMEM
SMEM = pltpu.SMEM
Z, X, C, Y = 4, 4, 2, 4
CAP, ROWS, WIDTH, FF, HD, HEADS, TOK = 96, 256, 2048, 512, 128, 4, 1024
WEIGHT = 4
EARLY = ("pack", "fetch", "expert", "weights")
BLOCKS = Z * X * C


def dot(a, b):
    return lax.dot_general(a, b, (((1,), (0,)), ((), ())), preferred_element_type=f32)


def dot_t(a, b):
    return lax.dot_general(a, b, (((1,), (1,)), ((), ())), preferred_element_type=f32)


def t_dot(a, b):
    return lax.dot_general(a, b, (((0,), (0,)), ((), ())), preferred_element_type=f32)


def split(a):
    hi = a.astype(bf16)
    return hi, (a - hi.astype(f32)).astype(bf16)


def full():
    return pl.BlockSpec(memory_space=VMEM)


def scalars():
    return pl.BlockSpec(memory_space=SMEM)


def call(body, name, outs, ins, flops=0, moved=0, grid=None, in_specs=None, out_specs=None, limit=24, scratch=(), free=(), near=(), held=()):
    weight = 4 if name in EARLY else WEIGHT
    kwargs = {} if grid is None else {"grid": grid}
    specs = in_specs or [full() for _ in ins]
    ins = [
        a if spec.memory_space is SMEM or i in free else pltpu.with_memory_space_constraint(a, VMEM if i in held else pltpu.HBM)
        for i, (a, spec) in enumerate(zip(ins, specs))
    ]
    return pl.pallas_call(
        body,
        name=name,
        out_shape=[(VMEM if near is True or i in near else pltpu.HBM)(s, t) for i, (s, t) in enumerate(outs)],
        in_specs=specs,
        out_specs=out_specs or [full() for _ in outs],
        scratch_shapes=scratch,
        compiler_params=pltpu.CompilerParams(vmem_limit_bytes=limit << 20),
        cost_estimate=pl.CostEstimate(flops=weight * flops, bytes_accessed=weight * moved, transcendentals=0),
        **kwargs,
    )(*ins)


def pack_body(at_ref, ids_ref, gate_ref, moe_ref, cot_ref, place_ref, turned_ref, c0, c1, c2, c3, gate_col):
    @pl.when(pl.program_id(0) == 0)
    def _():
        rel = ids_ref[...] - at_ref[0]
        rel = jnp.where(rel < 0, rel + Y, rel)
        member = (lax.broadcasted_iota(jnp.int32, (8, ROWS), 0) == rel).astype(f32)
        row = lax.broadcasted_iota(jnp.int32, (ROWS, ROWS), 0)
        col = lax.broadcasted_iota(jnp.int32, (ROWS, ROWS), 1)
        earlier = dot(member.astype(bf16), (row < col).astype(bf16))
        slot = jnp.sum(earlier * member, axis=0, keepdims=True).astype(jnp.int32)
        target = rel * CAP + slot
        places = lax.broadcasted_iota(jnp.int32, (Y * CAP, ROWS), 0)
        place_ref[...] = (places == target).astype(bf16)
        spots_col = jnp.sum(jnp.where(row == col, target.astype(f32), 0.0), axis=1, keepdims=True)
        lanes = lax.broadcasted_iota(jnp.int32, (ROWS, Y * CAP), 1)
        turned_ref[...] = (lanes == spots_col.astype(jnp.int32)).astype(bf16)
        gate = gate_ref[...].astype(f32)
        gate_col[...] = jnp.sum(jnp.where(row == col, gate, 0.0), axis=1, keepdims=True)

    place = place_ref[...]
    scaled = (gate_col[...] * cot_ref[...].astype(f32)).astype(bf16)
    for half, rows in enumerate((moe_ref[...], scaled)):
        part = dot(place, rows).astype(bf16)
        for s, chunk in enumerate((c0, c1, c2, c3)):
            chunk[half] = part[s * CAP : (s + 1) * CAP]


def pack(at, ids, gates, moe_in, grad_out):
    step = 1024
    outs = [((Y * CAP, ROWS), bf16), ((ROWS, Y * CAP), bf16)] + [((2, CAP, WIDTH), bf16)] * Y
    ins = (at, ids, gates, moe_in, grad_out)
    row = pl.BlockSpec((1, ROWS), lambda j: (0, 0))
    tile = pl.BlockSpec((ROWS, step), lambda j: (0, j))
    return call(
        pack_body,
        "pack",
        outs,
        ins,
        2 * 384 * 256 * 4096,
        5 << 20,
        grid=(WIDTH // step,),
        in_specs=[scalars(), row, row, tile, tile],
        out_specs=[pl.BlockSpec((Y * CAP, ROWS), lambda j: (0, 0)), pl.BlockSpec((ROWS, Y * CAP), lambda j: (0, 0))]
        + [pl.BlockSpec((2, CAP, step), lambda j: (0, 0, j))] * Y,
        scratch=[VMEM((ROWS, 1), f32)],
        limit=16,
    )


BACK = WIDTH + 128
N = Y * CAP
BUNDLE = 2 * WIDTH + 3 * FF
GB, HID = 2 * WIDTH, 2 * WIDTH + 2 * FF
STEP = 256


def expert_body(r0, r1, r2, r3, wp, wb, b0, b1, b2, b3, held, back, in_sem, out_sem):
    arrived = (r0, r1, r2, r3)
    backs = (b0, b1, b2, b3)
    tiles = FF // STEP

    def incoming(half, s):
        dst = held.at[pl.ds(s * CAP, CAP), pl.ds(half * WIDTH, WIDTH)]
        return pltpu.make_async_copy(arrived[s].at[half], dst, in_sem.at[half * Y + s])

    for s in range(Y):
        incoming(0, s).start()
    for s in range(Y):
        incoming(1, s).start()
    for s in range(Y):
        incoming(0, s).wait()
    total = jnp.zeros((N, 1), f32)
    for j in range(tiles):
        at, up = j * STEP, FF + j * STEP
        first = dot(held[:, :WIDTH], wp[0, :, at : at + STEP])
        second = dot(held[:, :WIDTH], wp[0, :, up : up + STEP])
        if j == 0:
            for s in range(Y):
                incoming(1, s).wait()
        grad_hidden = dot_t(held[:, WIDTH:GB], wb[0, at : at + STEP, :])
        s = 1.0 / (1.0 + jnp.exp(-first))
        silu = first * s
        hidden = (silu * second).astype(bf16)
        held[:, HID + at : HID + at + STEP] = hidden
        total += jnp.sum(hidden.astype(f32) * grad_hidden, axis=1, keepdims=True)
        slope = s * (1.0 + first * (1.0 - s))
        held[:, GB + at : GB + at + STEP] = (grad_hidden * second * slope).astype(bf16)
        held[:, GB + up : GB + up + STEP] = (grad_hidden * silu).astype(bf16)
    hi, lo = split(total)
    lane = lax.broadcasted_iota(jnp.int32, (N, 128), 1)
    back[:, WIDTH:] = jnp.where(lane == 0, hi.astype(f32), lo.astype(f32)).astype(bf16)
    outgoing = []
    bounds = (0, WIDTH // 2, BACK)
    for part in range(2):
        lo_col, hi_col = bounds[part], bounds[part + 1]
        for at in range(lo_col, min(hi_col, WIDTH), STEP):
            back[:, at : at + STEP] = dot_t(held[:, GB:HID], wp[0, at : at + STEP, :]).astype(bf16)
        cols = pl.ds(lo_col, hi_col - lo_col)
        for s in range(Y):
            src = back.at[pl.ds(s * CAP, CAP), cols]
            copy = pltpu.make_async_copy(src, backs[s].at[:, cols], out_sem.at[part * Y + s])
            copy.start()
            outgoing.append(copy)
    for copy in outgoing:
        copy.wait()


def anywhere():
    return pl.BlockSpec(memory_space=pl.ANY)


def fetch_body(*refs):
    half = len(refs) // 2
    sem = refs[-1]
    copies = [pltpu.make_async_copy(refs[i], refs[half + i], sem.at[i]) for i in range(half)]
    for copy in copies:
        copy.start()
    for copy in copies:
        copy.wait()


def fetch(*arrays):
    return call(
        fetch_body,
        "fetch",
        [(a.shape, a.dtype) for a in arrays],
        arrays,
        0,
        12 << 20,
        in_specs=[anywhere() for _ in arrays],
        scratch=[pltpu.SemaphoreType.DMA((len(arrays),))],
        limit=2,
        near=True,
    )


def expert(chunks, w_pair, w_back):
    outs = [((CAP, BACK), bf16)] * Y + [((N, BUNDLE), bf16)]
    ins = (*chunks, w_pair, w_back)
    return call(
        expert_body,
        "expert",
        outs,
        ins,
        5 * 2 * N * WIDTH * FF,
        14 << 20,
        in_specs=[anywhere() for _ in chunks] + [full(), full()],
        out_specs=[anywhere()] * Y + [full()],
        scratch=[
            VMEM((N, BACK), bf16),
            pltpu.SemaphoreType.DMA((2 * Y,)),
            pltpu.SemaphoreType.DMA((2 * Y,)),
        ],
        limit=16,
        free=(1, 2, 3),
        held=(4, 5),
        near=(Y,),
    )


def chooser(core, wide, run):
    row = lax.broadcasted_iota(jnp.int32, (wide // 2, wide), 0)
    col = lax.broadcasted_iota(jnp.int32, (wide // 2, wide), 1)
    return (col == (row // run) * (2 * run) + core * run + row % run).astype(bf16)


def weights_body(at_ref, mine, other, out_hbm, out, rows_t, hid_t, sem):
    core = at_ref[4]
    pick_row, pick_hid = chooser(core, 512, 64), chooser(core, 128, 16)
    for k, src in enumerate((mine, other)):
        for i in range(Z):
            rows_t[k, i * 256 : (i + 1) * 256, :] = dot_t(pick_row, src[:, i * 512 : (i + 1) * 512]).astype(bf16)
            cols = slice(HID + i * 128, HID + (i + 1) * 128)
            hid_t[k, i * 64 : (i + 1) * 64, :] = dot_t(pick_hid, src[:, cols]).astype(bf16)
    for j in range(4):
        cols = slice(GB + j * STEP, GB + (j + 1) * STEP)
        up = (dot(rows_t[0], mine[:, cols]) + dot(rows_t[1], other[:, cols])).astype(bf16)
        for k in range(Z * X):
            out[k, :64, j * STEP : (j + 1) * STEP] = up[k * 64 : (k + 1) * 64]
    copies = [pltpu.make_async_copy(out.at[:, pl.ds(0, 64)], out_hbm.at[:, pl.ds(0, 64)], sem.at[0])]
    copies[0].start()
    for j in range(8):
        cols = slice(WIDTH + j * STEP, WIDTH + (j + 1) * STEP)
        down = (dot(hid_t[0], mine[:, cols]) + dot(hid_t[1], other[:, cols])).astype(bf16)
        row, col = 64 + 16 * (j // 4), (j % 4) * STEP
        for k in range(Z * X):
            out[k, row : row + 16, col : col + STEP] = down[k * 16 : (k + 1) * 16]
        if j % 4 == 3:
            part = pl.ds(row, 16)
            copies.append(pltpu.make_async_copy(out.at[:, part], out_hbm.at[:, part], sem.at[1 + j // 4]))
            copies[-1].start()
    for copy in copies:
        copy.wait()


def weights(at, mine, other):
    return call(
        weights_body,
        "weights",
        [((Z * X, 96, 1024), bf16)],
        (at, mine, other),
        3 * 2 * N * WIDTH * FF,
        12 << 20,
        in_specs=[scalars(), full(), full()],
        out_specs=[anywhere()],
        scratch=[
            VMEM((Z * X, 96, 1024), bf16),
            VMEM((2, 1024, N), bf16),
            VMEM((2, 256, N), bf16),
            pltpu.SemaphoreType.DMA((3,)),
        ],
        limit=16,
        held=(1, 2),
    )[0]


def gather_sum_body(pieces_ref, up_ref, down_ref):
    for j in range(2):
        at = j * 512
        total = pieces_ref[0, :, at : at + 512].astype(f32)
        for k in range(1, Z * X):
            total = total + pieces_ref[k, :, at : at + 512].astype(f32)
        up_ref[0, :, at : at + 512] = total[:64]
        down_ref[0, :, at : at + 512] = total[64:80]
        down_ref[0, :, 1024 + at : 1024 + at + 512] = total[80:96]


def project_body(*refs):
    own, rest, place_hbm, turned_hbm, gate, cot_hbm, r0, r1, r2, r3, resid_hbm, gates, o0, o1, o2, o3 = refs[:16]
    place, turned, cot, back, w, resid, in_sem, w_sem, out_sem = refs[16:]
    copies = [
        pltpu.make_async_copy(r, back.at[pl.ds(s * CAP, CAP), :], in_sem.at[s]) for s, r in enumerate((r0, r1, r2, r3))
    ]
    copies.append(pltpu.make_async_copy(turned_hbm, turned, in_sem.at[4]))
    late = pltpu.make_async_copy(place_hbm, place, in_sem.at[6])
    copies.append(pltpu.make_async_copy(cot_hbm, cot, in_sem.at[5]))
    slabs = [pltpu.make_async_copy(own, w.at[0], w_sem.at[0])]
    for s in range(1, Y):
        slabs.append(pltpu.make_async_copy(rest.at[:, s - 1], w.at[s].reshape(rest.shape[0], -1, WIDTH), w_sem.at[s]))
    for copy in copies + slabs + [late]:
        copy.start()
    for copy in copies:
        copy.wait()
    wide = 512
    for j in range(WIDTH // wide):
        cols = slice(j * wide, (j + 1) * wide)
        resid[:, cols] = (cot[:, cols].astype(f32) + dot(turned[...], back[:, cols])).astype(bf16)
    sent = [pltpu.make_async_copy(resid, resid_hbm, out_sem)]
    sent[0].start()
    for s, out in enumerate((o0, o1, o2, o3)):
        slabs[s].wait()
        out[...] = dot_t(resid[...], w[s]).astype(bf16)
    late.wait()
    tail = back[:, WIDTH:].astype(f32)
    picked = jnp.sum(place[...].astype(f32) * (tail[:, 0:1] + tail[:, 1:2]), axis=0, keepdims=True)
    gates[...] = (picked / gate[...].astype(f32)).astype(bf16)
    for copy in sent:
        copy.wait()


def project(w_out, rest, place, turned, gate_row, grad_out, backs):
    shapes = [(ROWS, WIDTH), (1, ROWS)] + [(ROWS, 512)] * Y
    ins = (w_out, rest, place, turned, gate_row, grad_out, *backs)
    in_specs, out_specs = [anywhere() for _ in ins], [anywhere() for _ in shapes]
    in_specs[4] = full()
    out_specs[1:] = [full()] * 5
    return call(
        project_body,
        "project",
        [(s, bf16) for s in shapes],
        ins,
        2 * ROWS * WIDTH * WIDTH + 2 * ROWS * N * WIDTH,
        10 << 20,
        in_specs=in_specs,
        out_specs=out_specs,
        scratch=[
            VMEM((N, ROWS), bf16),
            VMEM((ROWS, N), bf16),
            VMEM((ROWS, WIDTH), bf16),
            VMEM((N, BACK), bf16),
            VMEM((Y, 512, WIDTH), bf16),
            VMEM((ROWS, WIDTH), bf16),
            pltpu.SemaphoreType.DMA((7,)),
            pltpu.SemaphoreType.DMA((Y,)),
            pltpu.SemaphoreType.DMA,
        ],
        limit=20,
        near=(2, 3, 4, 5),
    )


def state_body(at_ref, g0, g1, g2, g3, q_ref, grad_ref, keep_ref, send_ref):
    y, block = at_ref[0], at_ref[1]
    ramp = lax.broadcasted_iota(jnp.int32, (ROWS, 1), 0)
    sums = [jnp.zeros((HD, 2 * HD), f32) for _ in range(HEADS)]
    for s, g in enumerate((g0, g1, g2, g3)):
        off = pl.multiple_of(lax.rem(y + s, Y) * ROWS, ROWS)
        inverse = 1.0 / (3 * BLOCKS * TOK + block * TOK + off + ramp + 1).astype(f32)
        grad_ref[pl.ds(off, ROWS), :] = g[...]
        for h in range(HEADS):
            cols = slice(h * HD, (h + 1) * HD)
            both = jnp.concatenate(split(g[:, cols].astype(f32) * inverse), axis=1)
            sums[h] += t_dot(q_ref[pl.ds(off, ROWS), cols], both)
    sums = [total[:, :HD] + total[:, HD:] for total in sums]
    first = at_ref[4] == 0
    for h in range(HEADS // 2):
        rows = slice(h * HD, (h + 1) * HD)
        keep_ref[rows, :] = jnp.where(first, sums[h], sums[h + 2])
        send_ref[rows, :] = jnp.where(first, sums[h + 2], sums[h])


def head_state(at, grads, queries):
    return call(
        state_body,
        "state",
        [((TOK, HEADS * HD), bf16), ((HEADS * HD // 2, HD), f32), ((HEADS * HD // 2, HD), f32)],
        (at, *grads, queries),
        HEADS * 2 * TOK * HD * 2 * HD,
        4 << 20,
        in_specs=[scalars()] + [full()] * 5,
        limit=8,
        held=(1, 2, 3, 4, 5),
        near=(0, 1, 2),
    )


def chip_body(state, other, chip, chip16):
    chip[...] = state[...] + other[...]
    chip16[...] = chip[...].astype(bf16)


def line_body(chip, x1, x2, x3, line16):
    total = chip[...] + x1[...].astype(f32) + x2[...].astype(f32) + x3[...].astype(f32)
    line16[...] = total.astype(bf16)


SUB = 256
PARTS = TOK // SUB
PAIR = 2


def triangle(lower):
    row = lax.broadcasted_iota(jnp.int32, (SUB, SUB), 0)
    col = lax.broadcasted_iota(jnp.int32, (SUB, SUB), 1)
    return (col <= row) if lower else (col >= row)


def query_part(block, h, g_ref, v_ref, k_ref, prior_ref, out_ref):
    mask = triangle(True)
    ramp = lax.broadcasted_iota(jnp.int32, (SUB, 1), 0)
    cols = slice(h * HD, (h + 1) * HD)
    prior = jnp.concatenate(split(prior_ref[h]), axis=0)
    for i in range(PARTS):
        rows, upto = slice(i * SUB, (i + 1) * SUB), (i + 1) * SUB
        g = g_ref[rows, cols]
        mix = dot_t(g, v_ref[:upto, cols])
        edge = jnp.where(mask, mix[:, i * SUB :], 0.0).astype(bf16)
        if i:
            edge = jnp.concatenate([mix[:, : i * SUB].astype(bf16), edge], axis=1)
        before = dot_t(g, prior)
        total = before[:, :HD] + before[:, HD:] + dot(edge, k_ref[:upto, cols])
        count = (3 * BLOCKS * TOK + block * TOK + i * SUB + ramp + 1).astype(f32)
        out_ref[rows, cols] = (total / count).astype(bf16)


def later_part(block, h, a_ref, b_ref, c_ref, out_ref):
    mask = triangle(False)
    ramp = lax.broadcasted_iota(jnp.int32, (1, TOK), 1)
    inverse = 1.0 / (3 * BLOCKS * TOK + block * TOK + ramp + 1).astype(f32)
    cols = slice(h * HD, (h + 1) * HD)
    for i in range(PARTS):
        at = i * SUB
        rows = slice(at, at + SUB)
        mix = dot_t(a_ref[rows, cols], b_ref[at:, cols]) * inverse[:, at:]
        edge = jnp.where(mask, mix[:, :SUB], 0.0).astype(bf16)
        if i < PARTS - 1:
            edge = jnp.concatenate([edge, mix[:, SUB:].astype(bf16)], axis=1)
        out_ref[rows, cols] = dot(edge, c_ref[at:, cols]).astype(bf16)


def query_key_body(at_ref, q_ref, k_ref, v_ref, g_ref, prior_ref, out_ref, key_ref):
    block = at_ref[1]
    for h in range(HEADS):
        query_part(block, h, g_ref, v_ref, k_ref, prior_ref, out_ref)
        later_part(block, h, v_ref, g_ref, q_ref, key_ref)


def value_body(at_ref, q_ref, k_ref, g_ref, value_ref):
    for h in range(HEADS):
        later_part(at_ref[1], h, k_ref, q_ref, g_ref, value_ref)


def head_call(body, name, ins, outs, near):
    return call(
        body,
        name,
        [((TOK, HEADS * HD), bf16)] * outs,
        ins,
        10 * HEADS * 4 * SUB * SUB * HD * outs,
        6 << 20,
        in_specs=[scalars()] + [full()] * (len(ins) - 1),
        limit=16,
        held=range(1, len(ins)),
        near=(near,),
    )


def later_body(spot_ref, keep, other, x1, x2, x3, z1, z2, z3, own, send):
    z, x, core = spot_ref[2], spot_ref[3], spot_ref[4]
    later = jnp.zeros(keep.shape, f32)
    for s, a, b in ((1, x1, z1), (2, x2, z2), (3, x3, z3)):
        later += jnp.where(s > x, a[...].astype(f32), 0.0) + jnp.where(s > z, b[...].astype(f32), 0.0)
    own[...] = later + jnp.where(core == 0, other[...], 0.0)
    send[...] = later + jnp.where(core == 1, keep[...], 0.0)


def final_body(spot_ref, own, got, v_ref, k_ref, key_ref, value_ref, key_hbm, value_hbm, outs, sem):
    core = spot_ref[4]
    copies = []
    for h in range(HEADS):
        rows, cols = slice((h % 2) * HD, (h % 2 + 1) * HD), slice(h * HD, (h + 1) * HD)
        hi, lo = split(jnp.where(core == h // 2, own[rows], got[rows]))
        key = dot_t(v_ref[:, cols], jnp.concatenate([hi, lo], axis=0))
        outs[0, :, cols] = (key_ref[:, cols].astype(f32) + key[:, :HD] + key[:, HD:]).astype(bf16)
        value = dot(k_ref[:, cols], jnp.concatenate([hi, lo], axis=1))
        outs[1, :, cols] = (value_ref[:, cols].astype(f32) + value[:, :HD] + value[:, HD:]).astype(bf16)
        here = pl.ds(h * HD, HD)
        for k, out in enumerate((key_hbm, value_hbm)):
            copy = pltpu.make_async_copy(outs.at[k, :, here], out.at[:, here], sem.at[2 * h + k])
            copy.start()
            copies.append(copy)
    for copy in copies:
        copy.wait()


def final(spot, sums, values, keys, key_here, value_here):
    return call(
        final_body,
        "final",
        [((TOK, HEADS * HD), bf16)] * 2,
        (spot, *sums, values, keys, key_here, value_here),
        HEADS * 8 * TOK * HD * HD,
        8 << 20,
        in_specs=[scalars()] + [full()] * 6,
        out_specs=[anywhere()] * 2,
        scratch=[VMEM((2, TOK, HEADS * HD), bf16), pltpu.SemaphoreType.DMA((2 * HEADS,))],
        limit=12,
        held=range(1, 7),
    )


def index(z, x, c):
    return (z * X + x) * C + c


def spots():
    return [(z, x, c) for z in range(Z) for x in range(X) for c in range(C)]


def along_y(a, s):
    return lax.ppermute(a, "exp", [(i, (i + s) % Y) for i in range(Y)])


def along_x(a, s):
    return lax.ppermute(a, "ctx", [(index(z, x, c), index(z, (x + s) % X, c)) for z, x, c in spots()])


def along_z(a, s):
    return lax.ppermute(a, "ctx", [(index(z, x, c), index((z + s) % Z, x, c)) for z, x, c in spots()])


def across(a):
    return lax.ppermute(a, "ctx", [(i, i ^ 1) for i in range(BLOCKS)])


def on_device(
    attn_query,
    attn_key,
    attn_value,
    prefix_state,
    moe_in,
    grad_out,
    router_gates,
    expert_ids,
    w_gate_up,
    w_down,
    w_out,
):
    y = lax.axis_index("exp")
    block = lax.axis_index("ctx")
    z, x, c = block >> 3, (block >> 1) & 3, block & 1
    at = jnp.stack([y, block, z, x, c]).astype(jnp.int32)

    slab = w_out.shape[0] // BLOCKS
    piece = lax.dynamic_slice_in_dim(w_out, block * slab, slab, 0)
    pieces = jnp.concatenate([along_y(piece, s) for s in (1, 2, 3)], axis=0)
    gate_row = router_gates.reshape(1, ROWS)
    place, turned, *chunks = pack(at, expert_ids.reshape(1, ROWS), gate_row, moe_in, grad_out)
    pieces, chunks[1] = lax.optimization_barrier((pieces, chunks[1]))
    rest = lax.all_gather(pieces[None], "ctx", axis=0, tiled=True)
    rest = rest.reshape(BLOCKS, 3, slab, WIDTH)

    held = [chunks[0]] + [along_y(chunks[s], s) for s in (1, 2, 3)]
    w_pair, chunks[0] = lax.optimization_barrier((w_gate_up, chunks[0]))
    held[0] = chunks[0]
    prior = prefix_state[0]
    w_pair, w_back = fetch(w_pair, w_down)
    queries, keys, values = attn_query, attn_key, attn_value
    b0, b1, b2, b3, bundle = expert(held, w_pair, w_back)
    backs = [b0] + [along_y(b, -s) for s, b in ((1, b1), (2, b2), (3, b3))]
    partial = weights(at, bundle, across(bundle))
    _, backs[2], backs[3] = lax.optimization_barrier((partial, backs[2], backs[3]))
    groups = [[index(i, j, k) for i in range(Z) for j in range(X)] for k in range(C)]
    exchanged = lax.all_to_all(partial, "ctx", 0, 0, axis_index_groups=groups, tiled=True)

    grad_resid, gates_out, *per_head = project(w_out, rest, place, turned, gate_row, grad_out, backs)
    grad_gates = gates_out.reshape(ROWS, 1)
    grads = [per_head[0]] + [along_y(per_head[s], -s) for s in (1, 2, 3)]
    attn_grad, mine, send = head_state(at, grads, queries)

    other = across(send)
    size = (HEADS * HD // 2, HD)
    outs = [(size, f32), (size, bf16)]
    chip, chip16 = call(chip_body, "chip", outs, (mine, other), limit=4, held=(0, 1), near=(0, 1))
    from_x = [along_x(chip16, s) for s in (1, 2, 3)]
    ins = (at, queries, keys, values, attn_grad, prior)
    grad_query, key_here = head_call(query_key_body, "query_key", ins, 2, 1)
    chip, key_here = lax.optimization_barrier((chip, key_here))
    (line16,) = call(line_body, "line", [(size, bf16)], (chip, *from_x), limit=4, held=range(4), near=(0,))
    from_z = [along_z(line16, s) for s in (1, 2, 3)]
    (value_here,) = head_call(value_body, "value", (at, queries, keys, attn_grad), 1, 0)
    value_here, from_z[2] = lax.optimization_barrier((value_here, from_z[2]))
    ins = (at, mine, other, *from_x, *from_z)
    specs = [scalars()] + [full()] * 8
    own, send = call(later_body, "later", [(size, f32)] * 2, ins, in_specs=specs, limit=4, held=range(1, 9), near=(0, 1))
    grad_key, grad_value = final(at, (own, across(send)), values, keys, key_here, value_here)

    exchanged, grad_key = lax.optimization_barrier((exchanged, grad_key))
    outs = [((1, 64, 1024), f32), ((1, 16, WIDTH), f32)]
    grad_gate_up, grad_down = call(gather_sum_body, "gather_sum", outs, (exchanged,), 0, 4 << 20, free=(0,))
    return (grad_query, grad_key, grad_value, grad_resid, grad_gates, grad_gate_up, grad_down)


def solution(mesh):
    whole = P(("ctx", "exp"), None)
    split_cols = P("ctx", "exp")
    return jax.shard_map(
        on_device,
        mesh=mesh,
        in_specs=(
            split_cols,
            split_cols,
            split_cols,
            P("ctx", "exp", None, None),
            whole,
            whole,
            whole,
            whole,
            P("exp", None, None),
            P("exp", None, None),
            P("exp", None),
        ),
        out_specs=(
            split_cols,
            split_cols,
            split_cols,
            whole,
            whole,
            P("exp", "ctx", None),
            P("exp", "ctx", None),
        ),
        check_vma=False,
    )
```

```python
import jax
import jax.numpy as jnp
from jax import lax
from jax.experimental import pallas as pl
from jax.experimental.pallas import tpu as pltpu
from jax.sharding import PartitionSpec as P

bf16 = jnp.bfloat16
f32 = jnp.float32
VMEM = pltpu.VMEM
SMEM = pltpu.SMEM
Z, X, C, Y = 4, 4, 2, 4
CAP, ROWS, WIDTH, FF, HD, HEADS, TOK = 96, 256, 2048, 512, 128, 4, 1024
WEIGHT = 3
EARLY = ("pack", "fetch", "expert", "own_weights", "weights")
BLOCKS = Z * X * C


def dot(a, b):
    return lax.dot_general(a, b, (((1,), (0,)), ((), ())), preferred_element_type=f32)


def dot_t(a, b):
    return lax.dot_general(a, b, (((1,), (1,)), ((), ())), preferred_element_type=f32)


def t_dot(a, b):
    return lax.dot_general(a, b, (((0,), (0,)), ((), ())), preferred_element_type=f32)


def split(a):
    hi = a.astype(bf16)
    return hi, (a - hi.astype(f32)).astype(bf16)


def full():
    return pl.BlockSpec(memory_space=VMEM)


def scalars():
    return pl.BlockSpec(memory_space=SMEM)


def call(body, name, outs, ins, flops=0, moved=0, grid=None, in_specs=None, out_specs=None, limit=24, scratch=(), free=(), near=(), held=()):
    weight = 4 if name in EARLY else WEIGHT
    kwargs = {} if grid is None else {"grid": grid}
    specs = in_specs or [full() for _ in ins]
    ins = [
        a if spec.memory_space is SMEM or i in free else pltpu.with_memory_space_constraint(a, VMEM if i in held else pltpu.HBM)
        for i, (a, spec) in enumerate(zip(ins, specs))
    ]
    return pl.pallas_call(
        body,
        name=name,
        out_shape=[(VMEM if near is True or i in near else pltpu.HBM)(s, t) for i, (s, t) in enumerate(outs)],
        in_specs=specs,
        out_specs=out_specs or [full() for _ in outs],
        scratch_shapes=scratch,
        compiler_params=pltpu.CompilerParams(vmem_limit_bytes=limit << 20),
        cost_estimate=pl.CostEstimate(flops=weight * flops, bytes_accessed=weight * moved, transcendentals=0),
        **kwargs,
    )(*ins)


def pack_body(at_ref, ids_ref, gate_ref, moe_ref, cot_ref, place_ref, turned_ref, c0, c1, c2, c3, gate_col):
    @pl.when(pl.program_id(0) == 0)
    def _():
        rel = ids_ref[...] - at_ref[0]
        rel = jnp.where(rel < 0, rel + Y, rel)
        member = (lax.broadcasted_iota(jnp.int32, (8, ROWS), 0) == rel).astype(f32)
        row = lax.broadcasted_iota(jnp.int32, (ROWS, ROWS), 0)
        col = lax.broadcasted_iota(jnp.int32, (ROWS, ROWS), 1)
        earlier = dot(member.astype(bf16), (row < col).astype(bf16))
        slot = jnp.sum(earlier * member, axis=0, keepdims=True).astype(jnp.int32)
        target = rel * CAP + slot
        places = lax.broadcasted_iota(jnp.int32, (Y * CAP, ROWS), 0)
        place_ref[...] = (places == target).astype(bf16)
        spots_col = jnp.sum(jnp.where(row == col, target.astype(f32), 0.0), axis=1, keepdims=True)
        lanes = lax.broadcasted_iota(jnp.int32, (ROWS, Y * CAP), 1)
        turned_ref[...] = (lanes == spots_col.astype(jnp.int32)).astype(bf16)
        gate = gate_ref[...].astype(f32)
        gate_col[...] = jnp.sum(jnp.where(row == col, gate, 0.0), axis=1, keepdims=True)

    place = place_ref[...]
    scaled = (gate_col[...] * cot_ref[...].astype(f32)).astype(bf16)
    for half, rows in enumerate((moe_ref[...], scaled)):
        part = dot(place, rows).astype(bf16)
        for s, chunk in enumerate((c0, c1, c2, c3)):
            chunk[half] = part[s * CAP : (s + 1) * CAP]


def pack(at, ids, gates, moe_in, grad_out):
    step = 1024
    outs = [((Y * CAP, ROWS), bf16), ((ROWS, Y * CAP), bf16)] + [((2, CAP, WIDTH), bf16)] * Y
    ins = (at, ids, gates, moe_in, grad_out)
    row = pl.BlockSpec((1, ROWS), lambda j: (0, 0))
    tile = pl.BlockSpec((ROWS, step), lambda j: (0, j))
    return call(
        pack_body,
        "pack",
        outs,
        ins,
        2 * 384 * 256 * 4096,
        5 << 20,
        grid=(WIDTH // step,),
        in_specs=[scalars(), row, row, tile, tile],
        out_specs=[pl.BlockSpec((Y * CAP, ROWS), lambda j: (0, 0)), pl.BlockSpec((ROWS, Y * CAP), lambda j: (0, 0))]
        + [pl.BlockSpec((2, CAP, step), lambda j: (0, 0, j))] * Y,
        scratch=[VMEM((ROWS, 1), f32)],
        limit=16,
    )


BACK = WIDTH + 128
N = Y * CAP
BUNDLE = 2 * WIDTH + 3 * FF
GB, HID = 2 * WIDTH, 2 * WIDTH + 2 * FF
STEP = 256


def expert_body(r0, r1, r2, r3, wp, wb, b0, b1, b2, b3, held, back, in_sem, out_sem):
    arrived = (r0, r1, r2, r3)
    backs = (b0, b1, b2, b3)
    tiles = FF // STEP

    def incoming(half, s):
        dst = held.at[pl.ds(s * CAP, CAP), pl.ds(half * WIDTH, WIDTH)]
        return pltpu.make_async_copy(arrived[s].at[half], dst, in_sem.at[half * Y + s])

    for s in range(Y):
        incoming(0, s).start()
    for s in range(Y):
        incoming(1, s).start()
    for s in range(Y):
        incoming(0, s).wait()
    total = jnp.zeros((N, 1), f32)
    for j in range(tiles):
        at, up = j * STEP, FF + j * STEP
        first = dot(held[:, :WIDTH], wp[0, :, at : at + STEP])
        second = dot(held[:, :WIDTH], wp[0, :, up : up + STEP])
        if j == 0:
            for s in range(Y):
                incoming(1, s).wait()
        grad_hidden = dot_t(held[:, WIDTH:GB], wb[0, at : at + STEP, :])
        s = 1.0 / (1.0 + jnp.exp(-first))
        silu = first * s
        hidden = (silu * second).astype(bf16)
        held[:, HID + at : HID + at + STEP] = hidden
        total += jnp.sum(hidden.astype(f32) * grad_hidden, axis=1, keepdims=True)
        slope = s * (1.0 + first * (1.0 - s))
        held[:, GB + at : GB + at + STEP] = (grad_hidden * second * slope).astype(bf16)
        held[:, GB + up : GB + up + STEP] = (grad_hidden * silu).astype(bf16)
    hi, lo = split(total)
    lane = lax.broadcasted_iota(jnp.int32, (N, 128), 1)
    back[:, WIDTH:] = jnp.where(lane == 0, hi.astype(f32), lo.astype(f32)).astype(bf16)
    outgoing = []
    bounds = (0, WIDTH // 2, BACK)
    for part in range(2):
        lo_col, hi_col = bounds[part], bounds[part + 1]
        for at in range(lo_col, min(hi_col, WIDTH), STEP):
            back[:, at : at + STEP] = dot_t(held[:, GB:HID], wp[0, at : at + STEP, :]).astype(bf16)
        cols = pl.ds(lo_col, hi_col - lo_col)
        for s in range(Y):
            src = back.at[pl.ds(s * CAP, CAP), cols]
            copy = pltpu.make_async_copy(src, backs[s].at[:, cols], out_sem.at[part * Y + s])
            copy.start()
            outgoing.append(copy)
    for copy in outgoing:
        copy.wait()


def anywhere():
    return pl.BlockSpec(memory_space=pl.ANY)


def fetch_body(*refs):
    half = len(refs) // 2
    sem = refs[-1]
    copies = [pltpu.make_async_copy(refs[i], refs[half + i], sem.at[i]) for i in range(half)]
    for copy in copies:
        copy.start()
    for copy in copies:
        copy.wait()


def fetch(*arrays):
    return call(
        fetch_body,
        "fetch",
        [(a.shape, a.dtype) for a in arrays],
        arrays,
        0,
        12 << 20,
        in_specs=[anywhere() for _ in arrays],
        scratch=[pltpu.SemaphoreType.DMA((len(arrays),))],
        limit=2,
        near=True,
    )


def expert(chunks, w_pair, w_back):
    outs = [((CAP, BACK), bf16)] * Y + [((N, BUNDLE), bf16)]
    ins = (*chunks, w_pair, w_back)
    return call(
        expert_body,
        "expert",
        outs,
        ins,
        5 * 2 * N * WIDTH * FF,
        14 << 20,
        in_specs=[anywhere() for _ in chunks] + [full(), full()],
        out_specs=[anywhere()] * Y + [full()],
        scratch=[
            VMEM((N, BACK), bf16),
            pltpu.SemaphoreType.DMA((2 * Y,)),
            pltpu.SemaphoreType.DMA((2 * Y,)),
        ],
        limit=16,
        free=(1, 2, 3),
        held=(4, 5),
        near=(Y,),
    )


def chooser(core, wide, run):
    row = lax.broadcasted_iota(jnp.int32, (wide // 2, wide), 0)
    col = lax.broadcasted_iota(jnp.int32, (wide // 2, wide), 1)
    return (col == (row // run) * (2 * run) + core * run + row % run).astype(bf16)


def turn(core, src, rows_t, hid_t):
    pick_row, pick_hid = chooser(core, 512, 64), chooser(core, 128, 16)
    for i in range(Z):
        rows_t[i * 256 : (i + 1) * 256, :] = dot_t(pick_row, src[:, i * 512 : (i + 1) * 512]).astype(bf16)
        cols = slice(HID + i * 128, HID + (i + 1) * 128)
        hid_t[i * 64 : (i + 1) * 64, :] = dot_t(pick_hid, src[:, cols]).astype(bf16)


def own_weights_body(at_ref, mine, up_ref, down_ref, rows_t, hid_t):
    turn(at_ref[4], mine, rows_t, hid_t)
    for j in range(4):
        up_ref[:, j * STEP : (j + 1) * STEP] = dot(rows_t[...], mine[:, GB + j * STEP : GB + (j + 1) * STEP])
    for j in range(8):
        at = WIDTH + j * STEP
        down_ref[:, j * STEP : (j + 1) * STEP] = dot(hid_t[...], mine[:, at : at + STEP])


def own_weights(at, mine):
    return call(
        own_weights_body,
        "own_weights",
        [((1024, 1024), f32), ((256, WIDTH), f32)],
        (at, mine),
        3 * N * WIDTH * FF,
        10 << 20,
        in_specs=[scalars(), full()],
        scratch=[VMEM((1024, N), bf16), VMEM((256, N), bf16)],
        limit=8,
        held=(1,),
        near=(0, 1),
    )


def weights_body(at_ref, up_ref, down_ref, other, out_hbm, out, rows_t, hid_t, sem):
    turn(at_ref[4], other, rows_t, hid_t)
    for j in range(4):
        here = slice(j * STEP, (j + 1) * STEP)
        up = (up_ref[:, here] + dot(rows_t[...], other[:, GB + j * STEP : GB + (j + 1) * STEP])).astype(bf16)
        for k in range(Z * X):
            out[k, :64, here] = up[k * 64 : (k + 1) * 64]
    copies = [pltpu.make_async_copy(out.at[:, pl.ds(0, 64)], out_hbm.at[:, pl.ds(0, 64)], sem.at[0])]
    copies[0].start()
    for j in range(8):
        here, at = slice(j * STEP, (j + 1) * STEP), WIDTH + j * STEP
        down = (down_ref[:, here] + dot(hid_t[...], other[:, at : at + STEP])).astype(bf16)
        row, col = 64 + 16 * (j // 4), (j % 4) * STEP
        for k in range(Z * X):
            out[k, row : row + 16, col : col + STEP] = down[k * 16 : (k + 1) * 16]
        if j % 4 == 3:
            part = pl.ds(row, 16)
            copies.append(pltpu.make_async_copy(out.at[:, part], out_hbm.at[:, part], sem.at[1 + j // 4]))
            copies[-1].start()
    for copy in copies:
        copy.wait()


def weights(at, own, other):
    return call(
        weights_body,
        "weights",
        [((Z * X, 96, 1024), bf16)],
        (at, *own, other),
        3 * N * WIDTH * FF,
        10 << 20,
        in_specs=[scalars(), full(), full(), full()],
        out_specs=[anywhere()],
        scratch=[
            VMEM((Z * X, 96, 1024), bf16),
            VMEM((1024, N), bf16),
            VMEM((256, N), bf16),
            pltpu.SemaphoreType.DMA((3,)),
        ],
        limit=12,
        held=(1, 2, 3),
    )[0]


def gather_sum_body(pieces_ref, up_ref, down_ref):
    for j in range(2):
        at = j * 512
        total = pieces_ref[0, :, at : at + 512].astype(f32)
        for k in range(1, Z * X):
            total = total + pieces_ref[k, :, at : at + 512].astype(f32)
        up_ref[0, :, at : at + 512] = total[:64]
        down_ref[0, :, at : at + 512] = total[64:80]
        down_ref[0, :, 1024 + at : 1024 + at + 512] = total[80:96]


def project_body(*refs):
    own, rest, place_hbm, turned_hbm, gate, cot_hbm, r0, r1, r2, r3, resid_hbm, gates, o0, o1, o2, o3 = refs[:16]
    place, turned, cot, back, w, resid, in_sem, w_sem, out_sem = refs[16:]
    copies = [
        pltpu.make_async_copy(r, back.at[pl.ds(s * CAP, CAP), :], in_sem.at[s]) for s, r in enumerate((r0, r1, r2, r3))
    ]
    copies.append(pltpu.make_async_copy(turned_hbm, turned, in_sem.at[4]))
    late = pltpu.make_async_copy(place_hbm, place, in_sem.at[6])
    copies.append(pltpu.make_async_copy(cot_hbm, cot, in_sem.at[5]))
    slabs = [pltpu.make_async_copy(own, w.at[0], w_sem.at[0])]
    for s in range(1, Y):
        slabs.append(pltpu.make_async_copy(rest.at[:, s - 1], w.at[s].reshape(rest.shape[0], -1, WIDTH), w_sem.at[s]))
    for copy in copies + slabs + [late]:
        copy.start()
    for copy in copies:
        copy.wait()
    wide = 512
    for j in range(WIDTH // wide):
        cols = slice(j * wide, (j + 1) * wide)
        resid[:, cols] = (cot[:, cols].astype(f32) + dot(turned[...], back[:, cols])).astype(bf16)
    sent = [pltpu.make_async_copy(resid, resid_hbm, out_sem)]
    sent[0].start()
    for s, out in enumerate((o0, o1, o2, o3)):
        slabs[s].wait()
        out[...] = dot_t(resid[...], w[s]).astype(bf16)
    late.wait()
    tail = back[:, WIDTH:].astype(f32)
    picked = jnp.sum(place[...].astype(f32) * (tail[:, 0:1] + tail[:, 1:2]), axis=0, keepdims=True)
    gates[...] = (picked / gate[...].astype(f32)).astype(bf16)
    for copy in sent:
        copy.wait()


def project(w_out, rest, place, turned, gate_row, grad_out, backs):
    shapes = [(ROWS, WIDTH), (1, ROWS)] + [(ROWS, 512)] * Y
    ins = (w_out, rest, place, turned, gate_row, grad_out, *backs)
    in_specs, out_specs = [anywhere() for _ in ins], [anywhere() for _ in shapes]
    in_specs[4] = full()
    out_specs[1:] = [full()] * 5
    return call(
        project_body,
        "project",
        [(s, bf16) for s in shapes],
        ins,
        2 * ROWS * WIDTH * WIDTH + 2 * ROWS * N * WIDTH,
        10 << 20,
        in_specs=in_specs,
        out_specs=out_specs,
        scratch=[
            VMEM((N, ROWS), bf16),
            VMEM((ROWS, N), bf16),
            VMEM((ROWS, WIDTH), bf16),
            VMEM((N, BACK), bf16),
            VMEM((Y, 512, WIDTH), bf16),
            VMEM((ROWS, WIDTH), bf16),
            pltpu.SemaphoreType.DMA((7,)),
            pltpu.SemaphoreType.DMA((Y,)),
            pltpu.SemaphoreType.DMA,
        ],
        limit=20,
        near=(2, 3, 4, 5),
    )


def state_body(at_ref, g0, g1, g2, g3, q_ref, grad_ref, state_ref):
    y, block = at_ref[0], at_ref[1]
    ramp = lax.broadcasted_iota(jnp.int32, (ROWS, 1), 0)
    sums = [jnp.zeros((HD, 2 * HD), f32) for _ in range(HEADS)]
    for s, g in enumerate((g0, g1, g2, g3)):
        off = pl.multiple_of(lax.rem(y + s, Y) * ROWS, ROWS)
        inverse = 1.0 / (3 * BLOCKS * TOK + block * TOK + off + ramp + 1).astype(f32)
        grad_ref[pl.ds(off, ROWS), :] = g[...]
        for h in range(HEADS):
            cols = slice(h * HD, (h + 1) * HD)
            both = jnp.concatenate(split(g[:, cols].astype(f32) * inverse), axis=1)
            sums[h] += t_dot(q_ref[pl.ds(off, ROWS), cols], both)
    for h in range(HEADS):
        state_ref[h * HD : (h + 1) * HD, :] = sums[h][:, :HD] + sums[h][:, HD:]


def head_state(at, grads, queries):
    return call(
        state_body,
        "state",
        [((TOK, HEADS * HD), bf16), ((HEADS * HD, HD), f32)],
        (at, *grads, queries),
        HEADS * 2 * TOK * HD * 2 * HD,
        4 << 20,
        in_specs=[scalars()] + [full()] * 5,
        limit=8,
        held=(1, 2, 3, 4, 5),
        near=(0, 1),
    )


def chip_body(state, other, chip, chip16):
    chip[...] = state[...] + other[...]
    chip16[...] = chip[...].astype(bf16)


def line_body(chip, x1, x2, x3, line16):
    total = chip[...] + x1[...].astype(f32) + x2[...].astype(f32) + x3[...].astype(f32)
    line16[...] = total.astype(bf16)


SUB = 256
PARTS = TOK // SUB
PAIR = 2


def triangle(lower):
    row = lax.broadcasted_iota(jnp.int32, (SUB, SUB), 0)
    col = lax.broadcasted_iota(jnp.int32, (SUB, SUB), 1)
    return (col <= row) if lower else (col >= row)


def query_part(block, h, g_ref, v_ref, k_ref, prior_ref, out_ref):
    mask = triangle(True)
    ramp = lax.broadcasted_iota(jnp.int32, (SUB, 1), 0)
    cols = slice(h * HD, (h + 1) * HD)
    prior = jnp.concatenate(split(prior_ref[h]), axis=0)
    for i in range(PARTS):
        rows, upto = slice(i * SUB, (i + 1) * SUB), (i + 1) * SUB
        g = g_ref[rows, cols]
        mix = dot_t(g, v_ref[:upto, cols])
        edge = jnp.where(mask, mix[:, i * SUB :], 0.0).astype(bf16)
        if i:
            edge = jnp.concatenate([mix[:, : i * SUB].astype(bf16), edge], axis=1)
        before = dot_t(g, prior)
        total = before[:, :HD] + before[:, HD:] + dot(edge, k_ref[:upto, cols])
        count = (3 * BLOCKS * TOK + block * TOK + i * SUB + ramp + 1).astype(f32)
        out_ref[rows, cols] = (total / count).astype(bf16)


def later_part(block, h, a_ref, b_ref, c_ref, out_ref):
    mask = triangle(False)
    ramp = lax.broadcasted_iota(jnp.int32, (1, TOK), 1)
    inverse = 1.0 / (3 * BLOCKS * TOK + block * TOK + ramp + 1).astype(f32)
    cols = slice(h * HD, (h + 1) * HD)
    for i in range(PARTS):
        at = i * SUB
        rows = slice(at, at + SUB)
        mix = dot_t(a_ref[rows, cols], b_ref[at:, cols]) * inverse[:, at:]
        edge = jnp.where(mask, mix[:, :SUB], 0.0).astype(bf16)
        if i < PARTS - 1:
            edge = jnp.concatenate([edge, mix[:, SUB:].astype(bf16)], axis=1)
        out_ref[rows, cols] = dot(edge, c_ref[at:, cols]).astype(bf16)


def query_key_body(at_ref, q_ref, k_ref, v_ref, g_ref, prior_ref, out_ref, key_ref):
    block = at_ref[1]
    for h in range(HEADS):
        query_part(block, h, g_ref, v_ref, k_ref, prior_ref, out_ref)
        later_part(block, h, v_ref, g_ref, q_ref, key_ref)


def value_body(at_ref, q_ref, k_ref, g_ref, value_ref):
    for h in range(HEADS):
        later_part(at_ref[1], h, k_ref, q_ref, g_ref, value_ref)


def head_call(body, name, ins, outs, near):
    return call(
        body,
        name,
        [((TOK, HEADS * HD), bf16)] * outs,
        ins,
        10 * HEADS * 4 * SUB * SUB * HD * outs,
        6 << 20,
        in_specs=[scalars()] + [full()] * (len(ins) - 1),
        limit=16,
        held=range(1, len(ins)),
        near=(near,),
    )


def final_body(spot_ref, other, x1, x2, x3, z1, z2, z3, v_ref, k_ref, key_ref, value_ref, key_hbm, value_hbm, outs, sem):
    z, x, core = spot_ref[2], spot_ref[3], spot_ref[4]
    copies = []
    for h in range(HEADS):
        rows, cols = slice(h * HD, (h + 1) * HD), slice(h * HD, (h + 1) * HD)
        later = jnp.where(core == 0, other[rows], 0.0)
        for s, a, b in ((1, x1, z1), (2, x2, z2), (3, x3, z3)):
            later += jnp.where(s > x, a[rows].astype(f32), 0.0) + jnp.where(s > z, b[rows].astype(f32), 0.0)
        hi, lo = split(later)
        key = dot_t(v_ref[:, cols], jnp.concatenate([hi, lo], axis=0))
        outs[0, :, cols] = (key_ref[:, cols].astype(f32) + key[:, :HD] + key[:, HD:]).astype(bf16)
        value = dot(k_ref[:, cols], jnp.concatenate([hi, lo], axis=1))
        outs[1, :, cols] = (value_ref[:, cols].astype(f32) + value[:, :HD] + value[:, HD:]).astype(bf16)
        here = pl.ds(h * HD, HD)
        for k, out in enumerate((key_hbm, value_hbm)):
            copy = pltpu.make_async_copy(outs.at[k, :, here], out.at[:, here], sem.at[2 * h + k])
            copy.start()
            copies.append(copy)
    for copy in copies:
        copy.wait()


def final(spot, sums, values, keys, key_here, value_here):
    return call(
        final_body,
        "final",
        [((TOK, HEADS * HD), bf16)] * 2,
        (spot, *sums, values, keys, key_here, value_here),
        HEADS * 8 * TOK * HD * HD,
        8 << 20,
        in_specs=[scalars()] + [full()] * 11,
        out_specs=[anywhere()] * 2,
        scratch=[VMEM((2, TOK, HEADS * HD), bf16), pltpu.SemaphoreType.DMA((2 * HEADS,))],
        limit=12,
        held=range(1, 12),
    )


def index(z, x, c):
    return (z * X + x) * C + c


def spots():
    return [(z, x, c) for z in range(Z) for x in range(X) for c in range(C)]


def along_y(a, s):
    return lax.ppermute(a, "exp", [(i, (i + s) % Y) for i in range(Y)])


def along_x(a, s):
    return lax.ppermute(a, "ctx", [(index(z, x, c), index(z, (x + s) % X, c)) for z, x, c in spots()])


def along_z(a, s):
    return lax.ppermute(a, "ctx", [(index(z, x, c), index((z + s) % Z, x, c)) for z, x, c in spots()])


def across(a):
    return lax.ppermute(a, "ctx", [(i, i ^ 1) for i in range(BLOCKS)])


def on_device(
    attn_query,
    attn_key,
    attn_value,
    prefix_state,
    moe_in,
    grad_out,
    router_gates,
    expert_ids,
    w_gate_up,
    w_down,
    w_out,
):
    y = lax.axis_index("exp")
    block = lax.axis_index("ctx")
    z, x, c = block >> 3, (block >> 1) & 3, block & 1
    at = jnp.stack([y, block, z, x, c]).astype(jnp.int32)

    slab = w_out.shape[0] // BLOCKS
    piece = lax.dynamic_slice_in_dim(w_out, block * slab, slab, 0)
    pieces = jnp.concatenate([along_y(piece, s) for s in (1, 2, 3)], axis=0)
    gate_row = router_gates.reshape(1, ROWS)
    place, turned, *chunks = pack(at, expert_ids.reshape(1, ROWS), gate_row, moe_in, grad_out)
    pieces, chunks[1] = lax.optimization_barrier((pieces, chunks[1]))
    rest = lax.all_gather(pieces[None], "ctx", axis=0, tiled=True)
    rest = rest.reshape(BLOCKS, 3, slab, WIDTH)

    held = [chunks[0]] + [along_y(chunks[s], s) for s in (1, 2, 3)]
    w_pair, chunks[0] = lax.optimization_barrier((w_gate_up, chunks[0]))
    held[0] = chunks[0]
    prior = prefix_state[0]
    w_pair, w_back = fetch(w_pair, w_down)
    queries, keys, values = attn_query, attn_key, attn_value
    b0, b1, b2, b3, bundle = expert(held, w_pair, w_back)
    backs = [b0] + [along_y(b, -s) for s, b in ((1, b1), (2, b2), (3, b3))]
    partial = weights(at, own_weights(at, bundle), across(bundle))
    _, backs[2], backs[3] = lax.optimization_barrier((partial, backs[2], backs[3]))
    groups = [[index(i, j, k) for i in range(Z) for j in range(X)] for k in range(C)]
    exchanged = lax.all_to_all(partial, "ctx", 0, 0, axis_index_groups=groups, tiled=True)

    grad_resid, gates_out, *per_head = project(w_out, rest, place, turned, gate_row, grad_out, backs)
    grad_gates = gates_out.reshape(ROWS, 1)
    grads = [per_head[0]] + [along_y(per_head[s], -s) for s in (1, 2, 3)]
    attn_grad, state = head_state(at, grads, queries)

    other = across(state)
    size = (HEADS * HD, HD)
    outs = [(size, f32), (size, bf16)]
    chip, chip16 = call(chip_body, "chip", outs, (state, other), limit=4, held=(0, 1), near=(0, 1))
    from_x = [along_x(chip16, s) for s in (1, 2, 3)]
    ins = (at, queries, keys, values, attn_grad, prior)
    grad_query, key_here = head_call(query_key_body, "query_key", ins, 2, 1)
    chip, key_here = lax.optimization_barrier((chip, key_here))
    (line16,) = call(line_body, "line", [(size, bf16)], (chip, *from_x), limit=4, held=range(4), near=(0,))
    from_z = [along_z(line16, s) for s in (1, 2, 3)]
    (value_here,) = head_call(value_body, "value", (at, queries, keys, attn_grad), 1, 0)
    sums = (other, *from_x, *from_z)
    grad_key, grad_value = final(at, sums, values, keys, key_here, value_here)

    exchanged, grad_key = lax.optimization_barrier((exchanged, grad_key))
    outs = [((1, 64, 1024), f32), ((1, 16, WIDTH), f32)]
    grad_gate_up, grad_down = call(gather_sum_body, "gather_sum", outs, (exchanged,), 0, 4 << 20, free=(0,))
    return (grad_query, grad_key, grad_value, grad_resid, grad_gates, grad_gate_up, grad_down)


def solution(mesh):
    whole = P(("ctx", "exp"), None)
    split_cols = P("ctx", "exp")
    return jax.shard_map(
        on_device,
        mesh=mesh,
        in_specs=(
            split_cols,
            split_cols,
            split_cols,
            P("ctx", "exp", None, None),
            whole,
            whole,
            whole,
            whole,
            P("exp", None, None),
            P("exp", None, None),
            P("exp", None),
        ),
        out_specs=(
            split_cols,
            split_cols,
            split_cols,
            whole,
            whole,
            P("exp", "ctx", None),
            P("exp", "ctx", None),
        ),
        check_vma=False,
    )
```

```python
import jax
import jax.numpy as jnp
from jax import lax
from jax.experimental import pallas as pl
from jax.experimental.pallas import tpu as pltpu
from jax.sharding import PartitionSpec as P

bf16 = jnp.bfloat16
f32 = jnp.float32
VMEM = pltpu.VMEM
SMEM = pltpu.SMEM
Z, X, C, Y = 4, 4, 2, 4
CAP, ROWS, WIDTH, FF, HD, HEADS, TOK = 96, 256, 2048, 512, 128, 4, 1024
WEIGHT = 3
EARLY = ("pack", "fetch", "expert", "own_weights", "weights")
BLOCKS = Z * X * C


def dot(a, b):
    return lax.dot_general(a, b, (((1,), (0,)), ((), ())), preferred_element_type=f32)


def dot_t(a, b):
    return lax.dot_general(a, b, (((1,), (1,)), ((), ())), preferred_element_type=f32)


def t_dot(a, b):
    return lax.dot_general(a, b, (((0,), (0,)), ((), ())), preferred_element_type=f32)


def split(a):
    hi = a.astype(bf16)
    return hi, (a - hi.astype(f32)).astype(bf16)


def full():
    return pl.BlockSpec(memory_space=VMEM)


def scalars():
    return pl.BlockSpec(memory_space=SMEM)


def call(body, name, outs, ins, flops=0, moved=0, grid=None, in_specs=None, out_specs=None, limit=24, scratch=(), free=(), near=(), held=()):
    weight = 4 if name in EARLY else WEIGHT
    kwargs = {} if grid is None else {"grid": grid}
    specs = in_specs or [full() for _ in ins]
    ins = [
        a if spec.memory_space is SMEM or i in free else pltpu.with_memory_space_constraint(a, VMEM if i in held else pltpu.HBM)
        for i, (a, spec) in enumerate(zip(ins, specs))
    ]
    return pl.pallas_call(
        body,
        name=name,
        out_shape=[(VMEM if near is True or i in near else pltpu.HBM)(s, t) for i, (s, t) in enumerate(outs)],
        in_specs=specs,
        out_specs=out_specs or [full() for _ in outs],
        scratch_shapes=scratch,
        compiler_params=pltpu.CompilerParams(vmem_limit_bytes=limit << 20),
        cost_estimate=pl.CostEstimate(flops=weight * flops, bytes_accessed=weight * moved, transcendentals=0),
        **kwargs,
    )(*ins)


def pack_body(at_ref, ids_ref, gate_ref, moe_hbm, cot_hbm, place_ref, turned_ref, c0, c1, c2, c3, moe, cot, sem):
    half = WIDTH // 2
    copies = []
    for k in range(2):
        cols = pl.ds(k * half, half)
        copies.append(pltpu.make_async_copy(moe_hbm.at[:, cols], moe.at[:, cols], sem.at[k]))
        copies.append(pltpu.make_async_copy(cot_hbm.at[:, cols], cot.at[:, cols], sem.at[2 + k]))
    for copy in copies:
        copy.start()
    rel = ids_ref[...] - at_ref[0]
    rel = jnp.where(rel < 0, rel + Y, rel)
    member = (lax.broadcasted_iota(jnp.int32, (8, ROWS), 0) == rel).astype(f32)
    row = lax.broadcasted_iota(jnp.int32, (ROWS, ROWS), 0)
    col = lax.broadcasted_iota(jnp.int32, (ROWS, ROWS), 1)
    earlier = dot(member.astype(bf16), (row < col).astype(bf16))
    slot = jnp.sum(earlier * member, axis=0, keepdims=True).astype(jnp.int32)
    target = rel * CAP + slot
    places = lax.broadcasted_iota(jnp.int32, (Y * CAP, ROWS), 0)
    place_ref[...] = (places == target).astype(bf16)
    spots_col = jnp.sum(jnp.where(row == col, target.astype(f32), 0.0), axis=1, keepdims=True)
    lanes = lax.broadcasted_iota(jnp.int32, (ROWS, Y * CAP), 1)
    turned_ref[...] = (lanes == spots_col.astype(jnp.int32)).astype(bf16)
    gate = gate_ref[...].astype(f32)
    gate_col = jnp.sum(jnp.where(row == col, gate, 0.0), axis=1, keepdims=True)
    step = 512
    for j in range(WIDTH // step):
        cols = slice(j * step, (j + 1) * step)
        if j % 2 == 0:
            copies[j].wait()
            copies[j + 1].wait()
        scaled = (gate_col * cot[:, cols].astype(f32)).astype(bf16)
        for part, rows in enumerate((moe[:, cols], scaled)):
            packed = dot(place_ref[...], rows).astype(bf16)
            for s, chunk in enumerate((c0, c1, c2, c3)):
                chunk[part, :, cols] = packed[s * CAP : (s + 1) * CAP]


def pack(at, ids, gates, moe_in, grad_out):
    outs = [((Y * CAP, ROWS), bf16), ((ROWS, Y * CAP), bf16)] + [((2, CAP, WIDTH), bf16)] * Y
    return call(
        pack_body,
        "pack",
        outs,
        (at, ids, gates, moe_in, grad_out),
        2 * 384 * 256 * 4096,
        5 << 20,
        in_specs=[scalars(), full(), full(), anywhere(), anywhere()],
        scratch=[VMEM((ROWS, WIDTH), bf16), VMEM((ROWS, WIDTH), bf16), pltpu.SemaphoreType.DMA((4,))],
        limit=10,
        near=(3, 4, 5),
    )


def join_body(a, b, c, out):
    rows = a.shape[0]
    for k, ref in enumerate((a, b, c)):
        out[k * rows : (k + 1) * rows, :] = ref[...]


BACK = WIDTH + 128
N = Y * CAP
BUNDLE = 2 * WIDTH + 3 * FF
GB, HID = 2 * WIDTH, 2 * WIDTH + 2 * FF
STEP = 256


def expert_body(r0, r1, r2, r3, wp, wb, b0, b1, b2, b3, held, back, in_sem, out_sem):
    arrived = (r0, r1, r2, r3)
    backs = (b0, b1, b2, b3)
    tiles = FF // STEP

    def incoming(half, s):
        dst = held.at[pl.ds(s * CAP, CAP), pl.ds(half * WIDTH, WIDTH)]
        return pltpu.make_async_copy(arrived[s].at[half], dst, in_sem.at[half * Y + s])

    for s in range(Y):
        incoming(0, s).start()
    for s in range(Y):
        incoming(1, s).start()
    for s in range(Y):
        incoming(0, s).wait()
    total = jnp.zeros((N, 1), f32)
    for j in range(tiles):
        at, up = j * STEP, FF + j * STEP
        first = dot(held[:, :WIDTH], wp[0, :, at : at + STEP])
        second = dot(held[:, :WIDTH], wp[0, :, up : up + STEP])
        if j == 0:
            for s in range(Y):
                incoming(1, s).wait()
        grad_hidden = dot_t(held[:, WIDTH:GB], wb[0, at : at + STEP, :])
        s = 1.0 / (1.0 + jnp.exp(-first))
        silu = first * s
        hidden = (silu * second).astype(bf16)
        held[:, HID + at : HID + at + STEP] = hidden
        total += jnp.sum(hidden.astype(f32) * grad_hidden, axis=1, keepdims=True)
        slope = s * (1.0 + first * (1.0 - s))
        held[:, GB + at : GB + at + STEP] = (grad_hidden * second * slope).astype(bf16)
        held[:, GB + up : GB + up + STEP] = (grad_hidden * silu).astype(bf16)
    hi, lo = split(total)
    lane = lax.broadcasted_iota(jnp.int32, (N, 128), 1)
    back[:, WIDTH:] = jnp.where(lane == 0, hi.astype(f32), lo.astype(f32)).astype(bf16)
    outgoing = []
    bounds = (0, WIDTH // 2, BACK)
    for part in range(2):
        lo_col, hi_col = bounds[part], bounds[part + 1]
        for at in range(lo_col, min(hi_col, WIDTH), STEP):
            back[:, at : at + STEP] = dot_t(held[:, GB:HID], wp[0, at : at + STEP, :]).astype(bf16)
        cols = pl.ds(lo_col, hi_col - lo_col)
        for s in range(Y):
            src = back.at[pl.ds(s * CAP, CAP), cols]
            copy = pltpu.make_async_copy(src, backs[s].at[:, cols], out_sem.at[part * Y + s])
            copy.start()
            outgoing.append(copy)
    for copy in outgoing:
        copy.wait()


def anywhere():
    return pl.BlockSpec(memory_space=pl.ANY)


def fetch_body(*refs):
    half = len(refs) // 2
    sem = refs[-1]
    copies = [pltpu.make_async_copy(refs[i], refs[half + i], sem.at[i]) for i in range(half)]
    for copy in copies:
        copy.start()
    for copy in copies:
        copy.wait()


def fetch(*arrays):
    return call(
        fetch_body,
        "fetch",
        [(a.shape, a.dtype) for a in arrays],
        arrays,
        0,
        12 << 20,
        in_specs=[anywhere() for _ in arrays],
        scratch=[pltpu.SemaphoreType.DMA((len(arrays),))],
        limit=2,
        near=True,
    )


def expert(chunks, w_pair, w_back):
    outs = [((CAP, BACK), bf16)] * Y + [((N, BUNDLE), bf16)]
    ins = (*chunks, w_pair, w_back)
    return call(
        expert_body,
        "expert",
        outs,
        ins,
        5 * 2 * N * WIDTH * FF,
        14 << 20,
        in_specs=[anywhere() for _ in chunks] + [full(), full()],
        out_specs=[anywhere()] * Y + [full()],
        scratch=[
            VMEM((N, BACK), bf16),
            pltpu.SemaphoreType.DMA((2 * Y,)),
            pltpu.SemaphoreType.DMA((2 * Y,)),
        ],
        limit=16,
        free=(1, 2, 3),
        held=(4, 5),
        near=(Y,),
    )


def chooser(core, wide, run):
    row = lax.broadcasted_iota(jnp.int32, (wide // 2, wide), 0)
    col = lax.broadcasted_iota(jnp.int32, (wide // 2, wide), 1)
    return (col == (row // run) * (2 * run) + core * run + row % run).astype(bf16)


def turn(core, src, rows_t, hid_t):
    pick_row, pick_hid = chooser(core, 512, 64), chooser(core, 128, 16)
    for i in range(Z):
        rows_t[i * 256 : (i + 1) * 256, :] = dot_t(pick_row, src[:, i * 512 : (i + 1) * 512]).astype(bf16)
        cols = slice(HID + i * 128, HID + (i + 1) * 128)
        hid_t[i * 64 : (i + 1) * 64, :] = dot_t(pick_hid, src[:, cols]).astype(bf16)


def own_weights_body(at_ref, mine, up_ref, down_ref, rows_t, hid_t):
    turn(at_ref[4], mine, rows_t, hid_t)
    for j in range(4):
        up_ref[:, j * STEP : (j + 1) * STEP] = dot(rows_t[...], mine[:, GB + j * STEP : GB + (j + 1) * STEP])
    for j in range(8):
        at = WIDTH + j * STEP
        down_ref[:, j * STEP : (j + 1) * STEP] = dot(hid_t[...], mine[:, at : at + STEP])


def own_weights(at, mine):
    return call(
        own_weights_body,
        "own_weights",
        [((1024, 1024), f32), ((256, WIDTH), f32)],
        (at, mine),
        3 * N * WIDTH * FF,
        10 << 20,
        in_specs=[scalars(), full()],
        scratch=[VMEM((1024, N), bf16), VMEM((256, N), bf16)],
        limit=8,
        held=(1,),
        near=(0, 1),
    )


def weights_body(at_ref, up_ref, down_ref, other, out_hbm, out, rows_t, hid_t, sem):
    turn(at_ref[4], other, rows_t, hid_t)
    for j in range(4):
        here = slice(j * STEP, (j + 1) * STEP)
        up = (up_ref[:, here] + dot(rows_t[...], other[:, GB + j * STEP : GB + (j + 1) * STEP])).astype(bf16)
        for k in range(Z * X):
            out[k, :64, here] = up[k * 64 : (k + 1) * 64]
    copies = [pltpu.make_async_copy(out.at[:, pl.ds(0, 64)], out_hbm.at[:, pl.ds(0, 64)], sem.at[0])]
    copies[0].start()
    for j in range(8):
        here, at = slice(j * STEP, (j + 1) * STEP), WIDTH + j * STEP
        down = (down_ref[:, here] + dot(hid_t[...], other[:, at : at + STEP])).astype(bf16)
        row, col = 64 + 16 * (j // 4), (j % 4) * STEP
        for k in range(Z * X):
            out[k, row : row + 16, col : col + STEP] = down[k * 16 : (k + 1) * 16]
        if j % 4 == 3:
            part = pl.ds(row, 16)
            copies.append(pltpu.make_async_copy(out.at[:, part], out_hbm.at[:, part], sem.at[1 + j // 4]))
            copies[-1].start()
    for copy in copies:
        copy.wait()


def weights(at, own, other):
    return call(
        weights_body,
        "weights",
        [((Z * X, 96, 1024), bf16)],
        (at, *own, other),
        3 * N * WIDTH * FF,
        10 << 20,
        in_specs=[scalars(), full(), full(), full()],
        out_specs=[anywhere()],
        scratch=[
            VMEM((Z * X, 96, 1024), bf16),
            VMEM((1024, N), bf16),
            VMEM((256, N), bf16),
            pltpu.SemaphoreType.DMA((3,)),
        ],
        limit=12,
        held=(1, 2, 3),
    )[0]


def gather_sum_body(pieces_ref, up_ref, down_ref):
    for j in range(2):
        at = j * 512
        total = pieces_ref[0, :, at : at + 512].astype(f32)
        for k in range(1, Z * X):
            total = total + pieces_ref[k, :, at : at + 512].astype(f32)
        up_ref[0, :, at : at + 512] = total[:64]
        down_ref[0, :, at : at + 512] = total[64:80]
        down_ref[0, :, 1024 + at : 1024 + at + 512] = total[80:96]


def project_body(*refs):
    own, rest, place_hbm, turned_hbm, gate, cot_hbm, r0, r1, r2, r3, resid_hbm, gates, o0, o1, o2, o3 = refs[:16]
    place, turned, cot, back, w, resid, in_sem, w_sem, out_sem = refs[16:]
    copies = [
        pltpu.make_async_copy(r, back.at[pl.ds(s * CAP, CAP), :], in_sem.at[s]) for s, r in enumerate((r0, r1, r2, r3))
    ]
    copies.append(pltpu.make_async_copy(turned_hbm, turned, in_sem.at[4]))
    late = pltpu.make_async_copy(place_hbm, place, in_sem.at[6])
    copies.append(pltpu.make_async_copy(cot_hbm, cot, in_sem.at[5]))
    slabs = [pltpu.make_async_copy(own, w.at[0], w_sem.at[0])]
    for s in range(1, Y):
        slabs.append(pltpu.make_async_copy(rest.at[:, s - 1], w.at[s].reshape(rest.shape[0], -1, WIDTH), w_sem.at[s]))
    for copy in copies + slabs + [late]:
        copy.start()
    for copy in copies:
        copy.wait()
    wide = 512
    for j in range(WIDTH // wide):
        cols = slice(j * wide, (j + 1) * wide)
        resid[:, cols] = (cot[:, cols].astype(f32) + dot(turned[...], back[:, cols])).astype(bf16)
    sent = [pltpu.make_async_copy(resid, resid_hbm, out_sem)]
    sent[0].start()
    for s, out in enumerate((o0, o1, o2, o3)):
        slabs[s].wait()
        out[...] = dot_t(resid[...], w[s]).astype(bf16)
    late.wait()
    tail = back[:, WIDTH:].astype(f32)
    picked = jnp.sum(place[...].astype(f32) * (tail[:, 0:1] + tail[:, 1:2]), axis=0, keepdims=True)
    gates[...] = (picked / gate[...].astype(f32)).astype(bf16)
    for copy in sent:
        copy.wait()


def project(w_out, rest, place, turned, gate_row, grad_out, backs):
    shapes = [(ROWS, WIDTH), (1, ROWS)] + [(ROWS, 512)] * Y
    ins = (w_out, rest, place, turned, gate_row, grad_out, *backs)
    in_specs, out_specs = [anywhere() for _ in ins], [anywhere() for _ in shapes]
    in_specs[4] = full()
    out_specs[1:] = [full()] * 5
    return call(
        project_body,
        "project",
        [(s, bf16) for s in shapes],
        ins,
        2 * ROWS * WIDTH * WIDTH + 2 * ROWS * N * WIDTH,
        10 << 20,
        in_specs=in_specs,
        out_specs=out_specs,
        scratch=[
            VMEM((N, ROWS), bf16),
            VMEM((ROWS, N), bf16),
            VMEM((ROWS, WIDTH), bf16),
            VMEM((N, BACK), bf16),
            VMEM((Y, 512, WIDTH), bf16),
            VMEM((ROWS, WIDTH), bf16),
            pltpu.SemaphoreType.DMA((7,)),
            pltpu.SemaphoreType.DMA((Y,)),
            pltpu.SemaphoreType.DMA,
        ],
        limit=20,
        near=(2, 3, 4, 5),
    )


def state_body(at_ref, g0, g1, g2, g3, q_ref, grad_ref, state_ref):
    y, block = at_ref[0], at_ref[1]
    ramp = lax.broadcasted_iota(jnp.int32, (ROWS, 1), 0)
    sums = [jnp.zeros((HD, 2 * HD), f32) for _ in range(HEADS)]
    for s, g in enumerate((g0, g1, g2, g3)):
        off = pl.multiple_of(lax.rem(y + s, Y) * ROWS, ROWS)
        inverse = 1.0 / (3 * BLOCKS * TOK + block * TOK + off + ramp + 1).astype(f32)
        grad_ref[pl.ds(off, ROWS), :] = g[...]
        for h in range(HEADS):
            cols = slice(h * HD, (h + 1) * HD)
            both = jnp.concatenate(split(g[:, cols].astype(f32) * inverse), axis=1)
            sums[h] += t_dot(q_ref[pl.ds(off, ROWS), cols], both)
    for h in range(HEADS):
        state_ref[h * HD : (h + 1) * HD, :] = sums[h][:, :HD] + sums[h][:, HD:]


def head_state(at, grads, queries):
    return call(
        state_body,
        "state",
        [((TOK, HEADS * HD), bf16), ((HEADS * HD, HD), f32)],
        (at, *grads, queries),
        HEADS * 2 * TOK * HD * 2 * HD,
        4 << 20,
        in_specs=[scalars()] + [full()] * 5,
        limit=8,
        held=(1, 2, 3, 4, 5),
        near=(0, 1),
    )


def chip_body(state, other, chip, chip16):
    chip[...] = state[...] + other[...]
    chip16[...] = chip[...].astype(bf16)


def line_body(chip, x1, x2, x3, line16):
    total = chip[...] + x1[...].astype(f32) + x2[...].astype(f32) + x3[...].astype(f32)
    line16[...] = total.astype(bf16)


SUB = 256
PARTS = TOK // SUB
PAIR = 2


def triangle(lower):
    row = lax.broadcasted_iota(jnp.int32, (SUB, SUB), 0)
    col = lax.broadcasted_iota(jnp.int32, (SUB, SUB), 1)
    return (col <= row) if lower else (col >= row)


def query_part(block, h, g_ref, v_ref, k_ref, prior_ref, out_ref):
    mask = triangle(True)
    ramp = lax.broadcasted_iota(jnp.int32, (SUB, 1), 0)
    cols = slice(h * HD, (h + 1) * HD)
    prior = jnp.concatenate(split(prior_ref[h]), axis=0)
    for i in range(PARTS):
        rows, upto = slice(i * SUB, (i + 1) * SUB), (i + 1) * SUB
        g = g_ref[rows, cols]
        mix = dot_t(g, v_ref[:upto, cols])
        edge = jnp.where(mask, mix[:, i * SUB :], 0.0).astype(bf16)
        if i:
            edge = jnp.concatenate([mix[:, : i * SUB].astype(bf16), edge], axis=1)
        before = dot_t(g, prior)
        total = before[:, :HD] + before[:, HD:] + dot(edge, k_ref[:upto, cols])
        count = (3 * BLOCKS * TOK + block * TOK + i * SUB + ramp + 1).astype(f32)
        out_ref[rows, cols] = (total / count).astype(bf16)


def later_part(block, h, a_ref, b_ref, c_ref, out_ref):
    mask = triangle(False)
    ramp = lax.broadcasted_iota(jnp.int32, (1, TOK), 1)
    inverse = 1.0 / (3 * BLOCKS * TOK + block * TOK + ramp + 1).astype(f32)
    cols = slice(h * HD, (h + 1) * HD)
    for i in range(PARTS):
        at = i * SUB
        rows = slice(at, at + SUB)
        mix = dot_t(a_ref[rows, cols], b_ref[at:, cols]) * inverse[:, at:]
        edge = jnp.where(mask, mix[:, :SUB], 0.0).astype(bf16)
        if i < PARTS - 1:
            edge = jnp.concatenate([edge, mix[:, SUB:].astype(bf16)], axis=1)
        out_ref[rows, cols] = dot(edge, c_ref[at:, cols]).astype(bf16)


def query_key_body(at_ref, q_ref, k_ref, v_ref, g_ref, prior_ref, out_ref, key_ref):
    block = at_ref[1]
    for h in range(HEADS):
        query_part(block, h, g_ref, v_ref, k_ref, prior_ref, out_ref)
        later_part(block, h, v_ref, g_ref, q_ref, key_ref)


def value_body(at_ref, q_ref, k_ref, g_ref, value_ref):
    for h in range(HEADS):
        later_part(at_ref[1], h, k_ref, q_ref, g_ref, value_ref)


def head_call(body, name, ins, outs, near):
    return call(
        body,
        name,
        [((TOK, HEADS * HD), bf16)] * outs,
        ins,
        10 * HEADS * 4 * SUB * SUB * HD * outs,
        6 << 20,
        in_specs=[scalars()] + [full()] * (len(ins) - 1),
        limit=16,
        held=range(1, len(ins)),
        near=(near,),
    )


def final_body(spot_ref, other, x1, x2, x3, z1, z2, z3, v_ref, k_ref, key_ref, value_ref, key_hbm, value_hbm, outs, sem):
    z, x, core = spot_ref[2], spot_ref[3], spot_ref[4]
    copies = []
    for h in range(HEADS):
        rows, cols = slice(h * HD, (h + 1) * HD), slice(h * HD, (h + 1) * HD)
        later = jnp.where(core == 0, other[rows], 0.0)
        for s, a, b in ((1, x1, z1), (2, x2, z2), (3, x3, z3)):
            later += jnp.where(s > x, a[rows].astype(f32), 0.0) + jnp.where(s > z, b[rows].astype(f32), 0.0)
        hi, lo = split(later)
        key = dot_t(v_ref[:, cols], jnp.concatenate([hi, lo], axis=0))
        outs[0, :, cols] = (key_ref[:, cols].astype(f32) + key[:, :HD] + key[:, HD:]).astype(bf16)
        value = dot(k_ref[:, cols], jnp.concatenate([hi, lo], axis=1))
        outs[1, :, cols] = (value_ref[:, cols].astype(f32) + value[:, :HD] + value[:, HD:]).astype(bf16)
        here = pl.ds(h * HD, HD)
        for k, out in enumerate((key_hbm, value_hbm)):
            copy = pltpu.make_async_copy(outs.at[k, :, here], out.at[:, here], sem.at[2 * h + k])
            copy.start()
            copies.append(copy)
    for copy in copies:
        copy.wait()


def final(spot, sums, values, keys, key_here, value_here):
    return call(
        final_body,
        "final",
        [((TOK, HEADS * HD), bf16)] * 2,
        (spot, *sums, values, keys, key_here, value_here),
        HEADS * 8 * TOK * HD * HD,
        8 << 20,
        in_specs=[scalars()] + [full()] * 11,
        out_specs=[anywhere()] * 2,
        scratch=[VMEM((2, TOK, HEADS * HD), bf16), pltpu.SemaphoreType.DMA((2 * HEADS,))],
        limit=12,
        held=range(1, 12),
    )


def index(z, x, c):
    return (z * X + x) * C + c


def spots():
    return [(z, x, c) for z in range(Z) for x in range(X) for c in range(C)]


def along_y(a, s):
    return lax.ppermute(a, "exp", [(i, (i + s) % Y) for i in range(Y)])


def along_x(a, s):
    return lax.ppermute(a, "ctx", [(index(z, x, c), index(z, (x + s) % X, c)) for z, x, c in spots()])


def along_z(a, s):
    return lax.ppermute(a, "ctx", [(index(z, x, c), index((z + s) % Z, x, c)) for z, x, c in spots()])


def across(a):
    return lax.ppermute(a, "ctx", [(i, i ^ 1) for i in range(BLOCKS)])


def on_device(
    attn_query,
    attn_key,
    attn_value,
    prefix_state,
    moe_in,
    grad_out,
    router_gates,
    expert_ids,
    w_gate_up,
    w_down,
    w_out,
):
    y = lax.axis_index("exp")
    block = lax.axis_index("ctx")
    z, x, c = block >> 3, (block >> 1) & 3, block & 1
    at = jnp.stack([y, block, z, x, c]).astype(jnp.int32)

    slab = w_out.shape[0] // BLOCKS
    piece = lax.dynamic_slice_in_dim(w_out, block * slab, slab, 0)
    pieces = [along_y(piece, s) for s in (1, 2, 3)]
    gate_row = router_gates.reshape(1, ROWS)
    place, turned, *chunks = pack(at, expert_ids.reshape(1, ROWS), gate_row, moe_in, grad_out)
    pieces[0], place = lax.optimization_barrier((pieces[0], place))
    outs = [((3 * slab, WIDTH), bf16)]
    (pieces,) = call(join_body, "join", outs, pieces, limit=2, free=range(3))
    rest = lax.all_gather(pieces[None], "ctx", axis=0, tiled=True)
    rest = rest.reshape(BLOCKS, 3, slab, WIDTH)

    held = [chunks[0]] + [along_y(chunks[s], s) for s in (1, 2, 3)]
    w_pair, chunks[0] = lax.optimization_barrier((w_gate_up, chunks[0]))
    held[0] = chunks[0]
    prior = prefix_state[0]
    w_pair, w_back = fetch(w_pair, w_down)
    queries, keys, values = attn_query, attn_key, attn_value
    b0, b1, b2, b3, bundle = expert(held, w_pair, w_back)
    backs = [b0] + [along_y(b, -s) for s, b in ((1, b1), (2, b2), (3, b3))]
    partial = weights(at, own_weights(at, bundle), across(bundle))
    _, backs[2], backs[3] = lax.optimization_barrier((partial, backs[2], backs[3]))
    groups = [[index(i, j, k) for i in range(Z) for j in range(X)] for k in range(C)]
    exchanged = lax.all_to_all(partial, "ctx", 0, 0, axis_index_groups=groups, tiled=True)

    grad_resid, gates_out, *per_head = project(w_out, rest, place, turned, gate_row, grad_out, backs)
    grad_gates = gates_out.reshape(ROWS, 1)
    grads = [per_head[0]] + [along_y(per_head[s], -s) for s in (1, 2, 3)]
    attn_grad, state = head_state(at, grads, queries)

    other = across(state)
    size = (HEADS * HD, HD)
    outs = [(size, f32), (size, bf16)]
    chip, chip16 = call(chip_body, "chip", outs, (state, other), limit=4, held=(0, 1), near=(0, 1))
    from_x = [along_x(chip16, s) for s in (1, 2, 3)]
    ins = (at, queries, keys, values, attn_grad, prior)
    grad_query, key_here = head_call(query_key_body, "query_key", ins, 2, 1)
    chip, key_here = lax.optimization_barrier((chip, key_here))
    (line16,) = call(line_body, "line", [(size, bf16)], (chip, *from_x), limit=4, held=range(4), near=(0,))
    from_z = [along_z(line16, s) for s in (1, 2, 3)]
    (value_here,) = head_call(value_body, "value", (at, queries, keys, attn_grad), 1, 0)
    sums = (other, *from_x, *from_z)
    grad_key, grad_value = final(at, sums, values, keys, key_here, value_here)

    exchanged, grad_key = lax.optimization_barrier((exchanged, grad_key))
    outs = [((1, 64, 1024), f32), ((1, 16, WIDTH), f32)]
    grad_gate_up, grad_down = call(gather_sum_body, "gather_sum", outs, (exchanged,), 0, 4 << 20, free=(0,))
    return (grad_query, grad_key, grad_value, grad_resid, grad_gates, grad_gate_up, grad_down)


def solution(mesh):
    whole = P(("ctx", "exp"), None)
    split_cols = P("ctx", "exp")
    return jax.shard_map(
        on_device,
        mesh=mesh,
        in_specs=(
            split_cols,
            split_cols,
            split_cols,
            P("ctx", "exp", None, None),
            whole,
            whole,
            whole,
            whole,
            P("exp", None, None),
            P("exp", None, None),
            P("exp", None),
        ),
        out_specs=(
            split_cols,
            split_cols,
            split_cols,
            whole,
            whole,
            P("exp", "ctx", None),
            P("exp", "ctx", None),
        ),
        check_vma=False,
    )
```

```python
import jax
import jax.numpy as jnp
from jax import lax
from jax.experimental import pallas as pl
from jax.experimental.pallas import tpu as pltpu
from jax.sharding import PartitionSpec as P

bf16 = jnp.bfloat16
f32 = jnp.float32
VMEM = pltpu.VMEM
SMEM = pltpu.SMEM
Z, X, C, Y = 4, 4, 2, 4
CAP, ROWS, WIDTH, FF, HD, HEADS, TOK = 96, 256, 2048, 512, 128, 4, 1024
WEIGHT = 3
EARLY = ("pack", "fetch", "expert", "own_weights", "weights")
BLOCKS = Z * X * C


def dot(a, b):
    return lax.dot_general(a, b, (((1,), (0,)), ((), ())), preferred_element_type=f32)


def dot_t(a, b):
    return lax.dot_general(a, b, (((1,), (1,)), ((), ())), preferred_element_type=f32)


def t_dot(a, b):
    return lax.dot_general(a, b, (((0,), (0,)), ((), ())), preferred_element_type=f32)


def split(a):
    hi = a.astype(bf16)
    return hi, (a - hi.astype(f32)).astype(bf16)


def full():
    return pl.BlockSpec(memory_space=VMEM)


def scalars():
    return pl.BlockSpec(memory_space=SMEM)


def call(body, name, outs, ins, flops=0, moved=0, grid=None, in_specs=None, out_specs=None, limit=24, scratch=(), free=(), near=(), held=()):
    weight = 4 if name in EARLY else WEIGHT
    kwargs = {} if grid is None else {"grid": grid}
    specs = in_specs or [full() for _ in ins]
    ins = [
        a if spec.memory_space is SMEM or i in free else pltpu.with_memory_space_constraint(a, VMEM if i in held else pltpu.HBM)
        for i, (a, spec) in enumerate(zip(ins, specs))
    ]
    return pl.pallas_call(
        body,
        name=name,
        out_shape=[(VMEM if near is True or i in near else pltpu.HBM)(s, t) for i, (s, t) in enumerate(outs)],
        in_specs=specs,
        out_specs=out_specs or [full() for _ in outs],
        scratch_shapes=scratch,
        compiler_params=pltpu.CompilerParams(vmem_limit_bytes=limit << 20),
        cost_estimate=pl.CostEstimate(flops=weight * flops, bytes_accessed=weight * moved, transcendentals=0),
        **kwargs,
    )(*ins)


def pack_body(at_ref, ids_ref, gate_ref, moe_ref, cot_ref, place_ref, turned_ref, c0, c1, c2, c3, gate_col):
    @pl.when(pl.program_id(0) == 0)
    def _():
        rel = ids_ref[...] - at_ref[0]
        rel = jnp.where(rel < 0, rel + Y, rel)
        member = (lax.broadcasted_iota(jnp.int32, (8, ROWS), 0) == rel).astype(f32)
        row = lax.broadcasted_iota(jnp.int32, (ROWS, ROWS), 0)
        col = lax.broadcasted_iota(jnp.int32, (ROWS, ROWS), 1)
        earlier = dot(member.astype(bf16), (row < col).astype(bf16))
        slot = jnp.sum(earlier * member, axis=0, keepdims=True).astype(jnp.int32)
        target = rel * CAP + slot
        places = lax.broadcasted_iota(jnp.int32, (Y * CAP, ROWS), 0)
        place_ref[...] = (places == target).astype(bf16)
        spots_col = jnp.sum(jnp.where(row == col, target.astype(f32), 0.0), axis=1, keepdims=True)
        lanes = lax.broadcasted_iota(jnp.int32, (ROWS, Y * CAP), 1)
        turned_ref[...] = (lanes == spots_col.astype(jnp.int32)).astype(bf16)
        gate = gate_ref[...].astype(f32)
        gate_col[...] = jnp.sum(jnp.where(row == col, gate, 0.0), axis=1, keepdims=True)

    place = place_ref[...]
    scaled = (gate_col[...] * cot_ref[...].astype(f32)).astype(bf16)
    for half, rows in enumerate((moe_ref[...], scaled)):
        part = dot(place, rows).astype(bf16)
        for s, chunk in enumerate((c0, c1, c2, c3)):
            chunk[half] = part[s * CAP : (s + 1) * CAP]


def pack(at, ids, gates, moe_in, grad_out):
    step = 1024
    outs = [((Y * CAP, ROWS), bf16), ((ROWS, Y * CAP), bf16)] + [((2, CAP, WIDTH), bf16)] * Y
    ins = (at, ids, gates, moe_in, grad_out)
    row = pl.BlockSpec((1, ROWS), lambda j: (0, 0))
    tile = pl.BlockSpec((ROWS, step), lambda j: (0, j))
    return call(
        pack_body,
        "pack",
        outs,
        ins,
        2 * 384 * 256 * 4096,
        5 << 20,
        grid=(WIDTH // step,),
        in_specs=[scalars(), row, row, tile, tile],
        out_specs=[pl.BlockSpec((Y * CAP, ROWS), lambda j: (0, 0)), pl.BlockSpec((ROWS, Y * CAP), lambda j: (0, 0))]
        + [pl.BlockSpec((2, CAP, step), lambda j: (0, 0, j))] * Y,
        scratch=[VMEM((ROWS, 1), f32)],
        limit=16,
    )


BACK = WIDTH + 128
N = Y * CAP
BUNDLE = 2 * WIDTH + 3 * FF
GB, HID = 2 * WIDTH, 2 * WIDTH + 2 * FF
STEP = 256


def expert_body(r0, r1, r2, r3, wp, wb, b0, b1, b2, b3, held, back, out_sem):
    arrived = (r0, r1, r2, r3)
    backs = (b0, b1, b2, b3)
    tiles = FF // STEP

    for s, r in enumerate(arrived):
        held[s * CAP : (s + 1) * CAP, :WIDTH] = r[0]
        held[s * CAP : (s + 1) * CAP, WIDTH:GB] = r[1]
    total = jnp.zeros((N, 1), f32)
    for j in range(tiles):
        at, up = j * STEP, FF + j * STEP
        first = dot(held[:, :WIDTH], wp[0, :, at : at + STEP])
        second = dot(held[:, :WIDTH], wp[0, :, up : up + STEP])
        grad_hidden = dot_t(held[:, WIDTH:GB], wb[0, at : at + STEP, :])
        s = 1.0 / (1.0 + jnp.exp(-first))
        silu = first * s
        hidden = (silu * second).astype(bf16)
        held[:, HID + at : HID + at + STEP] = hidden
        total += jnp.sum(hidden.astype(f32) * grad_hidden, axis=1, keepdims=True)
        slope = s * (1.0 + first * (1.0 - s))
        held[:, GB + at : GB + at + STEP] = (grad_hidden * second * slope).astype(bf16)
        held[:, GB + up : GB + up + STEP] = (grad_hidden * silu).astype(bf16)
    hi, lo = split(total)
    lane = lax.broadcasted_iota(jnp.int32, (N, 128), 1)
    back[:, WIDTH:] = jnp.where(lane == 0, hi.astype(f32), lo.astype(f32)).astype(bf16)
    outgoing = []
    bounds = (0, WIDTH // 2, BACK)
    for part in range(2):
        lo_col, hi_col = bounds[part], bounds[part + 1]
        for at in range(lo_col, min(hi_col, WIDTH), STEP):
            back[:, at : at + STEP] = dot_t(held[:, GB:HID], wp[0, at : at + STEP, :]).astype(bf16)
        cols = pl.ds(lo_col, hi_col - lo_col)
        for s in range(Y):
            src = back.at[pl.ds(s * CAP, CAP), cols]
            copy = pltpu.make_async_copy(src, backs[s].at[:, cols], out_sem.at[part * Y + s])
            copy.start()
            outgoing.append(copy)
    for copy in outgoing:
        copy.wait()


def anywhere():
    return pl.BlockSpec(memory_space=pl.ANY)


def fetch_body(*refs):
    half = len(refs) // 2
    sem = refs[-1]
    copies = [pltpu.make_async_copy(refs[i], refs[half + i], sem.at[i]) for i in range(half)]
    for copy in copies:
        copy.start()
    for copy in copies:
        copy.wait()


def fetch(*arrays):
    return call(
        fetch_body,
        "fetch",
        [(a.shape, a.dtype) for a in arrays],
        arrays,
        0,
        12 << 20,
        in_specs=[anywhere() for _ in arrays],
        scratch=[pltpu.SemaphoreType.DMA((len(arrays),))],
        limit=2,
        near=True,
    )


def expert(chunks, w_pair, w_back):
    outs = [((CAP, BACK), bf16)] * Y + [((N, BUNDLE), bf16)]
    ins = (*chunks, w_pair, w_back)
    return call(
        expert_body,
        "expert",
        outs,
        ins,
        5 * 2 * N * WIDTH * FF,
        14 << 20,
        in_specs=[full()] * (Y + 2),
        out_specs=[anywhere()] * Y + [full()],
        scratch=[
            VMEM((N, BACK), bf16),
            pltpu.SemaphoreType.DMA((2 * Y,)),
        ],
        limit=16,
        held=range(6),
        near=(Y,),
    )


def chooser(core, wide, run):
    row = lax.broadcasted_iota(jnp.int32, (wide // 2, wide), 0)
    col = lax.broadcasted_iota(jnp.int32, (wide // 2, wide), 1)
    return (col == (row // run) * (2 * run) + core * run + row % run).astype(bf16)


def turn(core, src, rows_t, hid_t):
    pick_row, pick_hid = chooser(core, 512, 64), chooser(core, 128, 16)
    for i in range(Z):
        rows_t[i * 256 : (i + 1) * 256, :] = dot_t(pick_row, src[:, i * 512 : (i + 1) * 512]).astype(bf16)
        cols = slice(HID + i * 128, HID + (i + 1) * 128)
        hid_t[i * 64 : (i + 1) * 64, :] = dot_t(pick_hid, src[:, cols]).astype(bf16)


def own_weights_body(at_ref, mine, up_ref, down_ref, rows_t, hid_t):
    turn(at_ref[4], mine, rows_t, hid_t)
    for j in range(4):
        up_ref[:, j * STEP : (j + 1) * STEP] = dot(rows_t[...], mine[:, GB + j * STEP : GB + (j + 1) * STEP])
    for j in range(8):
        at = WIDTH + j * STEP
        down_ref[:, j * STEP : (j + 1) * STEP] = dot(hid_t[...], mine[:, at : at + STEP])


def own_weights(at, mine):
    return call(
        own_weights_body,
        "own_weights",
        [((1024, 1024), f32), ((256, WIDTH), f32)],
        (at, mine),
        3 * N * WIDTH * FF,
        10 << 20,
        in_specs=[scalars(), full()],
        scratch=[VMEM((1024, N), bf16), VMEM((256, N), bf16)],
        limit=8,
        held=(1,),
        near=(0, 1),
    )


def weights_body(at_ref, up_ref, down_ref, other, out_hbm, out, rows_t, hid_t, sem):
    turn(at_ref[4], other, rows_t, hid_t)
    for j in range(4):
        here = slice(j * STEP, (j + 1) * STEP)
        up = (up_ref[:, here] + dot(rows_t[...], other[:, GB + j * STEP : GB + (j + 1) * STEP])).astype(bf16)
        for k in range(Z * X):
            out[k, :64, here] = up[k * 64 : (k + 1) * 64]
    copies = [pltpu.make_async_copy(out.at[:, pl.ds(0, 64)], out_hbm.at[:, pl.ds(0, 64)], sem.at[0])]
    copies[0].start()
    for j in range(8):
        here, at = slice(j * STEP, (j + 1) * STEP), WIDTH + j * STEP
        down = (down_ref[:, here] + dot(hid_t[...], other[:, at : at + STEP])).astype(bf16)
        row, col = 64 + 16 * (j // 4), (j % 4) * STEP
        for k in range(Z * X):
            out[k, row : row + 16, col : col + STEP] = down[k * 16 : (k + 1) * 16]
        if j % 4 == 3:
            part = pl.ds(row, 16)
            copies.append(pltpu.make_async_copy(out.at[:, part], out_hbm.at[:, part], sem.at[1 + j // 4]))
            copies[-1].start()
    for copy in copies:
        copy.wait()


def weights(at, own, other):
    return call(
        weights_body,
        "weights",
        [((Z * X, 96, 1024), bf16)],
        (at, *own, other),
        3 * N * WIDTH * FF,
        10 << 20,
        in_specs=[scalars(), full(), full(), full()],
        out_specs=[anywhere()],
        scratch=[
            VMEM((Z * X, 96, 1024), bf16),
            VMEM((1024, N), bf16),
            VMEM((256, N), bf16),
            pltpu.SemaphoreType.DMA((3,)),
        ],
        limit=12,
        held=(1, 2, 3),
    )[0]


def gather_sum_body(pieces_ref, up_ref, down_ref):
    for j in range(2):
        at = j * 512
        total = pieces_ref[0, :, at : at + 512].astype(f32)
        for k in range(1, Z * X):
            total = total + pieces_ref[k, :, at : at + 512].astype(f32)
        up_ref[0, :, at : at + 512] = total[:64]
        down_ref[0, :, at : at + 512] = total[64:80]
        down_ref[0, :, 1024 + at : 1024 + at + 512] = total[80:96]


def project_body(*refs):
    own, rest, place_hbm, turned_hbm, gate, cot_hbm, r0, r1, r2, r3, resid_hbm, gates, o0, o1, o2, o3 = refs[:16]
    place, turned, cot, back, w, resid, in_sem, w_sem, out_sem = refs[16:]
    copies = [
        pltpu.make_async_copy(r, back.at[pl.ds(s * CAP, CAP), :], in_sem.at[s]) for s, r in enumerate((r0, r1, r2, r3))
    ]
    copies.append(pltpu.make_async_copy(turned_hbm, turned, in_sem.at[4]))
    late = pltpu.make_async_copy(place_hbm, place, in_sem.at[6])
    copies.append(pltpu.make_async_copy(cot_hbm, cot, in_sem.at[5]))
    slabs = [pltpu.make_async_copy(own, w.at[0], w_sem.at[0])]
    for s in range(1, Y):
        slabs.append(pltpu.make_async_copy(rest.at[:, s - 1], w.at[s].reshape(rest.shape[0], -1, WIDTH), w_sem.at[s]))
    for copy in copies + slabs + [late]:
        copy.start()
    for copy in copies:
        copy.wait()
    wide = 512
    for j in range(WIDTH // wide):
        cols = slice(j * wide, (j + 1) * wide)
        resid[:, cols] = (cot[:, cols].astype(f32) + dot(turned[...], back[:, cols])).astype(bf16)
    sent = [pltpu.make_async_copy(resid, resid_hbm, out_sem)]
    sent[0].start()
    for s, out in enumerate((o0, o1, o2, o3)):
        slabs[s].wait()
        out[...] = dot_t(resid[...], w[s]).astype(bf16)
    late.wait()
    tail = back[:, WIDTH:].astype(f32)
    picked = jnp.sum(place[...].astype(f32) * (tail[:, 0:1] + tail[:, 1:2]), axis=0, keepdims=True)
    gates[...] = (picked / gate[...].astype(f32)).astype(bf16)
    for copy in sent:
        copy.wait()


def project(w_out, rest, place, turned, gate_row, grad_out, backs):
    shapes = [(ROWS, WIDTH), (1, ROWS)] + [(ROWS, 512)] * Y
    ins = (w_out, rest, place, turned, gate_row, grad_out, *backs)
    in_specs, out_specs = [anywhere() for _ in ins], [anywhere() for _ in shapes]
    in_specs[4] = full()
    out_specs[1:] = [full()] * 5
    return call(
        project_body,
        "project",
        [(s, bf16) for s in shapes],
        ins,
        2 * ROWS * WIDTH * WIDTH + 2 * ROWS * N * WIDTH,
        10 << 20,
        in_specs=in_specs,
        out_specs=out_specs,
        scratch=[
            VMEM((N, ROWS), bf16),
            VMEM((ROWS, N), bf16),
            VMEM((ROWS, WIDTH), bf16),
            VMEM((N, BACK), bf16),
            VMEM((Y, 512, WIDTH), bf16),
            VMEM((ROWS, WIDTH), bf16),
            pltpu.SemaphoreType.DMA((7,)),
            pltpu.SemaphoreType.DMA((Y,)),
            pltpu.SemaphoreType.DMA,
        ],
        limit=20,
        near=(2, 3, 4, 5),
    )


def state_body(at_ref, g0, g1, g2, g3, q_ref, grad_ref, state_ref):
    y, block = at_ref[0], at_ref[1]
    ramp = lax.broadcasted_iota(jnp.int32, (ROWS, 1), 0)
    sums = [jnp.zeros((HD, 2 * HD), f32) for _ in range(HEADS)]
    for s, g in enumerate((g0, g1, g2, g3)):
        off = pl.multiple_of(lax.rem(y + s, Y) * ROWS, ROWS)
        inverse = 1.0 / (3 * BLOCKS * TOK + block * TOK + off + ramp + 1).astype(f32)
        grad_ref[pl.ds(off, ROWS), :] = g[...]
        for h in range(HEADS):
            cols = slice(h * HD, (h + 1) * HD)
            both = jnp.concatenate(split(g[:, cols].astype(f32) * inverse), axis=1)
            sums[h] += t_dot(q_ref[pl.ds(off, ROWS), cols], both)
    for h in range(HEADS):
        state_ref[h * HD : (h + 1) * HD, :] = sums[h][:, :HD] + sums[h][:, HD:]


def head_state(at, grads, queries):
    return call(
        state_body,
        "state",
        [((TOK, HEADS * HD), bf16), ((HEADS * HD, HD), f32)],
        (at, *grads, queries),
        HEADS * 2 * TOK * HD * 2 * HD,
        4 << 20,
        in_specs=[scalars()] + [full()] * 5,
        limit=8,
        held=(1, 2, 3, 4, 5),
        near=(0, 1),
    )


def chip_body(state, other, chip, chip16):
    chip[...] = state[...] + other[...]
    chip16[...] = chip[...].astype(bf16)


def line_body(chip, x1, x2, x3, line16):
    total = chip[...] + x1[...].astype(f32) + x2[...].astype(f32) + x3[...].astype(f32)
    line16[...] = total.astype(bf16)


SUB = 256
PARTS = TOK // SUB
PAIR = 2


def triangle(lower):
    row = lax.broadcasted_iota(jnp.int32, (SUB, SUB), 0)
    col = lax.broadcasted_iota(jnp.int32, (SUB, SUB), 1)
    return (col <= row) if lower else (col >= row)


def query_part(block, h, g_ref, v_ref, k_ref, prior_ref, out_ref):
    mask = triangle(True)
    ramp = lax.broadcasted_iota(jnp.int32, (SUB, 1), 0)
    cols = slice(h * HD, (h + 1) * HD)
    prior = jnp.concatenate(split(prior_ref[h]), axis=0)
    for i in range(PARTS):
        rows, upto = slice(i * SUB, (i + 1) * SUB), (i + 1) * SUB
        g = g_ref[rows, cols]
        mix = dot_t(g, v_ref[:upto, cols])
        edge = jnp.where(mask, mix[:, i * SUB :], 0.0).astype(bf16)
        if i:
            edge = jnp.concatenate([mix[:, : i * SUB].astype(bf16), edge], axis=1)
        before = dot_t(g, prior)
        total = before[:, :HD] + before[:, HD:] + dot(edge, k_ref[:upto, cols])
        count = (3 * BLOCKS * TOK + block * TOK + i * SUB + ramp + 1).astype(f32)
        out_ref[rows, cols] = (total / count).astype(bf16)


def later_part(block, h, a_ref, b_ref, c_ref, out_ref):
    mask = triangle(False)
    ramp = lax.broadcasted_iota(jnp.int32, (1, TOK), 1)
    inverse = 1.0 / (3 * BLOCKS * TOK + block * TOK + ramp + 1).astype(f32)
    cols = slice(h * HD, (h + 1) * HD)
    for i in range(PARTS):
        at = i * SUB
        rows = slice(at, at + SUB)
        mix = dot_t(a_ref[rows, cols], b_ref[at:, cols]) * inverse[:, at:]
        edge = jnp.where(mask, mix[:, :SUB], 0.0).astype(bf16)
        if i < PARTS - 1:
            edge = jnp.concatenate([edge, mix[:, SUB:].astype(bf16)], axis=1)
        out_ref[rows, cols] = dot(edge, c_ref[at:, cols]).astype(bf16)


def query_key_body(at_ref, q_ref, k_ref, v_ref, g_ref, prior_ref, out_ref, key_ref):
    block = at_ref[1]
    for h in range(HEADS):
        query_part(block, h, g_ref, v_ref, k_ref, prior_ref, out_ref)
        later_part(block, h, v_ref, g_ref, q_ref, key_ref)


def value_body(at_ref, q_ref, k_ref, g_ref, value_ref):
    for h in range(HEADS):
        later_part(at_ref[1], h, k_ref, q_ref, g_ref, value_ref)


def head_call(body, name, ins, outs, near):
    return call(
        body,
        name,
        [((TOK, HEADS * HD), bf16)] * outs,
        ins,
        10 * HEADS * 4 * SUB * SUB * HD * outs,
        6 << 20,
        in_specs=[scalars()] + [full()] * (len(ins) - 1),
        limit=16,
        held=range(1, len(ins)),
        near=(near,),
    )


def final_body(spot_ref, other, x1, x2, x3, z1, z2, z3, v_ref, k_ref, key_ref, value_ref, key_hbm, value_hbm, outs, sem):
    z, x, core = spot_ref[2], spot_ref[3], spot_ref[4]
    copies = []
    for h in range(HEADS):
        rows, cols = slice(h * HD, (h + 1) * HD), slice(h * HD, (h + 1) * HD)
        later = jnp.where(core == 0, other[rows], 0.0)
        for s, a, b in ((1, x1, z1), (2, x2, z2), (3, x3, z3)):
            later += jnp.where(s > x, a[rows].astype(f32), 0.0) + jnp.where(s > z, b[rows].astype(f32), 0.0)
        hi, lo = split(later)
        key = dot_t(v_ref[:, cols], jnp.concatenate([hi, lo], axis=0))
        outs[0, :, cols] = (key_ref[:, cols].astype(f32) + key[:, :HD] + key[:, HD:]).astype(bf16)
        value = dot(k_ref[:, cols], jnp.concatenate([hi, lo], axis=1))
        outs[1, :, cols] = (value_ref[:, cols].astype(f32) + value[:, :HD] + value[:, HD:]).astype(bf16)
        here = pl.ds(h * HD, HD)
        for k, out in enumerate((key_hbm, value_hbm)):
            copy = pltpu.make_async_copy(outs.at[k, :, here], out.at[:, here], sem.at[2 * h + k])
            copy.start()
            copies.append(copy)
    for copy in copies:
        copy.wait()


def final(spot, sums, values, keys, key_here, value_here):
    return call(
        final_body,
        "final",
        [((TOK, HEADS * HD), bf16)] * 2,
        (spot, *sums, values, keys, key_here, value_here),
        HEADS * 8 * TOK * HD * HD,
        8 << 20,
        in_specs=[scalars()] + [full()] * 11,
        out_specs=[anywhere()] * 2,
        scratch=[VMEM((2, TOK, HEADS * HD), bf16), pltpu.SemaphoreType.DMA((2 * HEADS,))],
        limit=12,
        held=range(1, 12),
    )


def index(z, x, c):
    return (z * X + x) * C + c


def spots():
    return [(z, x, c) for z in range(Z) for x in range(X) for c in range(C)]


def along_y(a, s):
    return lax.ppermute(a, "exp", [(i, (i + s) % Y) for i in range(Y)])


def along_x(a, s):
    return lax.ppermute(a, "ctx", [(index(z, x, c), index(z, (x + s) % X, c)) for z, x, c in spots()])


def along_z(a, s):
    return lax.ppermute(a, "ctx", [(index(z, x, c), index((z + s) % Z, x, c)) for z, x, c in spots()])


def across(a):
    return lax.ppermute(a, "ctx", [(i, i ^ 1) for i in range(BLOCKS)])


def on_device(
    attn_query,
    attn_key,
    attn_value,
    prefix_state,
    moe_in,
    grad_out,
    router_gates,
    expert_ids,
    w_gate_up,
    w_down,
    w_out,
):
    y = lax.axis_index("exp")
    block = lax.axis_index("ctx")
    z, x, c = block >> 3, (block >> 1) & 3, block & 1
    at = jnp.stack([y, block, z, x, c]).astype(jnp.int32)

    slab = w_out.shape[0] // BLOCKS
    piece = lax.dynamic_slice_in_dim(w_out, block * slab, slab, 0)
    pieces = jnp.concatenate([along_y(piece, s) for s in (1, 2, 3)], axis=0)
    gate_row = router_gates.reshape(1, ROWS)
    place, turned, *chunks = pack(at, expert_ids.reshape(1, ROWS), gate_row, moe_in, grad_out)
    pieces, chunks[1] = lax.optimization_barrier((pieces, chunks[1]))
    rest = lax.all_gather(pieces[None], "ctx", axis=0, tiled=True)
    rest = rest.reshape(BLOCKS, 3, slab, WIDTH)

    held = [chunks[0]] + [along_y(chunks[s], s) for s in (1, 2, 3)]
    w_pair, chunks[0] = lax.optimization_barrier((w_gate_up, chunks[0]))
    held[0] = chunks[0]
    prior = prefix_state[0]
    w_pair, w_back = fetch(w_pair, w_down)
    queries, keys, values = attn_query, attn_key, attn_value
    b0, b1, b2, b3, bundle = expert(held, w_pair, w_back)
    backs = [b0] + [along_y(b, -s) for s, b in ((1, b1), (2, b2), (3, b3))]
    partial = weights(at, own_weights(at, bundle), across(bundle))
    _, backs[2], backs[3] = lax.optimization_barrier((partial, backs[2], backs[3]))
    groups = [[index(i, j, k) for i in range(Z) for j in range(X)] for k in range(C)]
    exchanged = lax.all_to_all(partial, "ctx", 0, 0, axis_index_groups=groups, tiled=True)

    grad_resid, gates_out, *per_head = project(w_out, rest, place, turned, gate_row, grad_out, backs)
    grad_gates = gates_out.reshape(ROWS, 1)
    grads = [per_head[0]] + [along_y(per_head[s], -s) for s in (1, 2, 3)]
    attn_grad, state = head_state(at, grads, queries)

    other = across(state)
    size = (HEADS * HD, HD)
    outs = [(size, f32), (size, bf16)]
    chip, chip16 = call(chip_body, "chip", outs, (state, other), limit=4, held=(0, 1), near=(0, 1))
    from_x = [along_x(chip16, s) for s in (1, 2, 3)]
    ins = (at, queries, keys, values, attn_grad, prior)
    grad_query, key_here = head_call(query_key_body, "query_key", ins, 2, 1)
    chip, key_here = lax.optimization_barrier((chip, key_here))
    (line16,) = call(line_body, "line", [(size, bf16)], (chip, *from_x), limit=4, held=range(4), near=(0,))
    from_z = [along_z(line16, s) for s in (1, 2, 3)]
    (value_here,) = head_call(value_body, "value", (at, queries, keys, attn_grad), 1, 0)
    sums = (other, *from_x, *from_z)
    grad_key, grad_value = final(at, sums, values, keys, key_here, value_here)

    exchanged, grad_key = lax.optimization_barrier((exchanged, grad_key))
    outs = [((1, 64, 1024), f32), ((1, 16, WIDTH), f32)]
    grad_gate_up, grad_down = call(gather_sum_body, "gather_sum", outs, (exchanged,), 0, 4 << 20, free=(0,))
    return (grad_query, grad_key, grad_value, grad_resid, grad_gates, grad_gate_up, grad_down)


def solution(mesh):
    whole = P(("ctx", "exp"), None)
    split_cols = P("ctx", "exp")
    return jax.shard_map(
        on_device,
        mesh=mesh,
        in_specs=(
            split_cols,
            split_cols,
            split_cols,
            P("ctx", "exp", None, None),
            whole,
            whole,
            whole,
            whole,
            P("exp", None, None),
            P("exp", None, None),
            P("exp", None),
        ),
        out_specs=(
            split_cols,
            split_cols,
            split_cols,
            whole,
            whole,
            P("exp", "ctx", None),
            P("exp", "ctx", None),
        ),
        check_vma=False,
    )
```
